32 devices in a mesh: seq: 4 (over y, x), ctx: 4 (over z), fsdp: 2 (over core).
Axes of the slice: x: 2, y: 2, z: 4, core: 2. Of those that a mesh axis runs over, the one named last changes fastest.
Arguments:
- block_input: bfloat16 [8, 2048, 896], P(('seq', 'fsdp'), 'ctx'), may hold values from -6 to 6
- segment_ids: int32 [8, 2048], P(('seq', 'fsdp')), may hold values from 0 to 3, as said below
- out_cotangent: bfloat16 [8, 2048, 896], P(('seq', 'fsdp'), 'ctx'), may hold values from -6 to 6
- input_gain: bfloat16 [896], P('fsdp'), may hold values from 0.5 to 1.5
- query_weight: bfloat16 [896, 896], P('fsdp'), may hold values from -0.1875 to 0.1875
- query_bias: bfloat16 [896], P('fsdp'), may hold values from -3 to 3
- key_weight: bfloat16 [896, 128], P('fsdp'), may hold values from -0.1875 to 0.1875
- key_bias: bfloat16 [128], P('fsdp'), may hold values from -3 to 3
- value_weight: bfloat16 [896, 128], P('fsdp'), may hold values from -0.1875 to 0.1875
- value_bias: bfloat16 [128], P('fsdp'), may hold values from -3 to 3
- output_weight: bfloat16 [896, 896], P('fsdp'), may hold values from -0.75 to 0.75
- middle_gain: bfloat16 [896], P('fsdp'), may hold values from 0.5 to 1.5
- gate_weight: bfloat16 [896, 4864], P('fsdp'), may hold values from -0.1875 to 0.1875
- up_weight: bfloat16 [896, 4864], P('fsdp'), may hold values from -0.1875 to 0.1875
- down_weight: bfloat16 [4864, 896], P('fsdp'), may hold values from -0.078125 to 0.078125
Outputs:
- block_output: bfloat16 [8, 2048, 896], P(('seq', 'fsdp'), 'ctx')
- input_grad: bfloat16 [8, 2048, 896], P(('seq', 'fsdp'), 'ctx')
- input_gain_grad: float32 [896], P('fsdp')
- query_weight_grad: float32 [896, 896], P('fsdp')
- query_bias_grad: float32 [896], P('fsdp')
- key_weight_grad: float32 [896, 128], P('fsdp')
- key_bias_grad: float32 [128], P('fsdp')
- value_weight_grad: float32 [896, 128], P('fsdp')
- value_bias_grad: float32 [128], P('fsdp')
- output_weight_grad: float32 [896, 896], P('fsdp')
- middle_gain_grad: float32 [896], P('fsdp')
- gate_weight_grad: float32 [896, 4864], P('fsdp')
- up_weight_grad: float32 [896, 4864], P('fsdp')
- down_weight_grad: float32 [4864, 896], P('fsdp')
The draws below stay inside these ranges and needn't reach their ends.
Inputs may be any that keep to these rules, and one draw needn't show every extreme that they name: `segment_ids`: along each sequence the document numbers never fall; every sequence holds four documents 0, 1, 2, 3, and document 2 begins within the first 512 positions and ends within the last 512.
All inputs are finite; a program needn't handle non-finite values.
Results may differ from the reference program's by a relative error of at most 0.023.
Values may be sent and summed in bfloat16 or wider, within the bound.
No kernel may reach another device: no remote copies, remote signals or barrier semaphores. Data moves between devices by JAX's collectives and lax.ppermute only.
A program may use at most 320 MiB of HBM per device.

```python
import jax
import jax.numpy as jnp
from jax import lax

D = 896
HQ = 14
KVH = 2
HD = 64
FF = 4864
WINDOW = 1024
TOK_DEV = 512
SEQS = 8
LEN = 2048


def draw_segment_ids(key, part):
    key = jax.random.fold_in(key, 7)
    keys = jax.random.split(key, 3)
    first_cut = jax.random.randint(keys[0], (SEQS, 1), 1, TOK_DEV // 2 + 1)
    second_cut = first_cut + jax.random.randint(keys[1], (SEQS, 1), 1, TOK_DEV // 2)
    third_cut = LEN - jax.random.randint(keys[2], (SEQS, 1), 1, TOK_DEV)
    positions = jnp.arange(LEN, dtype=jnp.int32)[None, :]
    total = (positions >= first_cut).astype(jnp.int32) + (positions >= second_cut).astype(jnp.int32) + (positions >= third_cut).astype(jnp.int32)
    return total.astype(jnp.int32)


def steps_of(own_key, extent, cuts, low, largest):
    level = 1.0
    for position, blocks in cuts:
        heights = jax.random.uniform(jax.random.fold_in(jax.random.fold_in(own_key, 6), position), (blocks,), jnp.float32, low / len(cuts), largest / len(cuts))
        level = level * jnp.repeat(jnp.exp(heights), extent[position] // blocks).reshape((-1,) + (1,) * (len(extent) - 1 - position))
    return level


def scatter_about(rng, shape, deviation, most, cuts=(), kind=jnp.bfloat16):
    array = deviation * jax.random.normal(rng, shape, jnp.float32)
    if cuts:
        array = array * steps_of(rng, shape, cuts, -0.22, 0.18)
    return jnp.clip(array, -most, most).astype(kind)


def setup_inputs(seed: int = 0) -> dict:
    key_of = jax.random.split(jax.random.key(seed), 16)
    block_input = scatter_about(key_of[0], (SEQS, LEN, D), 1.0, 6.0, ((0, 8), (1, 4)))
    segment_ids = draw_segment_ids(jax.random.fold_in(key_of[15], 71), 0)
    out_cotangent = scatter_about(key_of[2], (SEQS, LEN, D), 1.0, 6.0, ((0, 8), (1, 4)))
    input_gain = jnp.clip(1.0 + 0.1 * jax.random.normal(key_of[3], (D,), jnp.float32), 0.5, 1.5).astype(jnp.bfloat16)
    query_weight = scatter_about(key_of[4], (D, HQ * HD), D ** -0.5, 0.1875, ((0, 2),))
    query_bias = scatter_about(key_of[5], (HQ * HD,), 0.5, 3.0, ((0, 2),))
    key_weight = scatter_about(key_of[6], (D, KVH * HD), D ** -0.5, 0.1875, ((0, 2),))
    key_bias = scatter_about(key_of[7], (KVH * HD,), 0.5, 3.0, ((0, 2),))
    value_weight = scatter_about(key_of[8], (D, KVH * HD), D ** -0.5, 0.1875, ((0, 2),))
    value_bias = scatter_about(key_of[9], (KVH * HD,), 0.5, 3.0, ((0, 2),))
    output_weight = scatter_about(key_of[10], (HQ * HD, D), (HQ * HD // 16) ** -0.5, 0.75, ((0, 2),))
    middle_gain = jnp.clip(1.0 + 0.1 * jax.random.normal(key_of[11], (D,), jnp.float32), 0.5, 1.5).astype(jnp.bfloat16)
    gate_weight = scatter_about(key_of[12], (D, FF), D ** -0.5, 0.1875, ((0, 2),))
    up_weight = scatter_about(key_of[13], (D, FF), D ** -0.5, 0.1875, ((0, 2),))
    down_weight = scatter_about(key_of[14], (FF, D), FF ** -0.5, 0.078125, ((0, 2),))
    return dict(block_input=block_input, segment_ids=segment_ids, out_cotangent=out_cotangent, input_gain=input_gain, query_weight=query_weight, query_bias=query_bias, key_weight=key_weight, key_bias=key_bias, value_weight=value_weight, value_bias=value_bias, output_weight=output_weight, middle_gain=middle_gain, gate_weight=gate_weight, up_weight=up_weight, down_weight=down_weight)


@jax.custom_vjp
def low(v):
    return lax.optimization_barrier(v.astype(jnp.bfloat16)).astype(jnp.float32)

@jax.custom_vjp
def low_back(v):
    return v

def low_keep(v):
    return (low(v), None)

def low_pass(kept, grad):
    return (grad,)

def back_keep(v):
    return (v, None)

def back_low(kept, grad):
    return (low(grad),)
low.defvjp(low_keep, low_pass)
low_back.defvjp(back_keep, back_low)
theta_base = 1000000.0
eps_norm = 1e-06

def product(left, right):
    return jnp.dot(left, right, precision=lax.Precision.HIGHEST)

def rms_norm(values, gain):
    return values * lax.rsqrt(lax.optimization_barrier(jnp.mean(values * values, -1, keepdims=True)) + eps_norm) * gain

def rotate_half(values):
    half = values.shape[-1] // 2
    return jnp.concatenate([-values[..., half:], values[..., :half]], -1)

def rotate(values, cosine, sine):
    return values * cosine[:, None, :] + rotate_half(values) * sine[:, None, :]

def attend(query_rot, key_rot, value_low, seg_row):
    width = TOK_DEV
    group = HQ // KVH
    scale = HD ** (-0.5)
    key_pad = jnp.concatenate([jnp.zeros((WINDOW, KVH, HD), jnp.float32), key_rot], 0)
    value_pad = jnp.concatenate([jnp.zeros((WINDOW, KVH, HD), jnp.float32), value_low], 0)
    seg_pad = jnp.concatenate([jnp.full((WINDOW,), -1, jnp.int32), seg_row.astype(jnp.int32)], 0)

    def block(start):
        query = lax.dynamic_slice_in_dim(query_rot, start, width, 0).reshape(width, KVH, group, HD)
        keys = lax.dynamic_slice_in_dim(key_pad, start, WINDOW + width, 0)
        values = lax.dynamic_slice_in_dim(value_pad, start, WINDOW + width, 0)
        key_seg = lax.dynamic_slice_in_dim(seg_pad, start, WINDOW + width, 0)
        query_seg = lax.dynamic_slice_in_dim(seg_row.astype(jnp.int32), start, width, 0)
        query_index = start + jnp.arange(width, dtype=jnp.int32)
        key_index = start - WINDOW + jnp.arange(WINDOW + width, dtype=jnp.int32)
        distance = query_index[:, None] - key_index[None, :]
        visible = (key_seg[None, :] == query_seg[:, None]) & (key_index[None, :] >= 0) & (distance >= 0) & (distance < WINDOW)
        scores = low_back(jnp.einsum('tkgd,skd->kgts', query, keys, precision=lax.Precision.HIGHEST) * scale)
        masked = jnp.where(visible[None, None], scores, -1e+30)
        top = lax.optimization_barrier(jnp.max(masked, -1, keepdims=True))
        expo = jnp.exp(masked - top)
        probs = expo / lax.optimization_barrier(jnp.sum(expo, -1, keepdims=True))
        mixed = jnp.einsum('kgts,skd->tkgd', low(probs), values, precision=lax.Precision.HIGHEST)
        return mixed.reshape(width, HQ * HD)
    starts = jnp.arange(LEN // width, dtype=jnp.int32) * width
    return lax.map(jax.checkpoint(block), starts).reshape(LEN, HQ * HD)

def one_sequence(tokens, seg_row, params):
    gain_one, w_query, b_query, w_key, b_key, w_value, b_value, w_output, gain_two, w_gate, w_up, w_down = params
    positions = jnp.arange(LEN, dtype=jnp.float32)
    inverse = theta_base ** (-jnp.arange(0, HD, 2, dtype=jnp.float32) / HD)
    angle = positions[:, None] * inverse[None, :]
    cosine = jnp.concatenate([jnp.cos(angle), jnp.cos(angle)], -1)
    sine = jnp.concatenate([jnp.sin(angle), jnp.sin(angle)], -1)
    normed_one = low(rms_norm(tokens, gain_one))
    query_pre = low_back(product(normed_one, w_query) + b_query).reshape(LEN, HQ, HD)
    key_pre = low_back(product(normed_one, w_key) + b_key).reshape(LEN, KVH, HD)
    value_low = low(low_back(product(normed_one, w_value) + b_value)).reshape(LEN, KVH, HD)
    query_rot = low(rotate(query_pre, cosine, sine))
    key_rot = low(rotate(key_pre, cosine, sine))
    mixed = low(low_back(attend(query_rot, key_rot, value_low, seg_row)))
    hidden_one = tokens + low_back(product(mixed, w_output))
    normed_two = low(rms_norm(hidden_one, gain_two))
    gate_pre = low_back(product(normed_two, w_gate))
    up_pre = low_back(product(normed_two, w_up))
    inner = low(jax.nn.silu(gate_pre) * up_pre)
    return hidden_one + low_back(product(inner, w_down))

def reference(block_input, segment_ids, out_cotangent, input_gain, query_weight, query_bias, key_weight, key_bias, value_weight, value_bias, output_weight, middle_gain, gate_weight, up_weight, down_weight):
    params = tuple((p.astype(jnp.float32) for p in (input_gain, query_weight, query_bias, key_weight, key_bias, value_weight, value_bias, output_weight, middle_gain, gate_weight, up_weight, down_weight)))

    def forward(tokens_all, weights):

        def per_sequence(pair):
            return jax.checkpoint(one_sequence)(pair[0], pair[1], weights)
        return lax.map(per_sequence, (tokens_all, segment_ids))
    result, pullback = jax.vjp(forward, block_input.astype(jnp.float32), params)
    grad_tokens, grads = pullback(out_cotangent.astype(jnp.float32))
    return (result.astype(jnp.bfloat16), grad_tokens.astype(jnp.bfloat16), grads[0], grads[1], grads[2], grads[3], grads[4], grads[5], grads[6], grads[7], grads[8], grads[9], grads[10], grads[11])
```

```python
import functools

import jax
import jax.numpy as jnp
from jax import lax
from jax.experimental import pallas as pl
from jax.experimental.pallas import tpu as pltpu
from jax.sharding import PartitionSpec as P

HQ = 14
KVH = 2
HD = 64
WINDOW = 1024
PAIRS = HQ // 2
LANES = 128
HALF = 256

theta_base = 1000000.0
eps_norm = 1e-06
masked_score = -1e30
f32 = jnp.float32
bf16 = jnp.bfloat16
VMEM_BYTES = 58 * 1024 * 1024


def nn(a, b):
    return lax.dot_general(a, b, (((1,), (0,)), ((), ())), preferred_element_type=f32)


def nt(a, b):
    return lax.dot_general(a, b, (((1,), (1,)), ((), ())), preferred_element_type=f32)


def flip_lanes_half(values):
    width = values.shape[-1]
    lane = lax.broadcasted_iota(jnp.int32, values.shape, len(values.shape) - 1)
    up = pltpu.roll(values, width - 32, len(values.shape) - 1)
    down = pltpu.roll(values, 32, len(values.shape) - 1)
    return jnp.where((lane & 63) < 32, -up, down)


def call(kernel, out_shape, flops, moved, **kwargs):
    return pl.pallas_call(
        kernel,
        out_shape=out_shape,
        compiler_params=pltpu.CompilerParams(vmem_limit_bytes=VMEM_BYTES),
        cost_estimate=pl.CostEstimate(flops=flops, bytes_accessed=moved, transcendentals=0),
        **kwargs,
    )


def project_kernel(x_ref, gain_ref, w_ref, bias_ref, cos_ref, sin_ref, n1_ref, q_ref, kv_ref):
    count = x_ref.shape[0]
    step = 256

    def body(i, carry):
        rows = pl.ds(pl.multiple_of(i * step, step), step)
        x = x_ref[rows, :].astype(f32)
        scale = lax.rsqrt(jnp.mean(x * x, -1, keepdims=True) + eps_norm)
        normed = (x * scale * gain_ref[...]).astype(bf16)
        n1_ref[rows, :] = normed
        cosine = cos_ref[rows, :]
        sine = sin_ref[rows, :]
        out = nn(normed, w_ref[...]) + bias_ref[...]
        for j in range(PAIRS + 1):
            part = out[:, j * LANES : (j + 1) * LANES]
            part = part * cosine + flip_lanes_half(part) * sine
            if j < PAIRS:
                q_ref[rows, j * LANES : (j + 1) * LANES] = (part * HD**-0.5).astype(bf16)
            else:
                kv_ref[rows, :LANES] = part.astype(bf16)
        kv_ref[rows, LANES:] = out[:, (PAIRS + 1) * LANES :].astype(bf16)
        return carry

    lax.fori_loop(0, count // step, body, 0)


def project(x, gain, w, bias, cosine, sine):
    count, width = x.shape
    return call(
        project_kernel,
        (
            jax.ShapeDtypeStruct((count, width), bf16),
            jax.ShapeDtypeStruct((count, HQ * HD), bf16),
            jax.ShapeDtypeStruct((count, 2 * KVH * HD), bf16),
        ),
        2 * count * width * w.shape[1],
        6 * 1024 * 1024,
    )(x, gain, w, bias, cosine, sine)


def lane_low(shape):
    return lax.broadcasted_iota(jnp.int32, shape, len(shape) - 1) < HD


def spread_heads(source, target, row):
    values = source.astype(f32)
    other = pltpu.roll(values, HD, 1)
    low = lane_low(values.shape)
    rows = pl.ds(row, values.shape[0])
    target[0, 0, rows, :] = jnp.where(low, values, 0.0).astype(bf16)
    target[1, 0, rows, :] = jnp.where(low, 0.0, other).astype(bf16)
    target[0, 1, rows, :] = jnp.where(low, other, 0.0).astype(bf16)
    target[1, 1, rows, :] = jnp.where(low, 0.0, values).astype(bf16)


def turn_heads(source, target, column):
    values = source.astype(f32).T.astype(bf16)
    columns = pl.ds(column, values.shape[1])
    target[0, :, columns] = values[:HD]
    target[1, :, columns] = values[HD:]


def fill_bias(qseg_ref, kseg_ref, near_ref, far_ref, count):
    for t in range(count // HALF):
        columns = slice(t * HALF, (t + 1) * HALF)
        query = qseg_ref[:, columns]
        near = kseg_ref[count : 2 * count, :] == query
        near_ref[:, columns] = jnp.where(near, 0.0, masked_score)
        key = lax.broadcasted_iota(jnp.int32, (count, HALF), 0)
        token = lax.broadcasted_iota(jnp.int32, (count, HALF), 1) + t * HALF
        shape = (count, HALF)
        far = jnp.where(
            key <= token,
            jnp.broadcast_to(kseg_ref[:count, :], shape),
            jnp.broadcast_to(kseg_ref[2 * count :, :], shape),
        )
        far_ref[:, columns] = jnp.where(far == query, 0.0, masked_score)


def triangle():
    key = lax.broadcasted_iota(jnp.int32, (HALF, HALF), 0)
    token = lax.broadcasted_iota(jnp.int32, (HALF, HALF), 1)
    return key <= token


def tiles_of(t, count):
    if t == 0:
        plain = 2 * count + HALF
        plain_bias = HALF
    else:
        plain = 0
        plain_bias = 0
    diagonal = t * HALF
    return plain, plain_bias, diagonal, 2 * count + diagonal


def scores_of(keys, query, t, count, near_ref, far_ref, tri):
    plain, plain_bias, own, old = tiles_of(t, count)
    columns = slice(t * HALF, (t + 1) * HALF)
    near = nt(keys(count, count), query) + near_ref[:, columns]
    far = nt(keys(plain, HALF), query) + far_ref[plain_bias : plain_bias + HALF, columns]
    edge = jnp.where(tri, nt(keys(own, HALF), query), nt(keys(old, HALF), query))
    edge = edge + far_ref[own : own + HALF, columns]
    return near, far, edge


def attend_kernel(
    q_ref, kv0_ref, kv1_ref, kv2_ref, qseg_ref, kseg_ref, o_ref, lse_ref, k_s, vt_s, near_s, far_s
):
    count = q_ref.shape[0]
    pair = pl.program_id(0)

    @pl.when(pair == 0)
    def _():
        for i, ref in enumerate((kv0_ref, kv1_ref, kv2_ref)):
            spread_heads(ref[:, :LANES], k_s, i * count)
            turn_heads(ref[:, LANES:], vt_s, i * count)
        fill_bias(qseg_ref, kseg_ref, near_s, far_s, count)

    tri = triangle()
    for t in range(count // HALF):
        plain, _, own, old = tiles_of(t, count)
        rows = slice(t * HALF, (t + 1) * HALF)
        query = q_ref[rows, :]
        turned = []
        for half in range(2):
            group = (2 * pair + half) // (HQ // KVH)
            near, far, edge = scores_of(
                lambda start, size: k_s[half, group, start : start + size, :],
                query,
                t,
                count,
                near_s,
                far_s,
                tri,
            )
            top = jnp.maximum(
                jnp.max(near, 0, keepdims=True),
                jnp.maximum(jnp.max(far, 0, keepdims=True), jnp.max(edge, 0, keepdims=True)),
            )
            near = jnp.exp(near - top)
            far = jnp.exp(far - top)
            edge = jnp.exp(edge - top)
            total = (
                jnp.sum(near, 0, keepdims=True)
                + jnp.sum(far, 0, keepdims=True)
                + jnp.sum(edge, 0, keepdims=True)
            )
            lse_ref[0, half : half + 1, rows] = top + jnp.log(total)
            mixed = nn(vt_s[group, :, count : 2 * count], near.astype(bf16))
            mixed += nn(vt_s[group, :, plain : plain + HALF], far.astype(bf16))
            mixed += nn(vt_s[group, :, own : own + HALF], jnp.where(tri, edge, 0.0).astype(bf16))
            mixed += nn(vt_s[group, :, old : old + HALF], jnp.where(tri, 0.0, edge).astype(bf16))
            turned.append(mixed * (1.0 / total))
        o_ref[rows, :] = jnp.concatenate(turned, 0).T.astype(bf16)


def attend(q, kv0, kv1, kv2, qseg, kseg):
    count = q.shape[0]
    whole = lambda p: (0, 0)
    return call(
        attend_kernel,
        (
            jax.ShapeDtypeStruct((count, HQ * HD), bf16),
            jax.ShapeDtypeStruct((PAIRS, 8, count), f32),
        ),
        4 * HQ * count * 1280 * 256,
        4 * 1024 * 1024,
        grid=(PAIRS,),
        in_specs=[
            pl.BlockSpec((count, LANES), lambda p: (0, p)),
            pl.BlockSpec(kv0.shape, whole),
            pl.BlockSpec(kv1.shape, whole),
            pl.BlockSpec(kv2.shape, whole),
            pl.BlockSpec(qseg.shape, whole),
            pl.BlockSpec(kseg.shape, whole),
        ],
        out_specs=(
            pl.BlockSpec((count, LANES), lambda p: (0, p)),
            pl.BlockSpec((1, 8, count), lambda p: (p, 0, 0)),
        ),
        scratch_shapes=[
            pltpu.VMEM((2, KVH, 3 * count, LANES), bf16),
            pltpu.VMEM((KVH, HD, 3 * count), bf16),
            pltpu.VMEM((count, count), f32),
            pltpu.VMEM((count, count), f32),
        ],
    )(q, kv0, kv1, kv2, qseg, kseg)


def attend_back_kernel(
    q_ref,
    do_ref,
    kv0_ref,
    kv1_ref,
    kv2_ref,
    qseg_ref,
    kseg_ref,
    lse_ref,
    delta_ref,
    cos_ref,
    sin_ref,
    dq_ref,
    own_ref,
    one_ref,
    two_ref,
    k_s,
    v_s,
    kt_s,
    near_s,
    far_s,
    dk_s,
    dv_s,
):
    count = q_ref.shape[0]
    pair = pl.program_id(0)

    @pl.when(pair == 0)
    def _():
        for i, ref in enumerate((kv0_ref, kv1_ref, kv2_ref)):
            spread_heads(ref[:, :LANES], k_s, i * count)
            spread_heads(ref[:, LANES:], v_s, i * count)
            turn_heads(ref[:, :LANES], kt_s, i * count)
        fill_bias(qseg_ref, kseg_ref, near_s, far_s, count)
        dk_s[...] = jnp.zeros_like(dk_s)
        dv_s[...] = jnp.zeros_like(dv_s)

    tri = triangle()
    for t in range(count // HALF):
        plain, _, own, old = tiles_of(t, count)
        rows = slice(t * HALF, (t + 1) * HALF)
        query = q_ref[rows, :]
        grad = do_ref[rows, :]
        low = lane_low(query.shape)
        turned = []
        for half in range(2):
            group = (2 * pair + half) // (HQ // KVH)
            mine = low if half == 0 else jnp.logical_not(low)
            query_half = jnp.where(mine, query.astype(f32), 0.0).astype(bf16)
            grad_half = jnp.where(mine, grad.astype(f32), 0.0).astype(bf16)
            log_total = lse_ref[0, half : half + 1, rows]
            inner = delta_ref[0, half : half + 1, rows]
            scores = scores_of(
                lambda start, size: k_s[half, group, start : start + size, :],
                query,
                t,
                count,
                near_s,
                far_s,
                tri,
            )
            near, far, edge = (jnp.exp(part - log_total) for part in scores)
            values = lambda start, size: v_s[half, group, start : start + size, :]
            near_g = near * (nt(values(count, count), grad) - inner)
            far_g = far * (nt(values(plain, HALF), grad) - inner)
            edge_p = jnp.where(tri, nt(values(own, HALF), grad), nt(values(old, HALF), grad))
            edge_g = edge * (edge_p - inner)
            blocks = (
                (count, count, near, near_g),
                (plain, HALF, far, far_g),
                (own, HALF, jnp.where(tri, edge, 0.0), jnp.where(tri, edge_g, 0.0)),
                (old, HALF, jnp.where(tri, 0.0, edge), jnp.where(tri, 0.0, edge_g)),
            )
            total = None
            for start, size, weight, change in blocks:
                change = change.astype(bf16)
                keys = slice(start, start + size)
                dv_s[group, keys, :] += nn(weight.astype(bf16), grad_half)
                dk_s[group, keys, :] += nn(change, query_half)
                part = nn(kt_s[group, :, keys], change)
                total = part if total is None else total + part
            turned.append(total)
        turned = jnp.concatenate(turned, 0).T * HD**-0.5
        back = turned * cos_ref[rows, :] - flip_lanes_half(turned * sin_ref[rows, :])
        dq_ref[rows, :] = back.astype(bf16)

    @pl.when(pair == PAIRS - 1)
    def _():
        for i, (ref, cast) in enumerate(((own_ref, f32), (one_ref, bf16), (two_ref, bf16))):
            keys = slice(i * count, (i + 1) * count)
            for j, source in enumerate((dk_s, dv_s)):
                first = source[0, keys, :]
                second = source[1, keys, :]
                first = first + pltpu.roll(first, HD, 1)
                second = second + pltpu.roll(second, HD, 1)
                both = jnp.where(lane_low(first.shape), first, second)
                ref[:, j * LANES : (j + 1) * LANES] = both.astype(cast)


def attend_back(q, do, kv0, kv1, kv2, qseg, kseg, lse, delta, cosine, sine):
    count = q.shape[0]
    whole = lambda p: (0, 0)
    lane_block = pl.BlockSpec((count, LANES), lambda p: (0, p))
    row_block = pl.BlockSpec((1, 8, count), lambda p: (p, 0, 0))
    return call(
        attend_back_kernel,
        (
            jax.ShapeDtypeStruct((count, HQ * HD), bf16),
            jax.ShapeDtypeStruct((count, 2 * LANES), f32),
            jax.ShapeDtypeStruct((count, 2 * LANES), bf16),
            jax.ShapeDtypeStruct((count, 2 * LANES), bf16),
        ),
        10 * HQ * count * 1280 * 256,
        6 * 1024 * 1024,
        grid=(PAIRS,),
        in_specs=[
            lane_block,
            lane_block,
            pl.BlockSpec(kv0.shape, whole),
            pl.BlockSpec(kv1.shape, whole),
            pl.BlockSpec(kv2.shape, whole),
            pl.BlockSpec(qseg.shape, whole),
            pl.BlockSpec(kseg.shape, whole),
            row_block,
            row_block,
            pl.BlockSpec(cosine.shape, whole),
            pl.BlockSpec(sine.shape, whole),
        ],
        out_specs=(
            lane_block,
            pl.BlockSpec((count, 2 * LANES), whole),
            pl.BlockSpec((count, 2 * LANES), whole),
            pl.BlockSpec((count, 2 * LANES), whole),
        ),
        scratch_shapes=[
            pltpu.VMEM((2, KVH, 3 * count, LANES), bf16),
            pltpu.VMEM((2, KVH, 3 * count, LANES), bf16),
            pltpu.VMEM((KVH, HD, 3 * count), bf16),
            pltpu.VMEM((count, count), f32),
            pltpu.VMEM((count, count), f32),
            pltpu.VMEM((KVH, 3 * count, LANES), f32),
            pltpu.VMEM((KVH, 3 * count, LANES), f32),
        ],
    )(q, do, kv0, kv1, kv2, qseg, kseg, lse, delta, cosine, sine)


def merge_kernel(x_ref, o_ref, w_ref, gain_ref, h1_ref, n2_ref):
    step = 256

    def body(i, carry):
        rows = pl.ds(pl.multiple_of(i * step, step), step)
        hidden = x_ref[rows, :].astype(f32) + nn(o_ref[rows, :], w_ref[...])
        h1_ref[rows, :] = hidden
        scale = lax.rsqrt(jnp.mean(hidden * hidden, -1, keepdims=True) + eps_norm)
        n2_ref[rows, :] = (hidden * scale * gain_ref[...]).astype(bf16)
        return carry

    lax.fori_loop(0, x_ref.shape[0] // step, body, 0)


def merge(x, o, w, gain):
    return call(
        merge_kernel,
        (jax.ShapeDtypeStruct(x.shape, f32), jax.ShapeDtypeStruct(x.shape, bf16)),
        2 * x.shape[0] * w.shape[0] * w.shape[1],
        6 * 1024 * 1024,
    )(x, o, w, gain)


def feed_kernel(*refs, first, width):
    me_ref, na_ref, nb_ref, ca_ref, cb_ref, wg_ref, wu_ref, wd_ref = refs[:8]
    refs = refs[8:]
    if not first:
        sums = refs[:4]
        refs = refs[4:]
    mine_ref, theirs_ref, down_ref = refs[:3]
    outs = refs[3:7]
    inner_s, gate_s, up_s, inner_t, normed_t = refs[7:]
    count = na_ref.shape[0]
    half_rows = mine_ref.shape[0] // (2 * width // LANES)
    step = 256

    for half, (normed_ref, grad_ref) in enumerate(((na_ref, ca_ref), (nb_ref, cb_ref))):
        result_ref, back_ref = outs[2 * half : 2 * half + 2]

        def body(i, carry, half=half, normed_ref=normed_ref, grad_ref=grad_ref,
                 result_ref=result_ref, back_ref=back_ref):
            rows = pl.ds(pl.multiple_of(i * step, step), step)
            both = pl.ds(pl.multiple_of(half * count + i * step, step), step)
            normed = normed_ref[rows, :]
            gate = nn(normed, wg_ref[...])
            up = nn(normed, wu_ref[...])
            change = nt(grad_ref[rows, :], wd_ref[...])
            sigmoid = 1.0 / (1.0 + jnp.exp(-gate))
            activated = gate * sigmoid
            inner = (activated * up).astype(bf16)
            gate_g = (change * up * sigmoid * (1.0 + gate * (1.0 - sigmoid))).astype(bf16)
            up_g = (change * activated).astype(bf16)
            inner_s[both, :] = inner
            gate_s[both, :] = gate_g
            up_s[both, :] = up_g
            result = nn(inner, wd_ref[...])
            back = nt(gate_g, wg_ref[...]) + nt(up_g, wu_ref[...])
            if not first:
                result = result + sums[2 * half][rows, :]
                back = back + sums[2 * half + 1][rows, :]
            result_ref[rows, :] = result
            back_ref[rows, :] = back
            return carry

        lax.fori_loop(0, count // step, body, 0)
        normed_t[:, half * count : (half + 1) * count] = normed_ref[...].T
        inner_t[:, half * count : (half + 1) * count] = inner_s[half * count : (half + 1) * count, :].T

    me = me_ref[0]
    start = 0
    while start < width:
        size = min(HALF, width - start)
        columns = slice(start, start + size)
        for kind, source in enumerate((gate_s, up_s)):
            grads = nn(normed_t[...], source[:, columns]).astype(bf16)
            for j in range(size // LANES):
                row = (kind * width // LANES + start // LANES + j) * half_rows
                tile = grads[:, j * LANES : (j + 1) * LANES]

                @pl.when(me == 0)
                def _():
                    mine_ref[row : row + half_rows, :] = tile[:half_rows]
                    theirs_ref[row : row + half_rows, :] = tile[half_rows:]

                @pl.when(me == 1)
                def _():
                    mine_ref[row : row + half_rows, :] = tile[half_rows:]
                    theirs_ref[row : row + half_rows, :] = tile[:half_rows]

        down = nn(inner_t[columns, :count], ca_ref[...]) + nn(inner_t[columns, count:], cb_ref[...])
        down = down.astype(bf16)
        for j in range(down.shape[1] // LANES):
            row = j * width + start
            down_ref[row : row + size, :] = down[:, j * LANES : (j + 1) * LANES]
        start += size


def feed(me, na, nb, ca, cb, wg, wu, wd, sums):
    count, features = na.shape
    width = wg.shape[1]
    rows = features * width // LANES
    first = sums is None
    spec = pl.BlockSpec(memory_space=pltpu.VMEM)
    sums = () if first else tuple(sums)
    token_out = jax.ShapeDtypeStruct((count, features), f32)
    return call(
        functools.partial(feed_kernel, first=first, width=width),
        (jax.ShapeDtypeStruct((rows, LANES), bf16),) * 3 + (token_out,) * 4,
        18 * 2 * count * features * width,
        40 * 1024 * 1024,
        in_specs=[pl.BlockSpec(memory_space=pltpu.SMEM)] + [spec] * (7 + len(sums)),
        out_specs=(spec,) * 7,
        scratch_shapes=[
            pltpu.VMEM((2 * count, width), bf16),
            pltpu.VMEM((2 * count, width), bf16),
            pltpu.VMEM((2 * count, width), bf16),
            pltpu.VMEM((width, 2 * count), bf16),
            pltpu.VMEM((features, 2 * count), bf16),
        ],
        input_output_aliases={} if first else {8 + i: 3 + i for i in range(4)},
    )(me, na, nb, ca, cb, wg, wu, wd, *sums)


def middle_kernel(
    me_ref, part_ref, got_ref, h1_ref, dy_ref, gain_ref, w_ref, o_ref, heads_ref,
    dh1_ref, do_ref, delta_ref, gg_ref, mine_ref, theirs_ref, low_s, ot_s,
):
    count, features = part_ref.shape
    step = 256
    gg_ref[...] = jnp.zeros_like(gg_ref)

    def body(i, carry):
        rows = pl.ds(pl.multiple_of(i * step, step), step)
        back = part_ref[rows, :] + got_ref[rows, :].astype(f32)
        hidden = h1_ref[rows, :]
        scale = lax.rsqrt(jnp.mean(hidden * hidden, -1, keepdims=True) + eps_norm)
        normal = hidden * scale
        gg_ref[...] += jnp.sum(back * normal, 0, keepdims=True)
        change = back * gain_ref[...]
        grad = dy_ref[rows, :].astype(f32) + scale * (
            change - normal * jnp.mean(change * normal, -1, keepdims=True)
        )
        dh1_ref[rows, :] = grad
        low = grad.astype(bf16)
        low_s[rows, :] = low
        attn_g = nt(low, w_ref[...]).astype(bf16)
        do_ref[rows, :] = attn_g
        product = attn_g.astype(f32) * o_ref[rows, :].astype(f32)
        sums = lax.dot_general(
            heads_ref[...], product, (((1,), (1,)), ((), ())),
            precision=lax.Precision.HIGHEST, preferred_element_type=f32,
        )
        delta_ref[:, rows] = sums
        return carry

    lax.fori_loop(0, count // step, body, 0)
    ot_s[...] = o_ref[...].T
    store_split(me_ref, nn(ot_s[...], low_s[...]).astype(bf16), mine_ref, theirs_ref, 0)


def store_split(me_ref, grads, mine_ref, theirs_ref, first_tile):
    half_rows = grads.shape[0] // 2
    me = me_ref[0]
    for j in range(grads.shape[1] // LANES):
        row = (first_tile + j) * half_rows
        tile = grads[:, j * LANES : (j + 1) * LANES]

        @pl.when(me == 0)
        def _():
            mine_ref[row : row + half_rows, :] = tile[:half_rows]
            theirs_ref[row : row + half_rows, :] = tile[half_rows:]

        @pl.when(me == 1)
        def _():
            mine_ref[row : row + half_rows, :] = tile[half_rows:]
            theirs_ref[row : row + half_rows, :] = tile[:half_rows]


def middle(me, part, got, h1, dy, gain, w, o, heads):
    count, features = part.shape
    spec = pl.BlockSpec(memory_space=pltpu.VMEM)
    rows = (features // 2) * (features // LANES)
    return call(
        middle_kernel,
        (
            jax.ShapeDtypeStruct((count, features), f32),
            jax.ShapeDtypeStruct((count, HQ * HD), bf16),
            jax.ShapeDtypeStruct((heads.shape[0], count), f32),
            jax.ShapeDtypeStruct((1, features), f32),
            jax.ShapeDtypeStruct((rows, LANES), bf16),
            jax.ShapeDtypeStruct((rows, LANES), bf16),
        ),
        4 * count * features * features,
        12 * 1024 * 1024,
        in_specs=[pl.BlockSpec(memory_space=pltpu.SMEM)] + [spec] * 8,
        out_specs=(spec,) * 6,
        scratch_shapes=[pltpu.VMEM((count, features), bf16), pltpu.VMEM((HQ * HD, count), bf16)],
    )(me, part, got, h1, dy, gain, w, o, heads)


def last_kernel(
    me_ref, dq_ref, own_ref, one_ref, two_ref, n1_ref, x_ref, gain_ref, w_ref, dh1_ref, cos_ref, sin_ref,
    dx_ref, gg_ref, gb_ref, mine_ref, theirs_ref, dp_s, n1t_s,
):
    count, features = n1_ref.shape
    width = HQ * HD
    step = 256
    gg_ref[...] = jnp.zeros_like(gg_ref)
    gb_ref[...] = jnp.zeros_like(gb_ref)

    def body(i, carry):
        rows = pl.ds(pl.multiple_of(i * step, step), step)
        pairs = own_ref[rows, :] + one_ref[rows, :].astype(f32) + two_ref[rows, :].astype(f32)
        key = pairs[:, :LANES]
        key = key * cos_ref[rows, :] - flip_lanes_half(key * sin_ref[rows, :])
        dp_s[rows, :width] = dq_ref[rows, :]
        dp_s[rows, width : width + LANES] = key.astype(bf16)
        dp_s[rows, width + LANES :] = pairs[:, LANES:].astype(bf16)
        grads = dp_s[rows, :]
        gb_ref[...] += jnp.sum(grads.astype(f32), 0, keepdims=True)
        back = nt(grads, w_ref[...])
        x = x_ref[rows, :].astype(f32)
        scale = lax.rsqrt(jnp.mean(x * x, -1, keepdims=True) + eps_norm)
        normal = x * scale
        gg_ref[...] += jnp.sum(back * normal, 0, keepdims=True)
        change = back * gain_ref[...]
        grad = dh1_ref[rows, :] + scale * (
            change - normal * jnp.mean(change * normal, -1, keepdims=True)
        )
        dx_ref[rows, :] = grad.astype(bf16)
        return carry

    lax.fori_loop(0, count // step, body, 0)
    n1t_s[...] = n1_ref[...].T
    store_split(me_ref, nn(n1t_s[...], dp_s[...]).astype(bf16), mine_ref, theirs_ref, 0)


def last(me, dq, own, one, two, n1, x, gain, w, dh1, cosine, sine):
    count, features = n1.shape
    spec = pl.BlockSpec(memory_space=pltpu.VMEM)
    rows = (features // 2) * (w.shape[1] // LANES)
    return call(
        last_kernel,
        (
            jax.ShapeDtypeStruct((count, features), bf16),
            jax.ShapeDtypeStruct((1, features), f32),
            jax.ShapeDtypeStruct((1, w.shape[1]), f32),
            jax.ShapeDtypeStruct((rows, LANES), bf16),
            jax.ShapeDtypeStruct((rows, LANES), bf16),
        ),
        4 * count * features * w.shape[1],
        14 * 1024 * 1024,
        in_specs=[pl.BlockSpec(memory_space=pltpu.SMEM)] + [spec] * 11,
        out_specs=(spec,) * 5,
        scratch_shapes=[
            pltpu.VMEM((count, w.shape[1]), bf16),
            pltpu.VMEM((features, count), bf16),
        ],
    )(me, dq, own, one, two, n1, x, gain, w, dh1, cosine, sine)


def swap(values):
    return lax.ppermute(values, "fsdp", [(0, 1), (1, 0)])


def flip(values, dim):
    axis, bit = dim
    size = lax.axis_size(axis)
    return lax.ppermute(values, axis, [(i, i ^ (1 << bit)) for i in range(size)])


def side(dim):
    axis, bit = dim
    return (lax.axis_index(axis) >> bit) & 1


def add(*terms):
    total = terms[0].astype(f32)
    for term in terms[1:]:
        total = total + term.astype(f32)
    return total.astype(bf16)


def take(array, index):
    return lax.dynamic_index_in_dim(array, index, 0, False)


def join(low, other, index):
    out = jnp.zeros((2,) + low.shape, low.dtype)
    out = lax.dynamic_update_index_in_dim(out, low, index, 0)
    return lax.dynamic_update_index_in_dim(out, other, 1 - index, 0)


def other_dims(dims):
    every = []
    for axis in ("seq", "ctx"):
        for bit in range(lax.axis_size(axis).bit_length() - 1):
            every.append((axis, bit))
    return [dim for dim in every if dim not in dims]


def sum_part(part, dims):
    rows = part.shape[0]
    one, two, three = dims
    a, b, c = (side(dim) for dim in dims)
    whole = part.reshape(2, 2, 2, rows // 8, LANES)
    got_one = flip(take(whole, 1 - a), one)
    kept = take(whole, a)
    got_two = flip(add(take(kept, 1 - b), take(got_one, 1 - b)), two)
    kept, got_one = take(kept, b), take(got_one, b)
    got_three = flip(add(take(kept, 1 - c), take(got_one, 1 - c), take(got_two, 1 - c)), three)
    total = add(take(kept, c), take(got_one, c), take(got_two, c), got_three)
    for dim in other_dims(dims):
        total = add(total, flip(total, dim))
    total = join(total, flip(total, three), c)
    total = join(total, flip(total, two), b)
    total = join(total, flip(total, one), a)
    return total.reshape(rows, LANES)


X, Y, Z = ("seq", 0), ("seq", 1), ("ctx", 0)


def untile(flat, tiles):
    rows = flat.shape[0] // tiles
    return flat.reshape(tiles, rows, LANES).transpose(1, 0, 2).reshape(rows, tiles * LANES)


def on_device(
    block_input,
    segment_ids,
    out_cotangent,
    input_gain,
    query_weight,
    query_bias,
    key_weight,
    key_bias,
    value_weight,
    value_bias,
    output_weight,
    middle_gain,
    gate_weight,
    up_weight,
    down_weight,
):
    me = lax.axis_index("fsdp")
    ctx = lax.axis_index("ctx")
    chunks = lax.axis_size("ctx")
    me_array = me.astype(jnp.int32).reshape(1)
    x = block_input[0]
    dy = out_cotangent[0]
    count, features = x.shape
    hidden = down_weight.shape[0]
    own_rows = query_weight.shape[0]
    kv_width = KVH * HD

    def whole(own, other):
        return join(own, other, me).reshape((2 * own.shape[0],) + own.shape[1:])

    projection = jnp.concatenate([query_weight, key_weight, value_weight], 1)
    w_in = whole(projection, swap(projection))
    vectors = jnp.concatenate([input_gain, query_bias, key_bias, value_bias, middle_gain])
    sizes = [v.shape[0] for v in (input_gain, query_bias, key_bias, value_bias, middle_gain)]
    other_vectors = swap(vectors)
    params = []
    place = 0
    for size in sizes:
        mine, theirs = vectors[place : place + size], other_vectors[place : place + size]
        pair = jnp.where(
            me == 0, jnp.concatenate([mine, theirs]), jnp.concatenate([theirs, mine])
        )
        params.append(pair.astype(f32)[None])
        place += size
    gain_one, b_query, b_key, b_value, gain_two = params
    bias = jnp.concatenate([b_query, b_key, b_value], 1)
    w_out = whole(output_weight, swap(output_weight))
    dy_other = swap(dy)

    first = ctx * count
    positions = (first + jnp.arange(count, dtype=jnp.int32)).astype(f32)
    inverse = theta_base ** (-jnp.arange(0, HD, 2, dtype=f32) / HD)
    angle = positions[:, None] * jnp.tile(inverse, LANES // inverse.shape[0])[None, :]
    cosine, sine = jnp.cos(angle), jnp.sin(angle)

    n1, q, kv = project(x, gain_one, w_in, bias, cosine, sine)

    reach = WINDOW // count
    before = [
        lax.ppermute(kv, "ctx", [(i, i + d) for i in range(chunks - d)])
        for d in range(1, reach + 1)
    ]
    seg_row = segment_ids[0]
    padded = jnp.concatenate([jnp.full((reach * count,), -1, jnp.int32), seg_row])
    query_seg = lax.dynamic_slice_in_dim(seg_row, first, count, 0)[None]
    key_seg = jnp.concatenate(
        [
            lax.dynamic_slice_in_dim(padded, first + (reach - d) * count, count, 0)
            for d in range(reach + 1)
        ]
    )[:, None]
    o, lse = attend(q, kv, *before, query_seg, key_seg)
    h1, n2 = merge(x, o, w_out, gain_two)
    n2_other = swap(n2)

    widths = (768, 768, 896)
    place = 0
    sums = None
    parts = []
    for width in widths:
        gate_up = []
        for weight in (gate_weight, up_weight):
            kept = lax.dynamic_slice_in_dim(weight, me * hidden + place, width, 1)
            sent = lax.dynamic_slice_in_dim(weight, (1 - me) * hidden + place, width, 1)
            gate_up.append(whole(kept, swap(sent)))
        down = down_weight[place : place + width]
        mine, theirs, down_grad, *sums = feed(
            me_array, n2, n2_other, dy, dy_other, *gate_up, down, sums
        )
        parts.append((down_grad, mine, swap(theirs)))
        place += width
    result_own, back_own, result_other, back_other = sums
    result = h1 + result_own + swap(result_other.astype(bf16)).astype(f32)
    block_output = result.astype(bf16)[None]

    row = jnp.arange(PAIRS * 8)[:, None]
    column = jnp.arange(HQ * HD)[None, :]
    heads = ((column // HD) == (row // 8) * 2 + row % 8) & (row % 8 < 2)
    dh1, do, delta, gg_two, out_mine, out_theirs = middle(
        me_array, back_own, swap(back_other.astype(bf16)), h1, dy, gain_two, w_out, o, heads.astype(f32)
    )
    delta = delta.reshape(PAIRS, 8, count)
    dq, own_pairs, *sent_pairs = attend_back(
        q, do, kv, *before, query_seg, key_seg, lse, delta, cosine, sine
    )
    got_pairs = [
        lax.ppermute(pairs, "ctx", [(i + d, i) for i in range(chunks - d)])
        for d, pairs in enumerate(sent_pairs, 1)
    ]
    dx, gg_one, g_bias, in_mine, in_theirs = last(
        me_array, dq, own_pairs, *got_pairs, n1, x, gain_one, w_in, dh1, cosine, sine
    )
    input_grad = dx[None]

    gates = jnp.zeros((own_rows, 2 * hidden), f32)
    ups = jnp.zeros((own_rows, 2 * hidden), f32)
    downs = []
    place = 0
    for width, (down_grad, mine, theirs) in zip(widths, parts):
        down_sum = sum_part(down_grad, (X, Y, Z))
        mine_sum = sum_part(mine, (Y, Z, X))
        theirs_sum = sum_part(theirs, (Z, X, Y))
        tiles = width // LANES
        for total, owner in ((mine_sum, me), (theirs_sum, 1 - me)):
            half = total.shape[0] // 2
            at = owner * hidden + place
            gates = lax.dynamic_update_slice(
                gates, untile(total[:half], tiles).astype(f32), (jnp.int32(0), at)
            )
            ups = lax.dynamic_update_slice(
                ups, untile(total[half:], tiles).astype(f32), (jnp.int32(0), at)
            )
        downs.append(untile(down_sum, features // LANES).astype(f32))
        place += width
    gw_down = jnp.concatenate(downs, 0)

    gw_out = lax.psum(add(out_mine, swap(out_theirs)), ("seq", "ctx"))
    gw_out = untile(gw_out, features // LANES).astype(f32)
    gw_in = lax.psum(add(in_mine, swap(in_theirs)), ("seq", "ctx"))
    gw_in = untile(gw_in, (HQ * HD + 2 * kv_width) // LANES).astype(f32)
    width = HQ * HD
    small = [
        gg_one[0],
        g_bias[0, :width],
        g_bias[0, width : width + kv_width],
        g_bias[0, width + kv_width :],
        gg_two[0],
    ]
    small_sums = lax.psum(jnp.concatenate(small), ("seq", "ctx", "fsdp"))
    shares = []
    place = 0
    for vector in small:
        size = vector.shape[0]
        total = small_sums[place : place + size]
        shares.append(lax.dynamic_slice_in_dim(total, me * (size // 2), size // 2, 0))
        place += size
    gg_one, gb_query, gb_key, gb_value, gg_two = shares
    return (
        block_output,
        input_grad,
        gg_one,
        gw_in[:, :width],
        gb_query,
        gw_in[:, width : width + kv_width],
        gb_key,
        gw_in[:, width + kv_width :],
        gb_value,
        gw_out,
        gg_two,
        gates,
        ups,
        gw_down,
    )


def solution(mesh):
    return jax.shard_map(
        on_device,
        mesh=mesh,
        in_specs=(
            P(("seq", "fsdp"), "ctx", None),
            P(("seq", "fsdp"), None),
            P(("seq", "fsdp"), "ctx", None),
            P("fsdp"),
            P("fsdp", None),
            P("fsdp"),
            P("fsdp", None),
            P("fsdp"),
            P("fsdp", None),
            P("fsdp"),
            P("fsdp", None),
            P("fsdp"),
            P("fsdp", None),
            P("fsdp", None),
            P("fsdp", None),
        ),
        out_specs=(
            P(("seq", "fsdp"), "ctx", None),
            P(("seq", "fsdp"), "ctx", None),
            P("fsdp"),
            P("fsdp", None),
            P("fsdp"),
            P("fsdp", None),
            P("fsdp"),
            P("fsdp", None),
            P("fsdp"),
            P("fsdp", None),
            P("fsdp"),
            P("fsdp", None),
            P("fsdp", None),
            P("fsdp", None),
        ),
        check_vma=False,
    )
```

```python
import functools

import jax
import jax.numpy as jnp
from jax import lax
from jax.experimental import pallas as pl
from jax.experimental.pallas import tpu as pltpu
from jax.sharding import PartitionSpec as P

HQ = 14
KVH = 2
HD = 64
WINDOW = 1024
PAIRS = HQ // 2
LANES = 128
HALF = 256

theta_base = 1000000.0
eps_norm = 1e-06
masked_score = -1e30
f32 = jnp.float32
bf16 = jnp.bfloat16
VMEM_BYTES = 58 * 1024 * 1024
WIDTHS = (1280, 1152)


def nn(a, b):
    return lax.dot_general(a, b, (((1,), (0,)), ((), ())), preferred_element_type=f32)


def nt(a, b):
    return lax.dot_general(a, b, (((1,), (1,)), ((), ())), preferred_element_type=f32)


def tn(a, b):
    return lax.dot_general(a, b, (((0,), (0,)), ((), ())), preferred_element_type=f32)


def flip_lanes_half(values):
    width = values.shape[-1]
    lane = lax.broadcasted_iota(jnp.int32, values.shape, len(values.shape) - 1)
    up = pltpu.roll(values, width - 32, len(values.shape) - 1)
    down = pltpu.roll(values, 32, len(values.shape) - 1)
    return jnp.where((lane & 63) < 32, -up, down)


def call(kernel, out_shape, flops, moved, **kwargs):
    return pl.pallas_call(
        kernel,
        out_shape=out_shape,
        compiler_params=pltpu.CompilerParams(vmem_limit_bytes=VMEM_BYTES),
        cost_estimate=pl.CostEstimate(flops=flops, bytes_accessed=moved, transcendentals=0),
        **kwargs,
    )


GAIN_ONE = slice(0, 896)
BIAS = slice(896, 2048)
GAIN_TWO = slice(2048, 2944)


def place_rows(target, own_ref, other_ref, me, columns=slice(None)):
    rows = own_ref.shape[0]
    target[pl.ds(pl.multiple_of(me * rows, rows), rows), columns] = own_ref[...]
    target[pl.ds(pl.multiple_of((1 - me) * rows, rows), rows), columns] = other_ref[...]


def project_kernel(
    place_ref, x_ref, params_ref, wq_ref, wk_ref, wv_ref, oq_ref, ok_ref, ov_ref, cos_ref, sin_ref,
    n1_ref, q_ref, kv_ref, w_ref,
):
    count = x_ref.shape[0]
    step = 256
    me = place_ref[0]
    width = HQ * HD
    place_rows(w_ref, wq_ref, oq_ref, me, slice(0, width))
    place_rows(w_ref, wk_ref, ok_ref, me, slice(width, width + LANES))
    place_rows(w_ref, wv_ref, ov_ref, me, slice(width + LANES, width + 2 * LANES))

    def body(i, carry):
        rows = pl.ds(pl.multiple_of(i * step, step), step)
        x = x_ref[rows, :].astype(f32)
        scale = lax.rsqrt(jnp.mean(x * x, -1, keepdims=True) + eps_norm)
        normed = (x * scale * params_ref[:, GAIN_ONE]).astype(bf16)
        n1_ref[rows, :] = normed
        cosine = cos_ref[rows, :]
        sine = sin_ref[rows, :]
        out = nn(normed, w_ref[...]) + params_ref[:, BIAS]
        for j in range(PAIRS + 1):
            part = out[:, j * LANES : (j + 1) * LANES]
            part = part * cosine + flip_lanes_half(part) * sine
            if j < PAIRS:
                q_ref[rows, j * LANES : (j + 1) * LANES] = (part * HD**-0.5).astype(bf16)
            else:
                kv_ref[rows, :LANES] = part.astype(bf16)
        kv_ref[rows, LANES:] = out[:, (PAIRS + 1) * LANES :].astype(bf16)
        return carry

    lax.fori_loop(0, count // step, body, 0)


def in_vmem(n):
    return [pl.BlockSpec(memory_space=pltpu.SMEM)] + [pl.BlockSpec(memory_space=pltpu.VMEM)] * n


def project(place, x, params, own, other, cosine, sine):
    count, width = x.shape
    columns = sum(w.shape[1] for w in own)
    return call(
        project_kernel,
        (
            jax.ShapeDtypeStruct((count, width), bf16),
            jax.ShapeDtypeStruct((count, HQ * HD), bf16),
            jax.ShapeDtypeStruct((count, 2 * KVH * HD), bf16),
            jax.ShapeDtypeStruct((width, columns), bf16),
        ),
        2 * count * width * columns,
        6 * 1024 * 1024,
        in_specs=in_vmem(10),
    )(place, x, params, *own, *other, cosine, sine)


def lane_low(shape):
    return lax.broadcasted_iota(jnp.int32, shape, len(shape) - 1) < HD


def spread_heads(source, target, row):
    values = source.astype(f32)
    other = pltpu.roll(values, HD, 1)
    low = lane_low(values.shape)
    rows = pl.ds(row, values.shape[0])
    target[0, 0, rows, :] = jnp.where(low, values, 0.0).astype(bf16)
    target[1, 0, rows, :] = jnp.where(low, 0.0, other).astype(bf16)
    target[0, 1, rows, :] = jnp.where(low, other, 0.0).astype(bf16)
    target[1, 1, rows, :] = jnp.where(low, 0.0, values).astype(bf16)


def turn_heads(source, target, column):
    values = source.astype(f32).T.astype(bf16)
    columns = pl.ds(column, values.shape[1])
    target[0, :, columns] = values[:HD]
    target[1, :, columns] = values[HD:]


def fill_bias(place_ref, seg_ref, near_ref, far_ref, count):
    ctx = place_ref[3]

    def segments(back):
        start = pl.multiple_of(jnp.maximum(ctx - back, 0) * count, count)
        row = seg_ref[:, pl.ds(start, count)].astype(f32)
        row = jnp.where(ctx >= back, row, -1.0)
        return row, jnp.broadcast_to(row, (LANES, count)).T

    own_row, own = segments(0)
    _, one = segments(1)
    _, two = segments(2)
    for t in range(count // LANES):
        columns = slice(t * LANES, (t + 1) * LANES)
        query = own_row[:, columns]
        near_ref[:, columns] = jnp.where(one == query, 0.0, masked_score)
        key = lax.broadcasted_iota(jnp.int32, (count, LANES), 0)
        token = lax.broadcasted_iota(jnp.int32, (count, LANES), 1) + t * LANES
        far = jnp.where(key <= token, own, two)
        far_ref[:, columns] = jnp.where(far == query, 0.0, masked_score)


def triangle():
    key = lax.broadcasted_iota(jnp.int32, (HALF, HALF), 0)
    token = lax.broadcasted_iota(jnp.int32, (HALF, HALF), 1)
    return key <= token


def tiles_of(t, count):
    if t == 0:
        plain = 2 * count + HALF
        plain_bias = HALF
    else:
        plain = 0
        plain_bias = 0
    diagonal = t * HALF
    return plain, plain_bias, diagonal, 2 * count + diagonal


def scores_of(keys, query, t, count, near_ref, far_ref, tri):
    plain, plain_bias, own, old = tiles_of(t, count)
    columns = slice(t * HALF, (t + 1) * HALF)
    near = nt(keys(count, count), query) + near_ref[:, columns]
    far = nt(keys(plain, HALF), query) + far_ref[plain_bias : plain_bias + HALF, columns]
    edge = jnp.where(tri, nt(keys(own, HALF), query), nt(keys(old, HALF), query))
    edge = edge + far_ref[own : own + HALF, columns]
    return near, far, edge


def attend_kernel(
    place_ref, q_ref, kv0_ref, kv1_ref, kv2_ref, seg_ref, o_ref, lse_ref, k_s, vt_s, near_s, far_s
):
    count = q_ref.shape[0]
    pair = pl.program_id(0)

    @pl.when(pair == 0)
    def _():
        for i, ref in enumerate((kv0_ref, kv1_ref, kv2_ref)):
            spread_heads(ref[:, :LANES], k_s, i * count)
            turn_heads(ref[:, LANES:], vt_s, i * count)
        fill_bias(place_ref, seg_ref, near_s, far_s, count)

    tri = triangle()
    for t in range(count // HALF):
        plain, _, own, old = tiles_of(t, count)
        rows = slice(t * HALF, (t + 1) * HALF)
        query = q_ref[rows, :]
        turned = []
        for half in range(2):
            group = (2 * pair + half) // (HQ // KVH)
            near, far, edge = scores_of(
                lambda start, size: k_s[half, group, start : start + size, :],
                query,
                t,
                count,
                near_s,
                far_s,
                tri,
            )
            top = jnp.maximum(
                jnp.max(near, 0, keepdims=True),
                jnp.maximum(jnp.max(far, 0, keepdims=True), jnp.max(edge, 0, keepdims=True)),
            )
            near = jnp.exp(near - top)
            far = jnp.exp(far - top)
            edge = jnp.exp(edge - top)
            total = (
                jnp.sum(near, 0, keepdims=True)
                + jnp.sum(far, 0, keepdims=True)
                + jnp.sum(edge, 0, keepdims=True)
            )
            lse_ref[0, half : half + 1, rows] = top + jnp.log(total)
            mixed = nn(vt_s[group, :, count : 2 * count], near.astype(bf16))
            mixed += nn(vt_s[group, :, plain : plain + HALF], far.astype(bf16))
            mixed += nn(vt_s[group, :, own : own + HALF], jnp.where(tri, edge, 0.0).astype(bf16))
            mixed += nn(vt_s[group, :, old : old + HALF], jnp.where(tri, 0.0, edge).astype(bf16))
            turned.append(mixed * (1.0 / total))
        o_ref[rows, :] = jnp.concatenate(turned, 0).T.astype(bf16)


def attend(place, q, kv0, kv1, kv2, seg):
    count = q.shape[0]
    whole = lambda p: (0, 0)
    return call(
        attend_kernel,
        (
            jax.ShapeDtypeStruct((count, HQ * HD), bf16),
            jax.ShapeDtypeStruct((PAIRS, 8, count), f32),
        ),
        4 * HQ * count * 1280 * 256,
        4 * 1024 * 1024,
        grid=(PAIRS,),
        in_specs=[
            pl.BlockSpec(memory_space=pltpu.SMEM),
            pl.BlockSpec((count, LANES), lambda p: (0, p)),
            pl.BlockSpec(kv0.shape, whole),
            pl.BlockSpec(kv1.shape, whole),
            pl.BlockSpec(kv2.shape, whole),
            pl.BlockSpec(seg.shape, whole),
        ],
        out_specs=(
            pl.BlockSpec((count, LANES), lambda p: (0, p)),
            pl.BlockSpec((1, 8, count), lambda p: (p, 0, 0)),
        ),
        scratch_shapes=[
            pltpu.VMEM((2, KVH, 3 * count, LANES), bf16),
            pltpu.VMEM((KVH, HD, 3 * count), bf16),
            pltpu.VMEM((count, count), f32),
            pltpu.VMEM((count, count), f32),
        ],
    )(place, q, kv0, kv1, kv2, seg)


def attend_back_kernel(*refs, first_pair, first, final):
    (place_ref, q_ref, do_ref, kv0_ref, kv1_ref, kv2_ref, seg_ref, lse_ref, cos_ref, sin_ref) = refs[:10]
    refs = refs[10:]
    if not first:
        dk_in, dv_in = refs[:2]
        refs = refs[2:]
    dq_ref = refs[0]
    refs = refs[1:]
    if final:
        own_ref, one_ref, two_ref = refs[:3]
        refs = refs[3:]
        k_s, v_s, kt_s, near_s, far_s, dk_s, dv_s = refs
    else:
        dk_s, dv_s = refs[:2]
        k_s, v_s, kt_s, near_s, far_s = refs[2:]
    count = q_ref.shape[0]
    step = pl.program_id(0)
    pair = step + first_pair

    @pl.when(step == 0)
    def _():
        for i, ref in enumerate((kv0_ref, kv1_ref, kv2_ref)):
            spread_heads(ref[:, :LANES], k_s, i * count)
            spread_heads(ref[:, LANES:], v_s, i * count)
            turn_heads(ref[:, :LANES], kt_s, i * count)
        fill_bias(place_ref, seg_ref, near_s, far_s, count)
        if first:
            dk_s[...] = jnp.zeros_like(dk_s)
            dv_s[...] = jnp.zeros_like(dv_s)
        else:
            dk_s[...] = dk_in[...]
            dv_s[...] = dv_in[...]

    tri = triangle()
    for t in range(count // HALF):
        plain, _, own, old = tiles_of(t, count)
        rows = slice(t * HALF, (t + 1) * HALF)
        query = q_ref[rows, :]
        grad = do_ref[rows, :]
        low = lane_low(query.shape)
        turned = []
        for half in range(2):
            group = (2 * pair + half) // (HQ // KVH)
            mine = low if half == 0 else jnp.logical_not(low)
            query_half = jnp.where(mine, query.astype(f32), 0.0).astype(bf16)
            grad_half = jnp.where(mine, grad.astype(f32), 0.0).astype(bf16)
            log_total = lse_ref[0, half : half + 1, rows]
            scores = scores_of(
                lambda start, size: k_s[half, group, start : start + size, :],
                query,
                t,
                count,
                near_s,
                far_s,
                tri,
            )
            near, far, edge = (jnp.exp(part - log_total) for part in scores)
            values = lambda start, size: v_s[half, group, start : start + size, :]
            near_p = nt(values(count, count), grad)
            far_p = nt(values(plain, HALF), grad)
            edge_p = jnp.where(tri, nt(values(own, HALF), grad), nt(values(old, HALF), grad))
            inner = (
                jnp.sum(near * near_p, 0, keepdims=True)
                + jnp.sum(far * far_p, 0, keepdims=True)
                + jnp.sum(edge * edge_p, 0, keepdims=True)
            )
            near_g = near * (near_p - inner)
            far_g = far * (far_p - inner)
            edge_g = edge * (edge_p - inner)
            blocks = (
                (count, count, near, near_g),
                (plain, HALF, far, far_g),
                (own, HALF, jnp.where(tri, edge, 0.0), jnp.where(tri, edge_g, 0.0)),
                (old, HALF, jnp.where(tri, 0.0, edge), jnp.where(tri, 0.0, edge_g)),
            )
            total = None
            for start, size, weight, change in blocks:
                change = change.astype(bf16)
                keys = slice(start, start + size)
                dv_s[group, keys, :] += nn(weight.astype(bf16), grad_half)
                dk_s[group, keys, :] += nn(change, query_half)
                part = nn(kt_s[group, :, keys], change)
                total = part if total is None else total + part
            turned.append(total)
        turned = jnp.concatenate(turned, 0).T * HD**-0.5
        back = turned * cos_ref[rows, :] - flip_lanes_half(turned * sin_ref[rows, :])
        dq_ref[rows, :] = back.astype(bf16)

    if final:

        @pl.when(pair == PAIRS - 1)
        def _():
            for i, (ref, cast) in enumerate(((own_ref, f32), (one_ref, bf16), (two_ref, bf16))):
                keys = slice(i * count, (i + 1) * count)
                for j, source in enumerate((dk_s, dv_s)):
                    one = source[0, keys, :]
                    two = source[1, keys, :]
                    one = one + pltpu.roll(one, HD, 1)
                    two = two + pltpu.roll(two, HD, 1)
                    both = jnp.where(lane_low(one.shape), one, two)
                    ref[:, j * LANES : (j + 1) * LANES] = both.astype(cast)


def attend_back(place, q, do, kv0, kv1, kv2, seg, lse, cosine, sine, sums, *, first_pair, pairs):
    count = q.shape[0]
    first = sums is None
    final = first_pair + pairs == PAIRS
    sums = () if first else tuple(sums)
    whole = lambda p: (0, 0)
    stacked = pl.BlockSpec((KVH, 3 * count, LANES), lambda p: (0, 0, 0))
    lane_block = pl.BlockSpec((count, LANES), lambda p: (0, p + first_pair))
    row_block = pl.BlockSpec((1, 8, count), lambda p: (p + first_pair, 0, 0))
    token_block = pl.BlockSpec((count, 2 * LANES), whole)
    stack = jax.ShapeDtypeStruct((KVH, 3 * count, LANES), f32)
    if final:
        outs = [jax.ShapeDtypeStruct((count, 2 * LANES), t) for t in (f32, bf16, bf16)]
        out_specs = [token_block] * 3
        scratch = [pltpu.VMEM(stack.shape, f32)] * 2
    else:
        outs = [stack, stack]
        out_specs = [stacked] * 2
        scratch = []
    return call(
        functools.partial(attend_back_kernel, first_pair=first_pair, first=first, final=final),
        (jax.ShapeDtypeStruct((count, pairs * LANES), bf16), *outs),
        10 * 2 * pairs * count * 1280 * 256,
        6 * 1024 * 1024,
        grid=(pairs,),
        in_specs=[
            pl.BlockSpec(memory_space=pltpu.SMEM),
            lane_block,
            lane_block,
            pl.BlockSpec(kv0.shape, whole),
            pl.BlockSpec(kv1.shape, whole),
            pl.BlockSpec(kv2.shape, whole),
            pl.BlockSpec(seg.shape, whole),
            row_block,
            pl.BlockSpec(cosine.shape, whole),
            pl.BlockSpec(sine.shape, whole),
        ]
        + [stacked] * len(sums),
        out_specs=(pl.BlockSpec((count, LANES), lambda p: (0, p)), *out_specs),
        scratch_shapes=[
            pltpu.VMEM((2, KVH, 3 * count, LANES), bf16),
            pltpu.VMEM((2, KVH, 3 * count, LANES), bf16),
            pltpu.VMEM((KVH, HD, 3 * count), bf16),
            pltpu.VMEM((count, count), f32),
            pltpu.VMEM((count, count), f32),
        ]
        + scratch,
    )(place, q, do, kv0, kv1, kv2, seg, lse, cosine, sine, *sums)


def merge_kernel(place_ref, x_ref, o_ref, own_ref, other_ref, params_ref, h1_ref, n2_ref, w_ref):
    step = 256
    place_rows(w_ref, own_ref, other_ref, place_ref[0])

    def body(i, carry):
        rows = pl.ds(pl.multiple_of(i * step, step), step)
        hidden = x_ref[rows, :].astype(f32) + nn(o_ref[rows, :], w_ref[...])
        h1_ref[rows, :] = hidden
        scale = lax.rsqrt(jnp.mean(hidden * hidden, -1, keepdims=True) + eps_norm)
        n2_ref[rows, :] = (hidden * scale * params_ref[:, GAIN_TWO]).astype(bf16)
        return carry

    lax.fori_loop(0, x_ref.shape[0] // step, body, 0)


def merge(place, x, o, own, other, params):
    return call(
        merge_kernel,
        (
            jax.ShapeDtypeStruct(x.shape, f32),
            jax.ShapeDtypeStruct(x.shape, bf16),
            jax.ShapeDtypeStruct((2 * own.shape[0], own.shape[1]), bf16),
        ),
        4 * x.shape[0] * own.shape[0] * own.shape[1],
        6 * 1024 * 1024,
        in_specs=in_vmem(5),
    )(place, x, o, own, other, params)


def change_kernel(ca_ref, cb_ref, down_ref, out_ref):
    count = ca_ref.shape[0]
    out_ref[:count, :] = nt(ca_ref[...], down_ref[...]).astype(bf16)
    out_ref[count:, :] = nt(cb_ref[...], down_ref[...]).astype(bf16)


def change(ca, cb, down):
    count, features = ca.shape
    hidden = down.shape[0]
    block = 2 * LANES
    steps = pl.cdiv(hidden, block)
    whole = pl.BlockSpec((count, features), lambda i: (0, 0))
    return call(
        change_kernel,
        jax.ShapeDtypeStruct((2 * count, hidden), bf16),
        4 * count * features * hidden,
        12 * 1024 * 1024,
        grid=(steps,),
        in_specs=[whole, whole, pl.BlockSpec((block, features), lambda i: (i, 0))],
        out_specs=pl.BlockSpec((2 * count, block), lambda i: (0, i)),
    )(ca, cb, down)


def feed_kernel(*refs, start, first, final, sides):
    n_grads = 1 if sides is None else 6
    place_ref, na_ref, nb_ref, ca_ref, cb_ref, gate_ref, gate_o_ref, up_ref, up_o_ref, down_ref, change_ref = refs[:11]
    refs = refs[11:]
    if not first:
        sums = refs[:4]
        refs = refs[4:]
    grad_refs = refs[:n_grads]
    outs = refs[n_grads : n_grads + 4]
    refs = refs[n_grads + 4 :]
    (na, nb, ca, cb, wg, wu, wd, change_s, inner_s, gate_s, up_s, *part_s) = refs[:14]
    refs = refs[14:]
    if not first:
        held = refs[:4]
        refs = refs[4:]
    totals = refs[:4]
    in_sem, sum_sem, out_sem = refs[4:]
    count, features = na.shape
    width = wg.shape[1]
    rows_held = gate_ref.shape[0]
    hidden = down_ref.shape[0]
    me = place_ref[0]
    lanes = pl.ds(pl.multiple_of(me * hidden + start, LANES), width)
    own_rows = pl.ds(pl.multiple_of(me * rows_held, rows_held), rows_held)
    other_rows = pl.ds(pl.multiple_of((1 - me) * rows_held, rows_held), rows_held)

    moves = [
        (na_ref, na),
        (gate_ref.at[:, lanes], wg.at[own_rows, :]),
        (gate_o_ref.at[:, lanes], wg.at[other_rows, :]),
        (up_ref.at[:, lanes], wu.at[own_rows, :]),
        (up_o_ref.at[:, lanes], wu.at[other_rows, :]),
        (change_ref.at[:, pl.ds(start, width)], change_s),
        (down_ref.at[pl.ds(start, width), :], wd),
        (nb_ref, nb),
        (ca_ref, ca),
        (cb_ref, cb),
    ]
    copies = [pltpu.make_async_copy(a, b, in_sem.at[i]) for i, (a, b) in enumerate(moves)]
    for copy in copies:
        copy.start()
    sum_copies = []
    if not first:
        sum_copies = [pltpu.make_async_copy(sums[i], held[i], sum_sem.at[i]) for i in range(4)]
        for copy in sum_copies:
            copy.start()
    for copy in copies[:7]:
        copy.wait()
    step = 256
    for half, normed_ref in enumerate((na, nb)):
        if half == 1:
            for copy in copies[7:]:
                copy.wait()
        for copy in sum_copies[2 * half : 2 * half + 2]:
            copy.wait()

        def body(i, carry, half=half, normed_ref=normed_ref):
            rows = pl.ds(pl.multiple_of(i * step, step), step)
            both = pl.ds(pl.multiple_of(half * count + i * step, step), step)
            normed = normed_ref[rows, :]
            gate = nn(normed, wg[...])
            up = nn(normed, wu[...])
            change = change_s[both, :].astype(f32)
            sigmoid = 1.0 / (1.0 + jnp.exp(-gate))
            activated = gate * sigmoid
            inner = (activated * up).astype(bf16)
            gate_g = (change * up * sigmoid * (1.0 + gate * (1.0 - sigmoid))).astype(bf16)
            up_g = (change * activated).astype(bf16)
            inner_s[both, :] = inner
            gate_s[both, :] = gate_g
            up_s[both, :] = up_g
            result = nn(inner, wd[...])
            back = nt(gate_g, wg[...]) + nt(up_g, wu[...])
            if not first:
                result = result + held[2 * half][rows, :].astype(f32)
                back = back + held[2 * half + 1][rows, :].astype(f32)
            totals[2 * half][rows, :] = result.astype(totals[2 * half].dtype)
            totals[2 * half + 1][rows, :] = back.astype(totals[2 * half + 1].dtype)
            return carry

        lax.fori_loop(0, count // step, body, 0)
    leaving = []

    def leave(source, target):
        copy = pltpu.make_async_copy(source, target, out_sem.at[len(leaving)])
        copy.start()
        leaving.append(copy)

    for i in range(4):
        leave(totals[i], outs[i])

    def part_leaves(i):
        rows = part_s[i].shape[0]
        if sides is None:
            leave(part_s[i], grad_refs[0].at[pl.ds(i * rows, rows), :])
            return
        keep, send = grad_refs[2 * i : 2 * i + 2]
        rows = rows // 2
        side = place_ref[sides[i]]
        leave(part_s[i].at[pl.ds(pl.multiple_of((1 - side) * rows, 16), rows), :], send)
        leave(part_s[i].at[pl.ds(pl.multiple_of(side * rows, 16), rows), :], keep)

    mine_s, theirs_s, down_s = part_s
    for kind, source in enumerate((gate_s, up_s)):
        for place in range(0, width, HALF):
            size = min(HALF, width - place)
            columns = slice(place, place + size)
            grads = tn(na[...], source[:count, columns]) + tn(nb[...], source[count:, columns])
            grads = grads.astype(bf16)
            for j in range(size // LANES):
                row = ((kind * width + place) // LANES + j) * rows_held
                tile = grads[:, j * LANES : (j + 1) * LANES]

                @pl.when(me == 0)
                def _():
                    mine_s[row : row + rows_held, :] = tile[:rows_held]
                    theirs_s[row : row + rows_held, :] = tile[rows_held:]

                @pl.when(me == 1)
                def _():
                    mine_s[row : row + rows_held, :] = tile[rows_held:]
                    theirs_s[row : row + rows_held, :] = tile[:rows_held]

    part_leaves(0)
    part_leaves(1)
    for place in range(0, width, HALF):
        size = min(HALF, width - place)
        columns = slice(place, place + size)
        grads = tn(inner_s[:count, columns], ca[...]) + tn(inner_s[count:, columns], cb[...])
        grads = grads.astype(bf16)
        for j in range(features // LANES):
            row = j * width + place
            down_s[row : row + size, :] = grads[:, j * LANES : (j + 1) * LANES]
    part_leaves(2)
    for copy in leaving:
        copy.wait()


def feed(place, na, nb, ca, cb, gate, gate_o, up, up_o, down, change, sums, *, start, width, final, sides):
    count, features = na.shape
    first = sums is None
    sums = () if first else tuple(sums)
    anywhere = pl.BlockSpec(memory_space=pl.ANY)
    rows = features * width // LANES
    tokens = (count, features)
    types = [f32 if final and i < 2 else bf16 for i in range(4)]
    totals = [jax.ShapeDtypeStruct(tokens, t) for t in types]
    if sides is None:
        outs = [jax.ShapeDtypeStruct((3 * rows, LANES), bf16)]
    else:
        outs = [jax.ShapeDtypeStruct((rows // 2, LANES), bf16)] * 6
    scratch = [pltpu.VMEM(tokens, bf16)] * 4
    scratch += [pltpu.VMEM((features, width), bf16)] * 2 + [pltpu.VMEM((width, features), bf16)]
    scratch += [pltpu.VMEM((2 * count, width), bf16)] * 4
    scratch += [pltpu.VMEM((rows, LANES), bf16)] * 3
    if not first:
        scratch += [pltpu.VMEM(tokens, bf16)] * 4
    scratch += [pltpu.VMEM(tokens, t) for t in types]
    scratch += [pltpu.SemaphoreType.DMA((n,)) for n in (10, 4, 10)]
    return call(
        functools.partial(feed_kernel, start=start, first=first, final=final, sides=sides),
        (*outs, *totals),
        18 * 2 * count * features * width,
        30 * 1024 * 1024,
        in_specs=[pl.BlockSpec(memory_space=pltpu.SMEM)] + [anywhere] * (10 + len(sums)),
        out_specs=(anywhere,) * (len(outs) + 4),
        scratch_shapes=scratch,
    )(place, na, nb, ca, cb, gate, gate_o, up, up_o, down, change, *sums)


def middle_kernel(
    place_ref, part_ref, got_ref, h1_ref, dy_ref, params_ref, w_ref, o_ref,
    dh1_ref, do_ref, gg_ref, mine_ref, theirs_ref, low_s,
):
    count, features = part_ref.shape
    step = 256
    gg_ref[...] = jnp.zeros_like(gg_ref)

    def body(i, carry):
        rows = pl.ds(pl.multiple_of(i * step, step), step)
        back = part_ref[rows, :] + got_ref[rows, :].astype(f32)
        hidden = h1_ref[rows, :]
        scale = lax.rsqrt(jnp.mean(hidden * hidden, -1, keepdims=True) + eps_norm)
        normal = hidden * scale
        gg_ref[...] += jnp.sum(back * normal, 0, keepdims=True)
        change = back * params_ref[:, GAIN_TWO]
        grad = dy_ref[rows, :].astype(f32) + scale * (
            change - normal * jnp.mean(change * normal, -1, keepdims=True)
        )
        dh1_ref[rows, :] = grad
        low = grad.astype(bf16)
        low_s[rows, :] = low
        do_ref[rows, :] = nt(low, w_ref[...]).astype(bf16)
        return carry

    lax.fori_loop(0, count // step, body, 0)
    store_split(place_ref, tn(o_ref[...], low_s[...]).astype(bf16), mine_ref, theirs_ref, 0)


def store_split(place_ref, grads, mine_ref, theirs_ref, first_tile):
    half_rows = grads.shape[0] // 2
    me = place_ref[0]
    for j in range(grads.shape[1] // LANES):
        row = (first_tile + j) * half_rows
        tile = grads[:, j * LANES : (j + 1) * LANES]

        @pl.when(me == 0)
        def _():
            mine_ref[row : row + half_rows, :] = tile[:half_rows]
            theirs_ref[row : row + half_rows, :] = tile[half_rows:]

        @pl.when(me == 1)
        def _():
            mine_ref[row : row + half_rows, :] = tile[half_rows:]
            theirs_ref[row : row + half_rows, :] = tile[:half_rows]


def middle(place, part, got, h1, dy, params, w, o):
    count, features = part.shape
    rows = (features // 2) * (features // LANES)
    return call(
        middle_kernel,
        (
            jax.ShapeDtypeStruct((count, features), f32),
            jax.ShapeDtypeStruct((count, HQ * HD), bf16),
            jax.ShapeDtypeStruct((1, features), f32),
            jax.ShapeDtypeStruct((rows, LANES), bf16),
            jax.ShapeDtypeStruct((rows, LANES), bf16),
        ),
        4 * count * features * features,
        12 * 1024 * 1024,
        in_specs=in_vmem(7),
        scratch_shapes=[pltpu.VMEM((count, features), bf16)],
    )(place, part, got, h1, dy, params, w, o)


def query_kernel(
    place_ref, dqa_ref, dqb_ref, n1_ref, w_ref, back_ref, gb_ref, mine_ref, theirs_ref, dp_s
):
    count = n1_ref.shape[0]
    width = HQ * HD
    split_at = dqa_ref.shape[1]
    step = 256
    gb_ref[...] = jnp.zeros_like(gb_ref)

    def body(i, carry):
        rows = pl.ds(pl.multiple_of(i * step, step), step)
        dp_s[rows, :split_at] = dqa_ref[rows, :]
        dp_s[rows, split_at:] = dqb_ref[rows, :]
        grads = dp_s[rows, :]
        gb_ref[...] += jnp.sum(grads.astype(f32), 0, keepdims=True)
        back_ref[rows, :] = nt(grads, w_ref[:, :width])
        return carry

    lax.fori_loop(0, count // step, body, 0)
    store_split(place_ref, tn(n1_ref[...], dp_s[...]).astype(bf16), mine_ref, theirs_ref, 0)


def query_back(place, dqa, dqb, n1, w):
    count, features = n1.shape
    width = HQ * HD
    rows = (features // 2) * (width // LANES)
    return call(
        query_kernel,
        (
            jax.ShapeDtypeStruct((count, features), f32),
            jax.ShapeDtypeStruct((1, width), f32),
            jax.ShapeDtypeStruct((rows, LANES), bf16),
            jax.ShapeDtypeStruct((rows, LANES), bf16),
        ),
        4 * count * features * width,
        10 * 1024 * 1024,
        in_specs=in_vmem(4),
        scratch_shapes=[pltpu.VMEM((count, width), bf16)],
    )(place, dqa, dqb, n1, w)


VECTOR_ROWS = 128


def last_kernel(
    place_ref, own_ref, one_ref, two_ref, n1_ref, x_ref, params_ref, w_ref, part_ref, dh1_ref, cos_ref, sin_ref,
    qm_ref, qt_ref, om_ref, ot_ref, gbq_ref, ggt_ref, dx_ref, mine_ref, theirs_ref, dp_s, gg_ref, gb_ref,
):
    count = n1_ref.shape[0]
    width = HQ * HD
    step = 256
    gg_ref[...] = jnp.zeros_like(gg_ref)
    gb_ref[...] = jnp.zeros_like(gb_ref)

    def body(i, carry):
        rows = pl.ds(pl.multiple_of(i * step, step), step)
        pairs = own_ref[rows, :] + one_ref[rows, :].astype(f32) + two_ref[rows, :].astype(f32)
        key = pairs[:, :LANES]
        key = key * cos_ref[rows, :] - flip_lanes_half(key * sin_ref[rows, :])
        dp_s[rows, :LANES] = key.astype(bf16)
        dp_s[rows, LANES:] = pairs[:, LANES:].astype(bf16)
        grads = dp_s[rows, :]
        gb_ref[...] += jnp.sum(grads.astype(f32), 0, keepdims=True)
        back = part_ref[rows, :] + nt(grads, w_ref[:, width:])
        x = x_ref[rows, :].astype(f32)
        scale = lax.rsqrt(jnp.mean(x * x, -1, keepdims=True) + eps_norm)
        normal = x * scale
        gg_ref[...] += jnp.sum(back * normal, 0, keepdims=True)
        change = back * params_ref[:, GAIN_ONE]
        grad = dh1_ref[rows, :] + scale * (
            change - normal * jnp.mean(change * normal, -1, keepdims=True)
        )
        dx_ref[rows, :] = grad.astype(bf16)
        return carry

    lax.fori_loop(0, count // step, body, 0)
    at = qm_ref.shape[0]
    tiles = (w_ref.shape[1] - width) // LANES
    rows_held = at * LANES // width
    store_split(
        place_ref, tn(n1_ref[...], dp_s[...]).astype(bf16), mine_ref, theirs_ref, at // rows_held
    )
    mine_ref[:at, :] = qm_ref[...]
    theirs_ref[:at, :] = qt_ref[...]
    at += tiles * rows_held
    after = at + om_ref.shape[0]
    mine_ref[at:after, :] = om_ref[...]
    theirs_ref[at:after, :] = ot_ref[...]
    vectors = []
    for ref in (gg_ref, gbq_ref, gb_ref, ggt_ref):
        vectors += [ref[:, j * LANES : (j + 1) * LANES] for j in range(ref.shape[1] // LANES)]
    vectors.append(jnp.zeros((VECTOR_ROWS - len(vectors), LANES), f32))
    vectors = jnp.concatenate(vectors, 0).astype(bf16)
    mine_ref[after:, :] = vectors
    theirs_ref[after:, :] = vectors


def last(place, own, one, two, n1, x, params, w, part, dh1, cosine, sine, qm, qt, om, ot, gbq, ggt):
    count, features = n1.shape
    columns = w.shape[1] - HQ * HD
    rows = (features // 2) * (columns // LANES) + qm.shape[0] + om.shape[0] + VECTOR_ROWS
    return call(
        last_kernel,
        (
            jax.ShapeDtypeStruct((count, features), bf16),
            jax.ShapeDtypeStruct((rows, LANES), bf16),
            jax.ShapeDtypeStruct((rows, LANES), bf16),
        ),
        4 * count * features * columns,
        14 * 1024 * 1024,
        in_specs=in_vmem(17),
        scratch_shapes=[
            pltpu.VMEM((count, columns), bf16),
            pltpu.VMEM((1, features), f32),
            pltpu.VMEM((1, columns), f32),
        ],
    )(place, own, one, two, n1, x, params, w, part, dh1, cosine, sine, qm, qt, om, ot, gbq, ggt)


def swap(values):
    return lax.ppermute(values, "fsdp", [(0, 1), (1, 0)])


def flip(values, dim):
    axis, bit = dim
    size = lax.axis_size(axis)
    return lax.ppermute(values, axis, [(i, i ^ (1 << bit)) for i in range(size)])


def side(dim):
    axis, bit = dim
    return (lax.axis_index(axis) >> bit) & 1


def add(*terms):
    total = terms[0].astype(f32)
    for term in terms[1:]:
        total = total + term.astype(f32)
    return total.astype(bf16)


def take(array, index):
    return lax.dynamic_index_in_dim(array, index, 0, False)


def join(low, other, index):
    out = jnp.zeros((2,) + low.shape, low.dtype)
    out = lax.dynamic_update_index_in_dim(out, low, index, 0)
    return lax.dynamic_update_index_in_dim(out, other, 1 - index, 0)


def rest_of_seq(values):
    for bit in range(2, lax.axis_size("seq").bit_length() - 1):
        values = add(values, flip(values, ("seq", bit)))
    return values


class Order:
    def __init__(self):
        self.token = None

    def __call__(self, step, *operands):
        if self.token is not None:
            operands, _ = lax.optimization_barrier((operands, self.token))
        out = step(*operands)
        self.token = jax.tree.leaves(out)[0]
        return out


def fold_kernel(place_ref, *refs, sides):
    n = 2 * len(sides)
    for i, number in enumerate(sides):
        kept, got = refs[2 * i : 2 * i + 2]
        keep, send = refs[n + 2 * i : n + 2 * i + 2]
        rows = keep.shape[0]
        side = place_ref[number]
        for target, at in ((keep, side), (send, 1 - side)):
            at = pl.ds(pl.multiple_of(at * rows, 16), rows)
            target[...] = (kept[at, :].astype(f32) + got[at, :].astype(f32)).astype(bf16)


def flatten(pairs):
    return [array for pair in pairs for array in pair]


def fold(place, pairs, sides):
    rows = [kept.shape[0] // 2 for kept, _ in pairs]
    outs = call(
        functools.partial(fold_kernel, sides=sides),
        tuple(jax.ShapeDtypeStruct((n, LANES), bf16) for n in rows for _ in range(2)),
        4 * sum(rows) * LANES,
        12 * sum(rows) * LANES,
        in_specs=in_vmem(2 * len(pairs)),
    )(place, *flatten(pairs))
    return list(zip(outs[::2], outs[1::2]))


def stack_kernel(*refs):
    total = refs[-1]
    at = 0
    for kept, got in zip(refs[:-1:2], refs[1:-1:2]):
        rows = kept.shape[0]
        total[at : at + rows, :] = (kept[...].astype(f32) + got[...].astype(f32)).astype(bf16)
        at += rows


def stack(pairs):
    rows = sum(kept.shape[0] for kept, _ in pairs)
    return call(
        stack_kernel, jax.ShapeDtypeStruct((rows, LANES), bf16), rows * LANES, 6 * rows * LANES
    )(*flatten(pairs))


def sum_kernel(*refs):
    n = 2 * len(refs) // 3
    for kept, got, total in zip(refs[:n:2], refs[1:n:2], refs[n:]):
        total[...] = (kept[...].astype(f32) + got[...].astype(f32)).astype(bf16)


def sum_parts(pairs):
    rows = [kept.shape[0] for kept, _ in pairs]
    return call(
        sum_kernel,
        tuple(jax.ShapeDtypeStruct((n, LANES), bf16) for n in rows),
        sum(rows) * LANES,
        6 * sum(rows) * LANES,
    )(*flatten(pairs))


def unstack_kernel(total, got, *parts):
    at = 0
    for part in parts:
        rows = part.shape[0]
        both = total[at : at + rows, :].astype(f32) + got[at : at + rows, :].astype(f32)
        part[...] = both.astype(bf16)
        at += rows


def unstack(total, got, sizes):
    return call(
        unstack_kernel,
        tuple(jax.ShapeDtypeStruct((n, LANES), bf16) for n in sizes),
        total.shape[0] * LANES,
        6 * total.shape[0] * LANES,
    )(total, got)


def join_kernel(place_ref, *refs, sides):
    for i, number in enumerate(sides):
        own, got = refs[2 * i : 2 * i + 2]
        both = refs[2 * len(sides) + i]
        rows = own.shape[0]
        side = place_ref[number]
        both[pl.ds(pl.multiple_of(side * rows, 16), rows), :] = own[...]
        both[pl.ds(pl.multiple_of((1 - side) * rows, 16), rows), :] = got[...]


def join_parts(place, pairs, sides):
    rows = [own.shape[0] for own, _ in pairs]
    return call(
        functools.partial(join_kernel, sides=sides),
        tuple(jax.ShapeDtypeStruct((2 * n, LANES), bf16) for n in rows),
        1,
        8 * sum(rows) * LANES,
        in_specs=in_vmem(2 * len(pairs)),
    )(place, *flatten(pairs))


def bring_halves(place_ref, refs, sides, targets, in_sem):
    copies = []
    for i, number in enumerate(sides):
        side = place_ref[number]
        rows = targets[i].shape[0] // 2
        for ref, at in ((refs[2 * i], side), (refs[2 * i + 1], 1 - side)):
            at = pl.ds(pl.multiple_of(at * rows, 16), rows)
            copy = pltpu.make_async_copy(ref, targets[i].at[at, :], in_sem.at[len(copies)])
            copy.start()
            copies.append(copy)
    for copy in copies:
        copy.wait()


def untile_kernel(*refs, start, width, first, sides, n_parts):
    place_ref = refs[0]
    parts = refs[1 : 1 + n_parts]
    refs = refs[1 + n_parts + (0 if first else 3) :]
    gate_ref, up_ref, down_ref, mine_s, theirs_s, downs_s, wide_s, down_s, in_sem, out_sem = refs
    me = place_ref[0]
    features = down_ref.shape[1]
    hidden = down_ref.shape[0]
    rows_held = gate_ref.shape[0]
    targets = (mine_s, theirs_s, downs_s)
    bring_halves(place_ref, parts, sides, targets, in_sem)
    leaving = []

    def leave(source, target):
        copy = pltpu.make_async_copy(source, target, out_sem.at[len(leaving)])
        copy.start()
        leaving.append(copy)

    tiles = width // LANES
    for i, (source, owner) in enumerate(((mine_s, me), (theirs_s, 1 - me))):
        lanes = pl.ds(pl.multiple_of(owner * hidden + start, LANES), width)
        for kind, target in enumerate((gate_ref, up_ref)):
            wide = wide_s.at[2 * i + kind]
            for j in range(tiles):
                row = (kind * tiles + j) * rows_held
                wide[:, j * LANES : (j + 1) * LANES] = source[row : row + rows_held, :].astype(f32)
            leave(wide, target.at[:, lanes])
    for j in range(features // LANES):
        row = j * width
        down_s[:, j * LANES : (j + 1) * LANES] = downs_s[row : row + width, :].astype(f32)
    leave(down_s, down_ref.at[pl.ds(start, width), :])
    for copy in leaving:
        copy.wait()


def untile(place, parts, outs, *, start, width, features, hidden, sides):
    first = outs is None
    rows_held = features // 2
    rows = features * width // LANES
    anywhere = pl.BlockSpec(memory_space=pl.ANY)
    outs = () if first else tuple(outs)
    n_parts = len(parts)
    return call(
        functools.partial(
            untile_kernel, start=start, width=width, first=first, sides=sides, n_parts=n_parts
        ),
        (
            jax.ShapeDtypeStruct((rows_held, 2 * hidden), f32),
            jax.ShapeDtypeStruct((rows_held, 2 * hidden), f32),
            jax.ShapeDtypeStruct((hidden, features), f32),
        ),
        3 * features * width,
        3 * features * width * 6,
        in_specs=[pl.BlockSpec(memory_space=pltpu.SMEM)] + [anywhere] * (n_parts + len(outs)),
        out_specs=(anywhere,) * 3,
        scratch_shapes=[pltpu.VMEM((rows, LANES), bf16)] * 3
        + [
            pltpu.VMEM((4, rows_held, width), f32),
            pltpu.VMEM((width, features), f32),
            pltpu.SemaphoreType.DMA((6,)),
            pltpu.SemaphoreType.DMA((5,)),
        ],
        input_output_aliases={} if first else {1 + n_parts + i: i for i in range(3)},
    )(place, *parts, *outs)


def split_kernel(place_ref, mine_ref, theirs_ref, *refs, sides):
    base = 0
    for i, number in enumerate(sides):
        side = place_ref[number]
        rows = refs[2 * i].shape[0]
        for target, at in zip(refs[2 * i : 2 * i + 2], (side, 1 - side)):
            at = pl.ds(pl.multiple_of(base + at * rows, 16), rows)
            target[...] = (mine_ref[at, :].astype(f32) + theirs_ref[at, :].astype(f32)).astype(bf16)
        base += 2 * rows


def split(place, mine, theirs, *, sides):
    rows = mine.shape[0] // (2 * len(sides))
    outs = call(
        functools.partial(split_kernel, sides=sides),
        (jax.ShapeDtypeStruct((rows, LANES), bf16),) * (2 * len(sides)),
        mine.shape[0] * LANES,
        6 * mine.shape[0] * LANES,
        in_specs=in_vmem(2),
    )(place, mine, theirs)
    return list(zip(outs[::2], outs[1::2]))


def untile_flat_kernel(*refs, sides):
    place_ref = refs[0]
    parts = refs[1 : 1 + 2 * len(sides)]
    *targets, vector_ref, flat_s, in_sem = refs[1 + 2 * len(sides) :]
    rows = flat_s.shape[0] // len(sides)
    halves = [flat_s.at[pl.ds(i * rows, rows), :] for i in range(len(sides))]
    bring_halves(place_ref, parts, sides, halves, in_sem)
    rows_held = targets[0].shape[0]
    row = 0
    for target in targets:
        for j in range(target.shape[1] // LANES):
            target[:, j * LANES : (j + 1) * LANES] = flat_s[row : row + rows_held, :].astype(f32)
            row += rows_held
    vector_ref[...] = flat_s[row:, :].astype(f32)


def untile_flat(place, parts, *, rows_held, widths, sides):
    rows = rows_held * sum(widths) // LANES + VECTOR_ROWS
    anywhere = pl.BlockSpec(memory_space=pl.ANY)
    return call(
        functools.partial(untile_flat_kernel, sides=sides),
        (
            *(jax.ShapeDtypeStruct((rows_held, width), f32) for width in widths),
            jax.ShapeDtypeStruct((VECTOR_ROWS, LANES), f32),
        ),
        rows * LANES,
        rows * LANES * 6,
        in_specs=[pl.BlockSpec(memory_space=pltpu.SMEM)] + [anywhere] * len(parts),
        out_specs=(pl.BlockSpec(memory_space=pltpu.VMEM),) * (len(widths) + 1),
        scratch_shapes=[
            pltpu.VMEM((rows, LANES), bf16), pltpu.SemaphoreType.DMA((2 * len(sides),))
        ],
    )(place, *parts)


class FlatSum:
    def __init__(self, place, order):
        self.place, self.order = place, order
        self.links, self.sides = ((X, Y), (Y, X)), ((1, 2), (2, 1))

    def over(self, arrays, level):
        return [flip(array, link) for array, link in zip(arrays, self.links[level])]

    def leave(self, mine, theirs):
        pairs = self.order(functools.partial(split, sides=self.sides[0]), self.place, mine, theirs)
        kept, sent = zip(*pairs)
        self.held = list(zip(kept, self.over(sent, 0)))

    def halve(self):
        pairs = self.order(lambda pairs: fold(self.place, pairs, self.sides[1]), self.held)
        kept, sent = zip(*pairs)
        self.held = list(zip(kept, self.over(sent, 1)))

    def sum(self):
        total = rest_of_seq(self.order(stack, self.held))
        self.total = total, flip(total, Z)

    def across(self):
        total = self.order(add, *self.total)
        for bit in range(2, lax.axis_size("ctx").bit_length() - 1):
            total = add(total, flip(total, ("ctx", bit)))
        self.total = total, flip(total, FAR)

    def turn(self):
        total, got = self.total
        sizes = (total.shape[0] // 2,) * 2
        own = self.order(lambda total, got: unstack(total, got, sizes), total, got)
        self.held = list(zip(own, self.over(own, 1)))

    def join(self):
        own = self.order(lambda pairs: join_parts(self.place, pairs, self.sides[1]), self.held)
        self.held = list(zip(own, self.over(own, 0)))


class LinkSum:
    def __init__(self, place, order):
        self.place, self.order = place, order
        links, numbers = (X, Y, Z), (1, 2, 4)
        self.links = [[links[(i + j) % 3] for i in range(3)] for j in range(3)]
        self.sides = [tuple(numbers[(i + j) % 3] for i in range(3)) for j in range(3)]

    def over(self, arrays, level):
        return [flip(array, link) for array, link in zip(arrays, self.links[level])]

    def leave(self, pairs):
        kept, sent = zip(*pairs)
        self.held = list(zip(kept, self.over(sent, 0)))

    def halve(self, level):
        pairs = self.order(lambda pairs: fold(self.place, pairs, self.sides[level]), self.held)
        kept, sent = zip(*pairs)
        self.held = list(zip(kept, self.over(sent, level)))

    def rest_of_axes(self, total):
        total = rest_of_seq(total)
        for bit in range(2, lax.axis_size("ctx").bit_length() - 1):
            total = add(total, flip(total, ("ctx", bit)))
        return total

    def across(self):
        self.sizes = [kept.shape[0] for kept, _ in self.held]
        total = self.rest_of_axes(self.order(stack, self.held))
        self.total = total, flip(total, FAR)

    def turn(self):
        own = list(self.order(lambda total, got: unstack(total, got, self.sizes), *self.total))
        own[1] = swap(own[1])
        self.held = list(zip(own, self.over(own, 2)))

    def across_each(self):
        totals = [self.rest_of_axes(total) for total in self.order(sum_parts, self.held)]
        self.held = [(total, flip(total, FAR)) for total in totals]

    def turn_each(self, i):
        own = self.order(add, *self.held[i])
        if i == 1:
            own = swap(own)
        self.held[i] = own, flip(own, self.links[2][i])

    def join(self, level):
        own = self.order(lambda pairs: join_parts(self.place, pairs, self.sides[level]), self.held)
        self.held = list(zip(own, self.over(own, level - 1)))

    @property
    def parts(self):
        return flatten(self.held)


X, Y, Z, FAR = ("seq", 0), ("seq", 1), ("ctx", 0), ("ctx", 1)


def on_device(
    block_input,
    segment_ids,
    out_cotangent,
    input_gain,
    query_weight,
    query_bias,
    key_weight,
    key_bias,
    value_weight,
    value_bias,
    output_weight,
    middle_gain,
    gate_weight,
    up_weight,
    down_weight,
):
    me = lax.axis_index("fsdp")
    ctx = lax.axis_index("ctx")
    chunks = lax.axis_size("ctx")
    place = jnp.stack([me, side(X), side(Y), ctx, side(Z)]).astype(jnp.int32)
    x = block_input[0]
    dy = out_cotangent[0]
    count, features = x.shape
    hidden = down_weight.shape[0]
    kv_width = KVH * HD

    own = (query_weight, key_weight, value_weight)
    other = tuple(swap(w) for w in own)
    vectors = (input_gain, query_bias, key_bias, value_bias, middle_gain)
    mine = jnp.concatenate(vectors)
    theirs = swap(mine)
    low = jnp.where(me == 0, mine, theirs).astype(f32)
    high = jnp.where(me == 0, theirs, mine).astype(f32)
    params = []
    at = 0
    for vector in vectors:
        size = vector.shape[0]
        params += [low[at : at + size], high[at : at + size]]
        at += size
    params = jnp.concatenate(params)[None]

    first = ctx * count
    positions = (first + jnp.arange(count, dtype=jnp.int32)).astype(f32)
    inverse = theta_base ** (-jnp.arange(0, HD, 2, dtype=f32) / HD)
    angle = positions[:, None] * jnp.tile(inverse, LANES // inverse.shape[0])[None, :]
    cosine, sine = jnp.cos(angle), jnp.sin(angle)

    n1, q, kv, w_in = project(place, x, params, own, other, cosine, sine)
    out_other = swap(output_weight)
    gate_other, up_other = swap(gate_weight), swap(up_weight)
    dy_other = swap(dy)

    reach = WINDOW // count
    before = [
        lax.ppermute(kv, "ctx", [(i, i + d) for i in range(chunks - d)])
        for d in range(1, reach + 1)
    ]
    order = Order()
    changes = order(change, dy, dy_other, down_weight)
    o, lse = order(attend, place, q, kv, *before, segment_ids)
    h1, n2, w_out = merge(place, x, o, output_weight, out_other, params)
    n2_other = swap(n2)

    widths = WIDTHS
    starts = tuple(sum(widths[:i]) for i in range(len(widths)))
    one, two = (LinkSum(place, order) for _ in range(2))
    first_sides = one.sides[0]

    def run_feed(i, token_sums):
        step = functools.partial(
            feed, start=starts[i], width=widths[i], final=i == len(widths) - 1, sides=first_sides
        )
        *grads, own_result, own_back, other_result, other_back = order(
            step, place, n2, n2_other, dy, dy_other, gate_weight, gate_other, up_weight, up_other,
            down_weight, changes, token_sums,
        )
        pairs = [(grads[2 * i], grads[2 * i + 1]) for i in range(3)]
        return pairs, (own_result, own_back, other_result, other_back)

    def run_untile(i, parts, outs):
        step = functools.partial(
            untile, start=starts[i], width=widths[i], features=features, hidden=hidden,
            sides=first_sides,
        )
        return order(step, place, parts, outs)

    pairs, token_sums = run_feed(0, None)
    one.leave(pairs)
    pairs, token_sums = run_feed(1, token_sums)
    own_result, own_back, other_result, other_back = token_sums
    got_back = swap(other_back)
    one.halve(1)

    dh1, do, gg_two, out_mine, out_theirs = order(
        middle, place, own_back, got_back, h1, dy, params, w_out, o
    )
    one.halve(2)
    one.across()
    pairs = order(lambda pairs: pairs, pairs)
    two.leave(pairs)
    back_operands = (place, q, do, kv, *before, segment_ids, lse, cosine, sine)
    dq_low, *pair_sums = order(
        functools.partial(attend_back, first_pair=0, pairs=4), *back_operands, None
    )
    two.halve(1)
    dq_high, own_pairs, *sent_pairs = order(
        functools.partial(attend_back, first_pair=4, pairs=3), *back_operands, pair_sums
    )
    got_pairs = [
        lax.ppermute(pairs, "ctx", [(i + d, i) for i in range(chunks - d)])
        for d, pairs in enumerate(sent_pairs, 1)
    ]
    one.turn()
    two.halve(2)
    back_part, gb_query, query_mine, query_theirs = order(
        query_back, place, dq_low, dq_high, n1, w_in
    )
    two.across_each()
    dx, mine, theirs = order(
        last, place, own_pairs, *got_pairs, n1, x, params, w_in, back_part, dh1, cosine, sine,
        query_mine, query_theirs, out_mine, out_theirs, gb_query, gg_two,
    )
    input_grad = dx[None]
    width = HQ * HD
    rest = FlatSum(place, order)
    got = swap(theirs)
    one.join(2)
    two.turn_each(0)
    rest.leave(mine, got)
    one.join(1)
    two.turn_each(1)
    rest.halve()
    two.turn_each(2)
    rest.sum()
    outs = run_untile(0, one.parts, None)
    two.join(2)
    rest.across()
    rest.turn()
    two.join(1)
    rest.join()
    block_output = order(
        lambda a, b, c: (a + b + c.astype(f32)).astype(bf16), h1, own_result, swap(other_result)
    )[None]
    gates, ups, gw_down = run_untile(1, two.parts, outs)
    gw_query, gw_key, gw_value, gw_out, vector = order(
        functools.partial(
            untile_flat, rows_held=features // 2, widths=(width, kv_width, kv_width, features),
            sides=rest.sides[0],
        ),
        place,
        flatten(rest.held),
    )
    vector = vector.reshape(-1)
    shares = []
    at = 0
    for size in (features, width, kv_width, kv_width, features):
        shares.append(lax.dynamic_slice_in_dim(vector, at + me * (size // 2), size // 2, 0))
        at += size
    gg_one, gb_query, gb_key, gb_value, gg_two = shares
    return (
        block_output,
        input_grad,
        gg_one,
        gw_query,
        gb_query,
        gw_key,
        gb_key,
        gw_value,
        gb_value,
        gw_out,
        gg_two,
        gates,
        ups,
        gw_down,
    )


def solution(mesh):
    return jax.shard_map(
        on_device,
        mesh=mesh,
        in_specs=(
            P(("seq", "fsdp"), "ctx", None),
            P(("seq", "fsdp"), None),
            P(("seq", "fsdp"), "ctx", None),
            P("fsdp"),
            P("fsdp", None),
            P("fsdp"),
            P("fsdp", None),
            P("fsdp"),
            P("fsdp", None),
            P("fsdp"),
            P("fsdp", None),
            P("fsdp"),
            P("fsdp", None),
            P("fsdp", None),
            P("fsdp", None),
        ),
        out_specs=(
            P(("seq", "fsdp"), "ctx", None),
            P(("seq", "fsdp"), "ctx", None),
            P("fsdp"),
            P("fsdp", None),
            P("fsdp"),
            P("fsdp", None),
            P("fsdp"),
            P("fsdp", None),
            P("fsdp"),
            P("fsdp", None),
            P("fsdp"),
            P("fsdp", None),
            P("fsdp", None),
            P("fsdp", None),
        ),
        check_vma=False,
    )
```

```python
import functools

import jax
import jax.numpy as jnp
from jax import lax
from jax.experimental import pallas as pl
from jax.experimental.pallas import tpu as pltpu
from jax.sharding import PartitionSpec as P

HQ = 14
KVH = 2
HD = 64
WINDOW = 1024
PAIRS = HQ // 2
LANES = 128
HALF = 256

theta_base = 1000000.0
eps_norm = 1e-06
masked_score = -1e30
f32 = jnp.float32
bf16 = jnp.bfloat16
VMEM_BYTES = 58 * 1024 * 1024
WIDTHS = (1280, 1152)


def nn(a, b):
    return lax.dot_general(a, b, (((1,), (0,)), ((), ())), preferred_element_type=f32)


def nt(a, b):
    return lax.dot_general(a, b, (((1,), (1,)), ((), ())), preferred_element_type=f32)


def tn(a, b):
    return lax.dot_general(a, b, (((0,), (0,)), ((), ())), preferred_element_type=f32)


def flip_lanes_half(values):
    width = values.shape[-1]
    lane = lax.broadcasted_iota(jnp.int32, values.shape, len(values.shape) - 1)
    up = pltpu.roll(values, width - 32, len(values.shape) - 1)
    down = pltpu.roll(values, 32, len(values.shape) - 1)
    return jnp.where((lane & 63) < 32, -up, down)


def call(kernel, out_shape, flops, moved, **kwargs):
    return pl.pallas_call(
        kernel,
        out_shape=out_shape,
        compiler_params=pltpu.CompilerParams(vmem_limit_bytes=VMEM_BYTES),
        cost_estimate=pl.CostEstimate(flops=flops, bytes_accessed=moved, transcendentals=0),
        **kwargs,
    )


GAIN_ONE = slice(0, 896)
BIAS = slice(896, 2048)
GAIN_TWO = slice(2048, 2944)


def place_rows(target, own_ref, other_ref, me, columns=slice(None)):
    rows = own_ref.shape[0]
    target[pl.ds(pl.multiple_of(me * rows, rows), rows), columns] = own_ref[...]
    target[pl.ds(pl.multiple_of((1 - me) * rows, rows), rows), columns] = other_ref[...]


def project_kernel(
    place_ref, x_ref, params_ref, wq_ref, wk_ref, wv_ref, oq_ref, ok_ref, ov_ref, cos_ref, sin_ref,
    n1_ref, q_ref, kv_ref, w_ref,
):
    count = x_ref.shape[0]
    step = 256
    me = place_ref[0]
    width = HQ * HD
    place_rows(w_ref, wq_ref, oq_ref, me, slice(0, width))
    place_rows(w_ref, wk_ref, ok_ref, me, slice(width, width + LANES))
    place_rows(w_ref, wv_ref, ov_ref, me, slice(width + LANES, width + 2 * LANES))

    def body(i, carry):
        rows = pl.ds(pl.multiple_of(i * step, step), step)
        x = x_ref[rows, :].astype(f32)
        scale = lax.rsqrt(jnp.mean(x * x, -1, keepdims=True) + eps_norm)
        normed = (x * scale * params_ref[:, GAIN_ONE]).astype(bf16)
        n1_ref[rows, :] = normed
        cosine = cos_ref[rows, :]
        sine = sin_ref[rows, :]
        out = nn(normed, w_ref[...]) + params_ref[:, BIAS]
        for j in range(PAIRS + 1):
            part = out[:, j * LANES : (j + 1) * LANES]
            part = part * cosine + flip_lanes_half(part) * sine
            if j < PAIRS:
                q_ref[rows, j * LANES : (j + 1) * LANES] = (part * HD**-0.5).astype(bf16)
            else:
                kv_ref[rows, :LANES] = part.astype(bf16)
        kv_ref[rows, LANES:] = out[:, (PAIRS + 1) * LANES :].astype(bf16)
        return carry

    lax.fori_loop(0, count // step, body, 0)


def in_vmem(n):
    return [pl.BlockSpec(memory_space=pltpu.SMEM)] + [pl.BlockSpec(memory_space=pltpu.VMEM)] * n


def project(place, x, params, own, other, cosine, sine):
    count, width = x.shape
    columns = sum(w.shape[1] for w in own)
    return call(
        project_kernel,
        (
            jax.ShapeDtypeStruct((count, width), bf16),
            jax.ShapeDtypeStruct((count, HQ * HD), bf16),
            jax.ShapeDtypeStruct((count, 2 * KVH * HD), bf16),
            jax.ShapeDtypeStruct((width, columns), bf16),
        ),
        2 * count * width * columns,
        6 * 1024 * 1024,
        in_specs=in_vmem(10),
    )(place, x, params, *own, *other, cosine, sine)


def lane_low(shape):
    return lax.broadcasted_iota(jnp.int32, shape, len(shape) - 1) < HD


def spread_heads(source, target, row):
    values = source.astype(f32)
    other = pltpu.roll(values, HD, 1)
    low = lane_low(values.shape)
    rows = pl.ds(row, values.shape[0])
    target[0, 0, rows, :] = jnp.where(low, values, 0.0).astype(bf16)
    target[1, 0, rows, :] = jnp.where(low, 0.0, other).astype(bf16)
    target[0, 1, rows, :] = jnp.where(low, other, 0.0).astype(bf16)
    target[1, 1, rows, :] = jnp.where(low, 0.0, values).astype(bf16)


def turn_heads(source, target, column):
    values = source.astype(f32).T.astype(bf16)
    columns = pl.ds(column, values.shape[1])
    target[0, :, columns] = values[:HD]
    target[1, :, columns] = values[HD:]


def fill_bias(place_ref, seg_ref, near_ref, far_ref, count):
    ctx = place_ref[3]

    def segments(back):
        start = pl.multiple_of(jnp.maximum(ctx - back, 0) * count, count)
        row = seg_ref[:, pl.ds(start, count)].astype(f32)
        row = jnp.where(ctx >= back, row, -1.0)
        return row, jnp.broadcast_to(row, (LANES, count)).T

    own_row, own = segments(0)
    _, one = segments(1)
    _, two = segments(2)
    for t in range(count // LANES):
        columns = slice(t * LANES, (t + 1) * LANES)
        query = own_row[:, columns]
        near_ref[:, columns] = jnp.where(one == query, 0.0, masked_score)
        key = lax.broadcasted_iota(jnp.int32, (count, LANES), 0)
        token = lax.broadcasted_iota(jnp.int32, (count, LANES), 1) + t * LANES
        far = jnp.where(key <= token, own, two)
        far_ref[:, columns] = jnp.where(far == query, 0.0, masked_score)


def triangle():
    key = lax.broadcasted_iota(jnp.int32, (HALF, HALF), 0)
    token = lax.broadcasted_iota(jnp.int32, (HALF, HALF), 1)
    return key <= token


def tiles_of(t, count):
    if t == 0:
        plain = 2 * count + HALF
        plain_bias = HALF
    else:
        plain = 0
        plain_bias = 0
    diagonal = t * HALF
    return plain, plain_bias, diagonal, 2 * count + diagonal


def scores_of(keys, query, t, count, near_ref, far_ref, tri):
    plain, plain_bias, own, old = tiles_of(t, count)
    columns = slice(t * HALF, (t + 1) * HALF)
    near = nt(keys(count, count), query) + near_ref[:, columns]
    far = nt(keys(plain, HALF), query) + far_ref[plain_bias : plain_bias + HALF, columns]
    edge = jnp.where(tri, nt(keys(own, HALF), query), nt(keys(old, HALF), query))
    edge = edge + far_ref[own : own + HALF, columns]
    return near, far, edge


def attend_kernel(
    place_ref, q_ref, kv0_ref, kv1_ref, kv2_ref, seg_ref, o_ref, lse_ref, k_s, vt_s, near_s, far_s
):
    count = q_ref.shape[0]
    pair = pl.program_id(0)

    @pl.when(pair == 0)
    def _():
        for i, ref in enumerate((kv0_ref, kv1_ref, kv2_ref)):
            spread_heads(ref[:, :LANES], k_s, i * count)
            turn_heads(ref[:, LANES:], vt_s, i * count)
        fill_bias(place_ref, seg_ref, near_s, far_s, count)

    tri = triangle()
    for t in range(count // HALF):
        plain, _, own, old = tiles_of(t, count)
        rows = slice(t * HALF, (t + 1) * HALF)
        query = q_ref[rows, :]
        turned = []
        for half in range(2):
            group = (2 * pair + half) // (HQ // KVH)
            near, far, edge = scores_of(
                lambda start, size: k_s[half, group, start : start + size, :],
                query,
                t,
                count,
                near_s,
                far_s,
                tri,
            )
            top = jnp.maximum(
                jnp.max(near, 0, keepdims=True),
                jnp.maximum(jnp.max(far, 0, keepdims=True), jnp.max(edge, 0, keepdims=True)),
            )
            near = jnp.exp(near - top)
            far = jnp.exp(far - top)
            edge = jnp.exp(edge - top)
            total = (
                jnp.sum(near, 0, keepdims=True)
                + jnp.sum(far, 0, keepdims=True)
                + jnp.sum(edge, 0, keepdims=True)
            )
            lse_ref[0, half : half + 1, rows] = top + jnp.log(total)
            mixed = nn(vt_s[group, :, count : 2 * count], near.astype(bf16))
            mixed += nn(vt_s[group, :, plain : plain + HALF], far.astype(bf16))
            mixed += nn(vt_s[group, :, own : own + HALF], jnp.where(tri, edge, 0.0).astype(bf16))
            mixed += nn(vt_s[group, :, old : old + HALF], jnp.where(tri, 0.0, edge).astype(bf16))
            turned.append(mixed * (1.0 / total))
        o_ref[rows, :] = jnp.concatenate(turned, 0).T.astype(bf16)


def attend(place, q, kv0, kv1, kv2, seg):
    count = q.shape[0]
    whole = lambda p: (0, 0)
    return call(
        attend_kernel,
        (
            jax.ShapeDtypeStruct((count, HQ * HD), bf16),
            jax.ShapeDtypeStruct((PAIRS, 8, count), f32),
        ),
        4 * HQ * count * 1280 * 256,
        4 * 1024 * 1024,
        grid=(PAIRS,),
        in_specs=[
            pl.BlockSpec(memory_space=pltpu.SMEM),
            pl.BlockSpec((count, LANES), lambda p: (0, p)),
            pl.BlockSpec(kv0.shape, whole),
            pl.BlockSpec(kv1.shape, whole),
            pl.BlockSpec(kv2.shape, whole),
            pl.BlockSpec(seg.shape, whole),
        ],
        out_specs=(
            pl.BlockSpec((count, LANES), lambda p: (0, p)),
            pl.BlockSpec((1, 8, count), lambda p: (p, 0, 0)),
        ),
        scratch_shapes=[
            pltpu.VMEM((2, KVH, 3 * count, LANES), bf16),
            pltpu.VMEM((KVH, HD, 3 * count), bf16),
            pltpu.VMEM((count, count), f32),
            pltpu.VMEM((count, count), f32),
        ],
    )(place, q, kv0, kv1, kv2, seg)


def attend_back_kernel(*refs, first_pair, first, final):
    (place_ref, q_ref, do_ref, kv0_ref, kv1_ref, kv2_ref, seg_ref, lse_ref, cos_ref, sin_ref) = refs[:10]
    refs = refs[10:]
    if not first:
        dk_in, dv_in = refs[:2]
        refs = refs[2:]
    dq_ref = refs[0]
    refs = refs[1:]
    if final:
        own_ref, one_ref, two_ref = refs[:3]
        refs = refs[3:]
        k_s, v_s, kt_s, near_s, far_s, dk_s, dv_s = refs
    else:
        dk_s, dv_s = refs[:2]
        k_s, v_s, kt_s, near_s, far_s = refs[2:]
    count = q_ref.shape[0]
    step = pl.program_id(0)
    pair = step + first_pair

    @pl.when(step == 0)
    def _():
        for i, ref in enumerate((kv0_ref, kv1_ref, kv2_ref)):
            spread_heads(ref[:, :LANES], k_s, i * count)
            spread_heads(ref[:, LANES:], v_s, i * count)
            turn_heads(ref[:, :LANES], kt_s, i * count)
        fill_bias(place_ref, seg_ref, near_s, far_s, count)
        if first:
            dk_s[...] = jnp.zeros_like(dk_s)
            dv_s[...] = jnp.zeros_like(dv_s)
        else:
            dk_s[...] = dk_in[...]
            dv_s[...] = dv_in[...]

    tri = triangle()
    for t in range(count // HALF):
        plain, _, own, old = tiles_of(t, count)
        rows = slice(t * HALF, (t + 1) * HALF)
        query = q_ref[rows, :]
        grad = do_ref[rows, :]
        low = lane_low(query.shape)
        turned = []
        for half in range(2):
            group = (2 * pair + half) // (HQ // KVH)
            mine = low if half == 0 else jnp.logical_not(low)
            query_half = jnp.where(mine, query.astype(f32), 0.0).astype(bf16)
            grad_half = jnp.where(mine, grad.astype(f32), 0.0).astype(bf16)
            log_total = lse_ref[0, half : half + 1, rows]
            scores = scores_of(
                lambda start, size: k_s[half, group, start : start + size, :],
                query,
                t,
                count,
                near_s,
                far_s,
                tri,
            )
            near, far, edge = (jnp.exp(part - log_total) for part in scores)
            values = lambda start, size: v_s[half, group, start : start + size, :]
            near_p = nt(values(count, count), grad)
            far_p = nt(values(plain, HALF), grad)
            edge_p = jnp.where(tri, nt(values(own, HALF), grad), nt(values(old, HALF), grad))
            inner = (
                jnp.sum(near * near_p, 0, keepdims=True)
                + jnp.sum(far * far_p, 0, keepdims=True)
                + jnp.sum(edge * edge_p, 0, keepdims=True)
            )
            near_g = near * (near_p - inner)
            far_g = far * (far_p - inner)
            edge_g = edge * (edge_p - inner)
            blocks = (
                (count, count, near, near_g),
                (plain, HALF, far, far_g),
                (own, HALF, jnp.where(tri, edge, 0.0), jnp.where(tri, edge_g, 0.0)),
                (old, HALF, jnp.where(tri, 0.0, edge), jnp.where(tri, 0.0, edge_g)),
            )
            total = None
            for start, size, weight, change in blocks:
                change = change.astype(bf16)
                keys = slice(start, start + size)
                dv_s[group, keys, :] += nn(weight.astype(bf16), grad_half)
                dk_s[group, keys, :] += nn(change, query_half)
                part = nn(kt_s[group, :, keys], change)
                total = part if total is None else total + part
            turned.append(total)
        turned = jnp.concatenate(turned, 0).T * HD**-0.5
        back = turned * cos_ref[rows, :] - flip_lanes_half(turned * sin_ref[rows, :])
        dq_ref[rows, :] = back.astype(bf16)

    if final:

        @pl.when(pair == PAIRS - 1)
        def _():
            for i, (ref, cast) in enumerate(((own_ref, f32), (one_ref, bf16), (two_ref, bf16))):
                keys = slice(i * count, (i + 1) * count)
                for j, source in enumerate((dk_s, dv_s)):
                    one = source[0, keys, :]
                    two = source[1, keys, :]
                    one = one + pltpu.roll(one, HD, 1)
                    two = two + pltpu.roll(two, HD, 1)
                    both = jnp.where(lane_low(one.shape), one, two)
                    ref[:, j * LANES : (j + 1) * LANES] = both.astype(cast)


def attend_back(place, q, do, kv0, kv1, kv2, seg, lse, cosine, sine, sums, *, first_pair, pairs):
    count = q.shape[0]
    first = sums is None
    final = first_pair + pairs == PAIRS
    sums = () if first else tuple(sums)
    whole = lambda p: (0, 0)
    stacked = pl.BlockSpec((KVH, 3 * count, LANES), lambda p: (0, 0, 0))
    lane_block = pl.BlockSpec((count, LANES), lambda p: (0, p + first_pair))
    row_block = pl.BlockSpec((1, 8, count), lambda p: (p + first_pair, 0, 0))
    token_block = pl.BlockSpec((count, 2 * LANES), whole)
    stack = jax.ShapeDtypeStruct((KVH, 3 * count, LANES), f32)
    if final:
        outs = [jax.ShapeDtypeStruct((count, 2 * LANES), t) for t in (f32, bf16, bf16)]
        out_specs = [token_block] * 3
        scratch = [pltpu.VMEM(stack.shape, f32)] * 2
    else:
        outs = [stack, stack]
        out_specs = [stacked] * 2
        scratch = []
    return call(
        functools.partial(attend_back_kernel, first_pair=first_pair, first=first, final=final),
        (jax.ShapeDtypeStruct((count, pairs * LANES), bf16), *outs),
        10 * 2 * pairs * count * 1280 * 256,
        6 * 1024 * 1024,
        grid=(pairs,),
        in_specs=[
            pl.BlockSpec(memory_space=pltpu.SMEM),
            lane_block,
            lane_block,
            pl.BlockSpec(kv0.shape, whole),
            pl.BlockSpec(kv1.shape, whole),
            pl.BlockSpec(kv2.shape, whole),
            pl.BlockSpec(seg.shape, whole),
            row_block,
            pl.BlockSpec(cosine.shape, whole),
            pl.BlockSpec(sine.shape, whole),
        ]
        + [stacked] * len(sums),
        out_specs=(pl.BlockSpec((count, LANES), lambda p: (0, p)), *out_specs),
        scratch_shapes=[
            pltpu.VMEM((2, KVH, 3 * count, LANES), bf16),
            pltpu.VMEM((2, KVH, 3 * count, LANES), bf16),
            pltpu.VMEM((KVH, HD, 3 * count), bf16),
            pltpu.VMEM((count, count), f32),
            pltpu.VMEM((count, count), f32),
        ]
        + scratch,
    )(place, q, do, kv0, kv1, kv2, seg, lse, cosine, sine, *sums)


def merge_kernel(place_ref, x_ref, o_ref, own_ref, other_ref, params_ref, h1_ref, n2_ref, w_ref):
    step = 256
    place_rows(w_ref, own_ref, other_ref, place_ref[0])

    def body(i, carry):
        rows = pl.ds(pl.multiple_of(i * step, step), step)
        hidden = x_ref[rows, :].astype(f32) + nn(o_ref[rows, :], w_ref[...])
        h1_ref[rows, :] = hidden
        scale = lax.rsqrt(jnp.mean(hidden * hidden, -1, keepdims=True) + eps_norm)
        n2_ref[rows, :] = (hidden * scale * params_ref[:, GAIN_TWO]).astype(bf16)
        return carry

    lax.fori_loop(0, x_ref.shape[0] // step, body, 0)


def merge(place, x, o, own, other, params):
    return call(
        merge_kernel,
        (
            jax.ShapeDtypeStruct(x.shape, f32),
            jax.ShapeDtypeStruct(x.shape, bf16),
            jax.ShapeDtypeStruct((2 * own.shape[0], own.shape[1]), bf16),
        ),
        4 * x.shape[0] * own.shape[0] * own.shape[1],
        6 * 1024 * 1024,
        in_specs=in_vmem(5),
    )(place, x, o, own, other, params)


def change_kernel(ca_ref, cb_ref, down_ref, out_ref):
    count = ca_ref.shape[0]
    out_ref[:count, :] = nt(ca_ref[...], down_ref[...]).astype(bf16)
    out_ref[count:, :] = nt(cb_ref[...], down_ref[...]).astype(bf16)


def change(ca, cb, down):
    count, features = ca.shape
    hidden = down.shape[0]
    block = 2 * LANES
    steps = pl.cdiv(hidden, block)
    whole = pl.BlockSpec((count, features), lambda i: (0, 0))
    return call(
        change_kernel,
        jax.ShapeDtypeStruct((2 * count, hidden), bf16),
        4 * count * features * hidden,
        12 * 1024 * 1024,
        grid=(steps,),
        in_specs=[whole, whole, pl.BlockSpec((block, features), lambda i: (i, 0))],
        out_specs=pl.BlockSpec((2 * count, block), lambda i: (0, i)),
    )(ca, cb, down)


def feed_kernel(*refs, start, first, sides):
    place_ref, na_ref, nb_ref, ca_ref, cb_ref, gate_ref, gate_o_ref, up_ref, up_o_ref, down_ref, change_ref = refs[:11]
    refs = refs[11:]
    if not first:
        sums = refs[:4]
        refs = refs[4:]
    grad_refs = refs[:6]
    outs = refs[6:10]
    refs = refs[10:]
    (n_s, c_s, wg, wu, wd, change_s, inner_s, gate_s, up_s, *part_s) = refs[:12]
    refs = refs[12:]
    if not first:
        held = refs[:2]
        refs = refs[2:]
    totals = refs[:2]
    in_sem, sum_sem, out_sem = refs[2:]
    tokens, features = n_s.shape
    count = tokens // 2
    width = wg.shape[1]
    rows_held = gate_ref.shape[0]
    hidden = down_ref.shape[0]
    me = place_ref[0]
    lanes = pl.ds(pl.multiple_of(me * hidden + start, LANES), width)
    own_rows = pl.ds(pl.multiple_of(me * rows_held, rows_held), rows_held)
    other_rows = pl.ds(pl.multiple_of((1 - me) * rows_held, rows_held), rows_held)
    low, high = pl.ds(0, count), pl.ds(count, count)

    moves = [
        (na_ref, n_s.at[low, :]),
        (nb_ref, n_s.at[high, :]),
        (gate_ref.at[:, lanes], wg.at[own_rows, :]),
        (gate_o_ref.at[:, lanes], wg.at[other_rows, :]),
        (up_ref.at[:, lanes], wu.at[own_rows, :]),
        (up_o_ref.at[:, lanes], wu.at[other_rows, :]),
        (change_ref.at[:, pl.ds(start, width)], change_s),
        (down_ref.at[pl.ds(start, width), :], wd),
        (ca_ref, c_s.at[low, :]),
        (cb_ref, c_s.at[high, :]),
    ]
    copies = [pltpu.make_async_copy(a, b, in_sem.at[i]) for i, (a, b) in enumerate(moves)]
    for copy in copies:
        copy.start()
    sum_copies = []
    if not first:
        places = ((held[0], low), (held[1], low), (held[0], high), (held[1], high))
        sum_copies = [
            pltpu.make_async_copy(sums[i], target.at[rows, :], sum_sem.at[i])
            for i, (target, rows) in enumerate(places)
        ]
        for copy in sum_copies:
            copy.start()
    for copy in copies[:8] + sum_copies:
        copy.wait()
    step = 256

    def body(i, carry):
        rows = pl.ds(pl.multiple_of(i * step, step), step)
        normed = n_s[rows, :]
        gate = nn(normed, wg[...])
        up = nn(normed, wu[...])
        change = change_s[rows, :].astype(f32)
        sigmoid = 1.0 / (1.0 + jnp.exp(-gate))
        activated = gate * sigmoid
        inner = (activated * up).astype(bf16)
        gate_g = (change * up * sigmoid * (1.0 + gate * (1.0 - sigmoid))).astype(bf16)
        up_g = (change * activated).astype(bf16)
        inner_s[rows, :] = inner
        gate_s[rows, :] = gate_g
        up_s[rows, :] = up_g
        result = nn(inner, wd[...])
        back = nt(gate_g, wg[...]) + nt(up_g, wu[...])
        if not first:
            result = result + held[0][rows, :].astype(f32)
            back = back + held[1][rows, :].astype(f32)
        totals[0][rows, :] = result.astype(bf16)
        totals[1][rows, :] = back.astype(bf16)
        return carry

    lax.fori_loop(0, tokens // step, body, 0)
    for copy in copies[8:]:
        copy.wait()
    leaving = []

    def leave(source, target):
        copy = pltpu.make_async_copy(source, target, out_sem.at[len(leaving)])
        copy.start()
        leaving.append(copy)

    for i, (total, rows) in enumerate(
        ((totals[0], low), (totals[1], low), (totals[0], high), (totals[1], high))
    ):
        leave(total.at[rows, :], outs[i])

    def part_leaves(i):
        keep, send = grad_refs[2 * i : 2 * i + 2]
        rows = part_s[i].shape[0] // 2
        side = place_ref[sides[i]]
        leave(part_s[i].at[pl.ds(pl.multiple_of((1 - side) * rows, 16), rows), :], send)
        leave(part_s[i].at[pl.ds(pl.multiple_of(side * rows, 16), rows), :], keep)

    mine_s, theirs_s, down_s = part_s

    def tiles_loop(body):
        def step(i, carry):
            body(i * HALF, HALF)
            return carry

        lax.fori_loop(0, width // HALF, step, 0)
        if width % HALF:
            body(width // HALF * HALF, width % HALF)

    def columns_of(at, size):
        return pl.ds(at if isinstance(at, int) else pl.multiple_of(at, HALF), size)

    def wide_grads(at, size):
        for kind, source in enumerate((gate_s, up_s)):
            grads = tn(n_s[...], source[:, columns_of(at, size)]).astype(bf16)
            for j in range(size // LANES):
                row = (kind * width // LANES + at // LANES + j) * rows_held
                rows = pl.ds(row if isinstance(row, int) else pl.multiple_of(row, 16), rows_held)
                tile = grads[:, j * LANES : (j + 1) * LANES]

                @pl.when(me == 0)
                def _():
                    mine_s[rows, :] = tile[:rows_held]
                    theirs_s[rows, :] = tile[rows_held:]

                @pl.when(me == 1)
                def _():
                    mine_s[rows, :] = tile[rows_held:]
                    theirs_s[rows, :] = tile[:rows_held]

    def down_grads(at, size):
        grads = tn(inner_s[:, columns_of(at, size)], c_s[...]).astype(bf16)
        for j in range(features // LANES):
            row = j * width + at
            rows = pl.ds(row if isinstance(row, int) else pl.multiple_of(row, 16), size)
            down_s[rows, :] = grads[:, j * LANES : (j + 1) * LANES]

    tiles_loop(wide_grads)
    part_leaves(0)
    part_leaves(1)
    tiles_loop(down_grads)
    part_leaves(2)
    for copy in leaving:
        copy.wait()


def feed(place, na, nb, ca, cb, gate, gate_o, up, up_o, down, change, sums, *, start, width, sides):
    count, features = na.shape
    first = sums is None
    sums = () if first else tuple(sums)
    anywhere = pl.BlockSpec(memory_space=pl.ANY)
    rows = features * width // LANES
    tokens = (2 * count, features)
    outs = [jax.ShapeDtypeStruct((rows // 2, LANES), bf16)] * 6
    outs += [jax.ShapeDtypeStruct((count, features), bf16)] * 4
    scratch = [pltpu.VMEM(tokens, bf16)] * 2
    scratch += [pltpu.VMEM((features, width), bf16)] * 2 + [pltpu.VMEM((width, features), bf16)]
    scratch += [pltpu.VMEM((2 * count, width), bf16)] * 4
    scratch += [pltpu.VMEM((rows, LANES), bf16)] * 3
    scratch += [pltpu.VMEM(tokens, bf16)] * (2 if first else 4)
    scratch += [pltpu.SemaphoreType.DMA((n,)) for n in (10, 4, 10)]
    return call(
        functools.partial(feed_kernel, start=start, first=first, sides=sides),
        tuple(outs),
        18 * 2 * count * features * width,
        30 * 1024 * 1024,
        in_specs=[pl.BlockSpec(memory_space=pltpu.SMEM)] + [anywhere] * (10 + len(sums)),
        out_specs=(anywhere,) * 10,
        scratch_shapes=scratch,
    )(place, na, nb, ca, cb, gate, gate_o, up, up_o, down, change, *sums)


def middle_kernel(
    place_ref, part_ref, got_ref, h1_ref, dy_ref, params_ref, w_ref, o_ref,
    dh1_ref, do_ref, gg_ref, mine_ref, theirs_ref, low_s,
):
    count, features = part_ref.shape
    step = 256
    gg_ref[...] = jnp.zeros_like(gg_ref)

    def body(i, carry):
        rows = pl.ds(pl.multiple_of(i * step, step), step)
        back = part_ref[rows, :].astype(f32) + got_ref[rows, :].astype(f32)
        hidden = h1_ref[rows, :]
        scale = lax.rsqrt(jnp.mean(hidden * hidden, -1, keepdims=True) + eps_norm)
        normal = hidden * scale
        gg_ref[...] += jnp.sum(back * normal, 0, keepdims=True)
        change = back * params_ref[:, GAIN_TWO]
        grad = dy_ref[rows, :].astype(f32) + scale * (
            change - normal * jnp.mean(change * normal, -1, keepdims=True)
        )
        dh1_ref[rows, :] = grad
        low = grad.astype(bf16)
        low_s[rows, :] = low
        do_ref[rows, :] = nt(low, w_ref[...]).astype(bf16)
        return carry

    lax.fori_loop(0, count // step, body, 0)
    store_split(place_ref, tn(o_ref[...], low_s[...]).astype(bf16), mine_ref, theirs_ref, 0)


def store_split(place_ref, grads, mine_ref, theirs_ref, first_tile):
    half_rows = grads.shape[0] // 2
    me = place_ref[0]
    for j in range(grads.shape[1] // LANES):
        row = (first_tile + j) * half_rows
        tile = grads[:, j * LANES : (j + 1) * LANES]

        @pl.when(me == 0)
        def _():
            mine_ref[row : row + half_rows, :] = tile[:half_rows]
            theirs_ref[row : row + half_rows, :] = tile[half_rows:]

        @pl.when(me == 1)
        def _():
            mine_ref[row : row + half_rows, :] = tile[half_rows:]
            theirs_ref[row : row + half_rows, :] = tile[:half_rows]


def middle(place, part, got, h1, dy, params, w, o):
    count, features = part.shape
    rows = (features // 2) * (features // LANES)
    return call(
        middle_kernel,
        (
            jax.ShapeDtypeStruct((count, features), f32),
            jax.ShapeDtypeStruct((count, HQ * HD), bf16),
            jax.ShapeDtypeStruct((1, features), f32),
            jax.ShapeDtypeStruct((rows, LANES), bf16),
            jax.ShapeDtypeStruct((rows, LANES), bf16),
        ),
        4 * count * features * features,
        12 * 1024 * 1024,
        in_specs=in_vmem(7),
        scratch_shapes=[pltpu.VMEM((count, features), bf16)],
    )(place, part, got, h1, dy, params, w, o)


def query_kernel(
    place_ref, dqa_ref, dqb_ref, n1_ref, w_ref, back_ref, gb_ref, mine_ref, theirs_ref, dp_s
):
    count = n1_ref.shape[0]
    width = HQ * HD
    split_at = dqa_ref.shape[1]
    step = 256
    gb_ref[...] = jnp.zeros_like(gb_ref)

    def body(i, carry):
        rows = pl.ds(pl.multiple_of(i * step, step), step)
        dp_s[rows, :split_at] = dqa_ref[rows, :]
        dp_s[rows, split_at:] = dqb_ref[rows, :]
        grads = dp_s[rows, :]
        gb_ref[...] += jnp.sum(grads.astype(f32), 0, keepdims=True)
        back_ref[rows, :] = nt(grads, w_ref[:, :width])
        return carry

    lax.fori_loop(0, count // step, body, 0)
    store_split(place_ref, tn(n1_ref[...], dp_s[...]).astype(bf16), mine_ref, theirs_ref, 0)


def query_back(place, dqa, dqb, n1, w):
    count, features = n1.shape
    width = HQ * HD
    rows = (features // 2) * (width // LANES)
    return call(
        query_kernel,
        (
            jax.ShapeDtypeStruct((count, features), f32),
            jax.ShapeDtypeStruct((1, width), f32),
            jax.ShapeDtypeStruct((rows, LANES), bf16),
            jax.ShapeDtypeStruct((rows, LANES), bf16),
        ),
        4 * count * features * width,
        10 * 1024 * 1024,
        in_specs=in_vmem(4),
        scratch_shapes=[pltpu.VMEM((count, width), bf16)],
    )(place, dqa, dqb, n1, w)


VECTOR_ROWS = 128


def last_kernel(
    place_ref, own_ref, one_ref, two_ref, n1_ref, x_ref, params_ref, w_ref, part_ref, dh1_ref, cos_ref, sin_ref,
    qm_ref, qt_ref, om_ref, ot_ref, gbq_ref, ggt_ref, dx_ref, mine_ref, theirs_ref, dp_s, gg_ref, gb_ref,
):
    count = n1_ref.shape[0]
    width = HQ * HD
    step = 256
    gg_ref[...] = jnp.zeros_like(gg_ref)
    gb_ref[...] = jnp.zeros_like(gb_ref)

    def body(i, carry):
        rows = pl.ds(pl.multiple_of(i * step, step), step)
        pairs = own_ref[rows, :] + one_ref[rows, :].astype(f32) + two_ref[rows, :].astype(f32)
        key = pairs[:, :LANES]
        key = key * cos_ref[rows, :] - flip_lanes_half(key * sin_ref[rows, :])
        dp_s[rows, :LANES] = key.astype(bf16)
        dp_s[rows, LANES:] = pairs[:, LANES:].astype(bf16)
        grads = dp_s[rows, :]
        gb_ref[...] += jnp.sum(grads.astype(f32), 0, keepdims=True)
        back = part_ref[rows, :] + nt(grads, w_ref[:, width:])
        x = x_ref[rows, :].astype(f32)
        scale = lax.rsqrt(jnp.mean(x * x, -1, keepdims=True) + eps_norm)
        normal = x * scale
        gg_ref[...] += jnp.sum(back * normal, 0, keepdims=True)
        change = back * params_ref[:, GAIN_ONE]
        grad = dh1_ref[rows, :] + scale * (
            change - normal * jnp.mean(change * normal, -1, keepdims=True)
        )
        dx_ref[rows, :] = grad.astype(bf16)
        return carry

    lax.fori_loop(0, count // step, body, 0)
    at = qm_ref.shape[0]
    tiles = (w_ref.shape[1] - width) // LANES
    rows_held = at * LANES // width
    store_split(
        place_ref, tn(n1_ref[...], dp_s[...]).astype(bf16), mine_ref, theirs_ref, at // rows_held
    )
    mine_ref[:at, :] = qm_ref[...]
    theirs_ref[:at, :] = qt_ref[...]
    at += tiles * rows_held
    after = at + om_ref.shape[0]
    mine_ref[at:after, :] = om_ref[...]
    theirs_ref[at:after, :] = ot_ref[...]
    vectors = []
    for ref in (gg_ref, gbq_ref, gb_ref, ggt_ref):
        vectors += [ref[:, j * LANES : (j + 1) * LANES] for j in range(ref.shape[1] // LANES)]
    vectors.append(jnp.zeros((VECTOR_ROWS - len(vectors), LANES), f32))
    vectors = jnp.concatenate(vectors, 0).astype(bf16)
    mine_ref[after:, :] = vectors
    theirs_ref[after:, :] = vectors


def last(place, own, one, two, n1, x, params, w, part, dh1, cosine, sine, qm, qt, om, ot, gbq, ggt):
    count, features = n1.shape
    columns = w.shape[1] - HQ * HD
    rows = (features // 2) * (columns // LANES) + qm.shape[0] + om.shape[0] + VECTOR_ROWS
    return call(
        last_kernel,
        (
            jax.ShapeDtypeStruct((count, features), bf16),
            jax.ShapeDtypeStruct((rows, LANES), bf16),
            jax.ShapeDtypeStruct((rows, LANES), bf16),
        ),
        4 * count * features * columns,
        14 * 1024 * 1024,
        in_specs=in_vmem(17),
        scratch_shapes=[
            pltpu.VMEM((count, columns), bf16),
            pltpu.VMEM((1, features), f32),
            pltpu.VMEM((1, columns), f32),
        ],
    )(place, own, one, two, n1, x, params, w, part, dh1, cosine, sine, qm, qt, om, ot, gbq, ggt)


def swap(values):
    return lax.ppermute(values, "fsdp", [(0, 1), (1, 0)])


def flip(values, dim):
    axis, bit = dim
    size = lax.axis_size(axis)
    return lax.ppermute(values, axis, [(i, i ^ (1 << bit)) for i in range(size)])


def side(dim):
    axis, bit = dim
    return (lax.axis_index(axis) >> bit) & 1


def add(*terms):
    total = terms[0].astype(f32)
    for term in terms[1:]:
        total = total + term.astype(f32)
    return total.astype(bf16)


def take(array, index):
    return lax.dynamic_index_in_dim(array, index, 0, False)


def join(low, other, index):
    out = jnp.zeros((2,) + low.shape, low.dtype)
    out = lax.dynamic_update_index_in_dim(out, low, index, 0)
    return lax.dynamic_update_index_in_dim(out, other, 1 - index, 0)


def rest_of_seq(values):
    for bit in range(2, lax.axis_size("seq").bit_length() - 1):
        values = add(values, flip(values, ("seq", bit)))
    return values


class Order:
    def __init__(self):
        self.token = None

    def __call__(self, step, *operands):
        if self.token is not None:
            operands, _ = lax.optimization_barrier((operands, self.token))
        out = step(*operands)
        self.token = jax.tree.leaves(out)[0]
        return out


def fold_kernel(place_ref, *refs, sides):
    n = 2 * len(sides)
    for i, number in enumerate(sides):
        kept, got = refs[2 * i : 2 * i + 2]
        keep, send = refs[n + 2 * i : n + 2 * i + 2]
        rows = keep.shape[0]
        side = place_ref[number]
        for target, at in ((keep, side), (send, 1 - side)):
            at = pl.ds(pl.multiple_of(at * rows, 16), rows)
            target[...] = (kept[at, :].astype(f32) + got[at, :].astype(f32)).astype(bf16)


def flatten(pairs):
    return [array for pair in pairs for array in pair]


def fold(place, pairs, sides):
    rows = [kept.shape[0] // 2 for kept, _ in pairs]
    outs = call(
        functools.partial(fold_kernel, sides=sides),
        tuple(jax.ShapeDtypeStruct((n, LANES), bf16) for n in rows for _ in range(2)),
        4 * sum(rows) * LANES,
        12 * sum(rows) * LANES,
        in_specs=in_vmem(2 * len(pairs)),
    )(place, *flatten(pairs))
    return list(zip(outs[::2], outs[1::2]))


def stack_kernel(*refs):
    total = refs[-1]
    at = 0
    for kept, got in zip(refs[:-1:2], refs[1:-1:2]):
        rows = kept.shape[0]
        total[at : at + rows, :] = (kept[...].astype(f32) + got[...].astype(f32)).astype(bf16)
        at += rows


def stack(pairs):
    rows = sum(kept.shape[0] for kept, _ in pairs)
    return call(
        stack_kernel, jax.ShapeDtypeStruct((rows, LANES), bf16), rows * LANES, 6 * rows * LANES
    )(*flatten(pairs))


def sum_kernel(*refs):
    n = 2 * len(refs) // 3
    for kept, got, total in zip(refs[:n:2], refs[1:n:2], refs[n:]):
        total[...] = (kept[...].astype(f32) + got[...].astype(f32)).astype(bf16)


def sum_parts(pairs):
    rows = [kept.shape[0] for kept, _ in pairs]
    return call(
        sum_kernel,
        tuple(jax.ShapeDtypeStruct((n, LANES), bf16) for n in rows),
        sum(rows) * LANES,
        6 * sum(rows) * LANES,
    )(*flatten(pairs))


def unstack_kernel(total, got, *parts):
    at = 0
    for part in parts:
        rows = part.shape[0]
        both = total[at : at + rows, :].astype(f32) + got[at : at + rows, :].astype(f32)
        part[...] = both.astype(bf16)
        at += rows


def unstack(total, got, sizes):
    return call(
        unstack_kernel,
        tuple(jax.ShapeDtypeStruct((n, LANES), bf16) for n in sizes),
        total.shape[0] * LANES,
        6 * total.shape[0] * LANES,
    )(total, got)


def join_kernel(place_ref, *refs, sides):
    for i, number in enumerate(sides):
        own, got = refs[2 * i : 2 * i + 2]
        both = refs[2 * len(sides) + i]
        rows = own.shape[0]
        side = place_ref[number]
        both[pl.ds(pl.multiple_of(side * rows, 16), rows), :] = own[...]
        both[pl.ds(pl.multiple_of((1 - side) * rows, 16), rows), :] = got[...]


def join_parts(place, pairs, sides):
    rows = [own.shape[0] for own, _ in pairs]
    return call(
        functools.partial(join_kernel, sides=sides),
        tuple(jax.ShapeDtypeStruct((2 * n, LANES), bf16) for n in rows),
        1,
        8 * sum(rows) * LANES,
        in_specs=in_vmem(2 * len(pairs)),
    )(place, *flatten(pairs))


def bring_halves(place_ref, refs, sides, targets, in_sem):
    copies = []
    for i, number in enumerate(sides):
        side = place_ref[number]
        rows = targets[i].shape[0] // 2
        for ref, at in ((refs[2 * i], side), (refs[2 * i + 1], 1 - side)):
            at = pl.ds(pl.multiple_of(at * rows, 16), rows)
            copy = pltpu.make_async_copy(ref, targets[i].at[at, :], in_sem.at[len(copies)])
            copy.start()
            copies.append(copy)
    for copy in copies:
        copy.wait()


def untile_kernel(*refs, start, width, first, sides, n_parts):
    place_ref = refs[0]
    parts = refs[1 : 1 + n_parts]
    refs = refs[1 + n_parts + (0 if first else 3) :]
    gate_ref, up_ref, down_ref, mine_s, theirs_s, downs_s, wide_s, down_s, in_sem, out_sem = refs
    me = place_ref[0]
    features = down_ref.shape[1]
    hidden = down_ref.shape[0]
    rows_held = gate_ref.shape[0]
    targets = (mine_s, theirs_s, downs_s)
    bring_halves(place_ref, parts, sides, targets, in_sem)
    leaving = []

    def leave(source, target):
        copy = pltpu.make_async_copy(source, target, out_sem.at[len(leaving)])
        copy.start()
        leaving.append(copy)

    tiles = width // LANES
    for i, (source, owner) in enumerate(((mine_s, me), (theirs_s, 1 - me))):
        lanes = pl.ds(pl.multiple_of(owner * hidden + start, LANES), width)
        for kind, target in enumerate((gate_ref, up_ref)):
            wide = wide_s.at[2 * i + kind]
            for j in range(tiles):
                row = (kind * tiles + j) * rows_held
                wide[:, j * LANES : (j + 1) * LANES] = source[row : row + rows_held, :].astype(f32)
            leave(wide, target.at[:, lanes])
    for j in range(features // LANES):
        row = j * width
        down_s[:, j * LANES : (j + 1) * LANES] = downs_s[row : row + width, :].astype(f32)
    leave(down_s, down_ref.at[pl.ds(start, width), :])
    for copy in leaving:
        copy.wait()


def untile(place, parts, outs, *, start, width, features, hidden, sides):
    first = outs is None
    rows_held = features // 2
    rows = features * width // LANES
    anywhere = pl.BlockSpec(memory_space=pl.ANY)
    outs = () if first else tuple(outs)
    n_parts = len(parts)
    return call(
        functools.partial(
            untile_kernel, start=start, width=width, first=first, sides=sides, n_parts=n_parts
        ),
        (
            jax.ShapeDtypeStruct((rows_held, 2 * hidden), f32),
            jax.ShapeDtypeStruct((rows_held, 2 * hidden), f32),
            jax.ShapeDtypeStruct((hidden, features), f32),
        ),
        3 * features * width,
        3 * features * width * 6,
        in_specs=[pl.BlockSpec(memory_space=pltpu.SMEM)] + [anywhere] * (n_parts + len(outs)),
        out_specs=(anywhere,) * 3,
        scratch_shapes=[pltpu.VMEM((rows, LANES), bf16)] * 3
        + [
            pltpu.VMEM((4, rows_held, width), f32),
            pltpu.VMEM((width, features), f32),
            pltpu.SemaphoreType.DMA((6,)),
            pltpu.SemaphoreType.DMA((5,)),
        ],
        input_output_aliases={} if first else {1 + n_parts + i: i for i in range(3)},
    )(place, *parts, *outs)


def split_kernel(place_ref, mine_ref, theirs_ref, *refs, sides):
    base = 0
    for i, number in enumerate(sides):
        side = place_ref[number]
        rows = refs[2 * i].shape[0]
        for target, at in zip(refs[2 * i : 2 * i + 2], (side, 1 - side)):
            at = pl.ds(pl.multiple_of(base + at * rows, 16), rows)
            target[...] = (mine_ref[at, :].astype(f32) + theirs_ref[at, :].astype(f32)).astype(bf16)
        base += 2 * rows


def split(place, mine, theirs, *, sides):
    rows = mine.shape[0] // (2 * len(sides))
    outs = call(
        functools.partial(split_kernel, sides=sides),
        (jax.ShapeDtypeStruct((rows, LANES), bf16),) * (2 * len(sides)),
        mine.shape[0] * LANES,
        6 * mine.shape[0] * LANES,
        in_specs=in_vmem(2),
    )(place, mine, theirs)
    return list(zip(outs[::2], outs[1::2]))


def untile_flat_kernel(*refs, sides):
    place_ref = refs[0]
    parts = refs[1 : 1 + 2 * len(sides)]
    *targets, vector_ref, flat_s, in_sem = refs[1 + 2 * len(sides) :]
    rows = flat_s.shape[0] // len(sides)
    halves = [flat_s.at[pl.ds(i * rows, rows), :] for i in range(len(sides))]
    bring_halves(place_ref, parts, sides, halves, in_sem)
    rows_held = targets[0].shape[0]
    row = 0
    for target in targets:
        for j in range(target.shape[1] // LANES):
            target[:, j * LANES : (j + 1) * LANES] = flat_s[row : row + rows_held, :].astype(f32)
            row += rows_held
    vector_ref[...] = flat_s[row:, :].astype(f32)


def untile_flat(place, parts, *, rows_held, widths, sides):
    rows = rows_held * sum(widths) // LANES + VECTOR_ROWS
    anywhere = pl.BlockSpec(memory_space=pl.ANY)
    return call(
        functools.partial(untile_flat_kernel, sides=sides),
        (
            *(jax.ShapeDtypeStruct((rows_held, width), f32) for width in widths),
            jax.ShapeDtypeStruct((VECTOR_ROWS, LANES), f32),
        ),
        rows * LANES,
        rows * LANES * 6,
        in_specs=[pl.BlockSpec(memory_space=pltpu.SMEM)] + [anywhere] * len(parts),
        out_specs=(pl.BlockSpec(memory_space=pltpu.VMEM),) * (len(widths) + 1),
        scratch_shapes=[
            pltpu.VMEM((rows, LANES), bf16), pltpu.SemaphoreType.DMA((2 * len(sides),))
        ],
    )(place, *parts)


class FlatSum:
    def __init__(self, place, order):
        self.place, self.order = place, order
        self.links, self.sides = ((X, Y), (Y, X)), ((1, 2), (2, 1))

    def over(self, arrays, level):
        return [flip(array, link) for array, link in zip(arrays, self.links[level])]

    def leave(self, mine, theirs):
        pairs = self.order(functools.partial(split, sides=self.sides[0]), self.place, mine, theirs)
        kept, sent = zip(*pairs)
        self.held = list(zip(kept, self.over(sent, 0)))

    def halve(self):
        pairs = self.order(lambda pairs: fold(self.place, pairs, self.sides[1]), self.held)
        kept, sent = zip(*pairs)
        self.held = list(zip(kept, self.over(sent, 1)))

    def sum(self):
        total = rest_of_seq(self.order(stack, self.held))
        self.total = total, flip(total, Z)

    def across(self):
        total = self.order(add, *self.total)
        for bit in range(2, lax.axis_size("ctx").bit_length() - 1):
            total = add(total, flip(total, ("ctx", bit)))
        self.total = total, flip(total, FAR)

    def turn(self):
        total, got = self.total
        sizes = (total.shape[0] // 2,) * 2
        own = self.order(lambda total, got: unstack(total, got, sizes), total, got)
        self.held = list(zip(own, self.over(own, 1)))

    def join(self):
        own = self.order(lambda pairs: join_parts(self.place, pairs, self.sides[1]), self.held)
        self.held = list(zip(own, self.over(own, 0)))


class LinkSum:
    def __init__(self, place, order):
        self.place, self.order = place, order
        links, numbers = (X, Y, Z), (1, 2, 4)
        self.links = [[links[(i + j) % 3] for i in range(3)] for j in range(3)]
        self.sides = [tuple(numbers[(i + j) % 3] for i in range(3)) for j in range(3)]

    def over(self, arrays, level):
        return [flip(array, link) for array, link in zip(arrays, self.links[level])]

    def leave(self, pairs):
        kept, sent = zip(*pairs)
        self.held = list(zip(kept, self.over(sent, 0)))

    def halve(self, level):
        pairs = self.order(lambda pairs: fold(self.place, pairs, self.sides[level]), self.held)
        kept, sent = zip(*pairs)
        self.held = list(zip(kept, self.over(sent, level)))

    def rest_of_axes(self, total):
        total = rest_of_seq(total)
        for bit in range(2, lax.axis_size("ctx").bit_length() - 1):
            total = add(total, flip(total, ("ctx", bit)))
        return total

    def across(self):
        self.sizes = [kept.shape[0] for kept, _ in self.held]
        total = self.rest_of_axes(self.order(stack, self.held))
        self.total = total, flip(total, FAR)

    def turn(self):
        own = list(self.order(lambda total, got: unstack(total, got, self.sizes), *self.total))
        own[1] = swap(own[1])
        self.held = list(zip(own, self.over(own, 2)))

    def across_each(self):
        totals = [self.rest_of_axes(total) for total in self.order(sum_parts, self.held)]
        self.held = [(total, flip(total, FAR)) for total in totals]

    def turn_each(self, i):
        own = self.order(add, *self.held[i])
        if i == 1:
            own = swap(own)
        self.held[i] = own, flip(own, self.links[2][i])

    def join(self, level):
        own = self.order(lambda pairs: join_parts(self.place, pairs, self.sides[level]), self.held)
        self.held = list(zip(own, self.over(own, level - 1)))

    @property
    def parts(self):
        return flatten(self.held)


X, Y, Z, FAR = ("seq", 0), ("seq", 1), ("ctx", 0), ("ctx", 1)


def on_device(
    block_input,
    segment_ids,
    out_cotangent,
    input_gain,
    query_weight,
    query_bias,
    key_weight,
    key_bias,
    value_weight,
    value_bias,
    output_weight,
    middle_gain,
    gate_weight,
    up_weight,
    down_weight,
):
    me = lax.axis_index("fsdp")
    ctx = lax.axis_index("ctx")
    chunks = lax.axis_size("ctx")
    place = jnp.stack([me, side(X), side(Y), ctx, side(Z)]).astype(jnp.int32)
    x = block_input[0]
    dy = out_cotangent[0]
    count, features = x.shape
    hidden = down_weight.shape[0]
    kv_width = KVH * HD

    own = (query_weight, key_weight, value_weight)
    other = tuple(swap(w) for w in own)
    vectors = (input_gain, query_bias, key_bias, value_bias, middle_gain)
    mine = jnp.concatenate(vectors)
    theirs = swap(mine)
    low = jnp.where(me == 0, mine, theirs).astype(f32)
    high = jnp.where(me == 0, theirs, mine).astype(f32)
    params = []
    at = 0
    for vector in vectors:
        size = vector.shape[0]
        params += [low[at : at + size], high[at : at + size]]
        at += size
    params = jnp.concatenate(params)[None]

    first = ctx * count
    positions = (first + jnp.arange(count, dtype=jnp.int32)).astype(f32)
    inverse = theta_base ** (-jnp.arange(0, HD, 2, dtype=f32) / HD)
    angle = positions[:, None] * jnp.tile(inverse, LANES // inverse.shape[0])[None, :]
    cosine, sine = jnp.cos(angle), jnp.sin(angle)

    n1, q, kv, w_in = project(place, x, params, own, other, cosine, sine)
    out_other = swap(output_weight)
    gate_other, up_other = swap(gate_weight), swap(up_weight)
    dy_other = swap(dy)

    reach = WINDOW // count
    before = [
        lax.ppermute(kv, "ctx", [(i, i + d) for i in range(chunks - d)])
        for d in range(1, reach + 1)
    ]
    order = Order()
    changes = order(change, dy, dy_other, down_weight)
    o, lse = order(attend, place, q, kv, *before, segment_ids)
    h1, n2, w_out = merge(place, x, o, output_weight, out_other, params)
    n2_other = swap(n2)

    widths = WIDTHS
    starts = tuple(sum(widths[:i]) for i in range(len(widths)))
    one, two = (LinkSum(place, order) for _ in range(2))
    first_sides = one.sides[0]

    def run_feed(i, token_sums):
        step = functools.partial(
            feed, start=starts[i], width=widths[i], sides=first_sides
        )
        *grads, own_result, own_back, other_result, other_back = order(
            step, place, n2, n2_other, dy, dy_other, gate_weight, gate_other, up_weight, up_other,
            down_weight, changes, token_sums,
        )
        pairs = [(grads[2 * i], grads[2 * i + 1]) for i in range(3)]
        return pairs, (own_result, own_back, other_result, other_back)

    def run_untile(i, parts, outs):
        step = functools.partial(
            untile, start=starts[i], width=widths[i], features=features, hidden=hidden,
            sides=first_sides,
        )
        return order(step, place, parts, outs)

    pairs, token_sums = run_feed(0, None)
    one.leave(pairs)
    pairs, token_sums = run_feed(1, token_sums)
    own_result, own_back, other_result, other_back = token_sums
    got_back = swap(other_back)
    one.halve(1)

    dh1, do, gg_two, out_mine, out_theirs = order(
        middle, place, own_back, got_back, h1, dy, params, w_out, o
    )
    one.halve(2)
    one.across()
    pairs = order(lambda pairs: pairs, pairs)
    two.leave(pairs)
    back_operands = (place, q, do, kv, *before, segment_ids, lse, cosine, sine)
    dq_low, *pair_sums = order(
        functools.partial(attend_back, first_pair=0, pairs=4), *back_operands, None
    )
    two.halve(1)
    dq_high, own_pairs, *sent_pairs = order(
        functools.partial(attend_back, first_pair=4, pairs=3), *back_operands, pair_sums
    )
    got_pairs = [
        lax.ppermute(pairs, "ctx", [(i + d, i) for i in range(chunks - d)])
        for d, pairs in enumerate(sent_pairs, 1)
    ]
    one.turn()
    two.halve(2)
    back_part, gb_query, query_mine, query_theirs = order(
        query_back, place, dq_low, dq_high, n1, w_in
    )
    two.across_each()
    dx, mine, theirs = order(
        last, place, own_pairs, *got_pairs, n1, x, params, w_in, back_part, dh1, cosine, sine,
        query_mine, query_theirs, out_mine, out_theirs, gb_query, gg_two,
    )
    input_grad = dx[None]
    width = HQ * HD
    rest = FlatSum(place, order)
    got = swap(theirs)
    one.join(2)
    two.turn_each(0)
    rest.leave(mine, got)
    one.join(1)
    two.turn_each(1)
    block_output = order(
        lambda a, b, c: (a + b.astype(f32) + c.astype(f32)).astype(bf16), h1, own_result, swap(other_result)
    )[None]
    rest.halve()
    two.turn_each(2)
    rest.sum()
    outs = run_untile(0, one.parts, None)
    two.join(2)
    rest.across()
    rest.turn()
    two.join(1)
    rest.join()
    gates, ups, gw_down = run_untile(1, two.parts, outs)
    gw_query, gw_key, gw_value, gw_out, vector = order(
        functools.partial(
            untile_flat, rows_held=features // 2, widths=(width, kv_width, kv_width, features),
            sides=rest.sides[0],
        ),
        place,
        flatten(rest.held),
    )
    vector = vector.reshape(-1)
    shares = []
    at = 0
    for size in (features, width, kv_width, kv_width, features):
        shares.append(lax.dynamic_slice_in_dim(vector, at + me * (size // 2), size // 2, 0))
        at += size
    gg_one, gb_query, gb_key, gb_value, gg_two = shares
    return (
        block_output,
        input_grad,
        gg_one,
        gw_query,
        gb_query,
        gw_key,
        gb_key,
        gw_value,
        gb_value,
        gw_out,
        gg_two,
        gates,
        ups,
        gw_down,
    )


def solution(mesh):
    return jax.shard_map(
        on_device,
        mesh=mesh,
        in_specs=(
            P(("seq", "fsdp"), "ctx", None),
            P(("seq", "fsdp"), None),
            P(("seq", "fsdp"), "ctx", None),
            P("fsdp"),
            P("fsdp", None),
            P("fsdp"),
            P("fsdp", None),
            P("fsdp"),
            P("fsdp", None),
            P("fsdp"),
            P("fsdp", None),
            P("fsdp"),
            P("fsdp", None),
            P("fsdp", None),
            P("fsdp", None),
        ),
        out_specs=(
            P(("seq", "fsdp"), "ctx", None),
            P(("seq", "fsdp"), "ctx", None),
            P("fsdp"),
            P("fsdp", None),
            P("fsdp"),
            P("fsdp", None),
            P("fsdp"),
            P("fsdp", None),
            P("fsdp"),
            P("fsdp", None),
            P("fsdp"),
            P("fsdp", None),
            P("fsdp", None),
            P("fsdp", None),
        ),
        check_vma=False,
    )
```

```python
import functools

import jax
import jax.numpy as jnp
from jax import lax
from jax.experimental import pallas as pl
from jax.experimental.pallas import tpu as pltpu
from jax.sharding import PartitionSpec as P

HQ = 14
KVH = 2
HD = 64
WINDOW = 1024
PAIRS = HQ // 2
LANES = 128
HALF = 256

theta_base = 1000000.0
eps_norm = 1e-06
masked_score = -1e30
f32 = jnp.float32
bf16 = jnp.bfloat16
VMEM_BYTES = 58 * 1024 * 1024
WIDTHS = (1280, 1152)


def nn(a, b):
    return lax.dot_general(a, b, (((1,), (0,)), ((), ())), preferred_element_type=f32)


def nt(a, b):
    return lax.dot_general(a, b, (((1,), (1,)), ((), ())), preferred_element_type=f32)


def tn(a, b):
    return lax.dot_general(a, b, (((0,), (0,)), ((), ())), preferred_element_type=f32)


def flip_lanes_half(values):
    width = values.shape[-1]
    lane = lax.broadcasted_iota(jnp.int32, values.shape, len(values.shape) - 1)
    up = pltpu.roll(values, width - 32, len(values.shape) - 1)
    down = pltpu.roll(values, 32, len(values.shape) - 1)
    return jnp.where((lane & 63) < 32, -up, down)


def call(kernel, out_shape, flops, moved, **kwargs):
    return pl.pallas_call(
        kernel,
        out_shape=out_shape,
        compiler_params=pltpu.CompilerParams(vmem_limit_bytes=VMEM_BYTES),
        cost_estimate=pl.CostEstimate(flops=flops, bytes_accessed=moved, transcendentals=0),
        **kwargs,
    )


GAIN_ONE = slice(0, 896)
BIAS = slice(896, 2048)
GAIN_TWO = slice(2048, 2944)


def place_rows(target, own_ref, other_ref, me, columns=slice(None)):
    rows = own_ref.shape[0]
    target[pl.ds(pl.multiple_of(me * rows, rows), rows), columns] = own_ref[...]
    target[pl.ds(pl.multiple_of((1 - me) * rows, rows), rows), columns] = other_ref[...]


def project_kernel(
    place_ref, x_ref, params_ref, wq_ref, wk_ref, wv_ref, oq_ref, ok_ref, ov_ref, cos_ref, sin_ref,
    n1_ref, q_ref, kv_ref, w_ref,
):
    count = x_ref.shape[0]
    step = 256
    me = place_ref[0]
    width = HQ * HD
    place_rows(w_ref, wq_ref, oq_ref, me, slice(0, width))
    place_rows(w_ref, wk_ref, ok_ref, me, slice(width, width + LANES))
    place_rows(w_ref, wv_ref, ov_ref, me, slice(width + LANES, width + 2 * LANES))

    def body(i, carry):
        rows = pl.ds(pl.multiple_of(i * step, step), step)
        x = x_ref[rows, :].astype(f32)
        scale = lax.rsqrt(jnp.mean(x * x, -1, keepdims=True) + eps_norm)
        normed = (x * scale * params_ref[:, GAIN_ONE]).astype(bf16)
        n1_ref[rows, :] = normed
        cosine = cos_ref[rows, :]
        sine = sin_ref[rows, :]
        out = nn(normed, w_ref[...]) + params_ref[:, BIAS]
        for j in range(PAIRS + 1):
            part = out[:, j * LANES : (j + 1) * LANES]
            part = part * cosine + flip_lanes_half(part) * sine
            if j < PAIRS:
                q_ref[rows, j * LANES : (j + 1) * LANES] = (part * HD**-0.5).astype(bf16)
            else:
                kv_ref[rows, :LANES] = part.astype(bf16)
        kv_ref[rows, LANES:] = out[:, (PAIRS + 1) * LANES :].astype(bf16)
        return carry

    lax.fori_loop(0, count // step, body, 0)


def in_vmem(n):
    return [pl.BlockSpec(memory_space=pltpu.SMEM)] + [pl.BlockSpec(memory_space=pltpu.VMEM)] * n


def project(place, x, params, own, other, cosine, sine):
    count, width = x.shape
    columns = sum(w.shape[1] for w in own)
    return call(
        project_kernel,
        (
            jax.ShapeDtypeStruct((count, width), bf16),
            jax.ShapeDtypeStruct((count, HQ * HD), bf16),
            jax.ShapeDtypeStruct((count, 2 * KVH * HD), bf16),
            jax.ShapeDtypeStruct((width, columns), bf16),
        ),
        2 * count * width * columns,
        6 * 1024 * 1024,
        in_specs=in_vmem(10),
    )(place, x, params, *own, *other, cosine, sine)


def lane_low(shape):
    return lax.broadcasted_iota(jnp.int32, shape, len(shape) - 1) < HD


def spread_heads(source, target, row):
    values = source.astype(f32)
    other = pltpu.roll(values, HD, 1)
    low = lane_low(values.shape)
    rows = pl.ds(row, values.shape[0])
    target[0, 0, rows, :] = jnp.where(low, values, 0.0).astype(bf16)
    target[1, 0, rows, :] = jnp.where(low, 0.0, other).astype(bf16)
    target[0, 1, rows, :] = jnp.where(low, other, 0.0).astype(bf16)
    target[1, 1, rows, :] = jnp.where(low, 0.0, values).astype(bf16)


def turn_heads(source, target, column):
    values = source.astype(f32).T.astype(bf16)
    columns = pl.ds(column, values.shape[1])
    target[0, :, columns] = values[:HD]
    target[1, :, columns] = values[HD:]


def fill_bias(place_ref, seg_ref, near_ref, far_ref, count):
    ctx = place_ref[3]

    def segments(back):
        start = pl.multiple_of(jnp.maximum(ctx - back, 0) * count, count)
        row = seg_ref[:, pl.ds(start, count)].astype(f32)
        row = jnp.where(ctx >= back, row, -1.0)
        return row, jnp.broadcast_to(row, (LANES, count)).T

    own_row, own = segments(0)
    _, one = segments(1)
    _, two = segments(2)
    for t in range(count // LANES):
        columns = slice(t * LANES, (t + 1) * LANES)
        query = own_row[:, columns]
        near_ref[:, columns] = jnp.where(one == query, 0.0, masked_score)
        key = lax.broadcasted_iota(jnp.int32, (count, LANES), 0)
        token = lax.broadcasted_iota(jnp.int32, (count, LANES), 1) + t * LANES
        far = jnp.where(key <= token, own, two)
        far_ref[:, columns] = jnp.where(far == query, 0.0, masked_score)


def triangle():
    key = lax.broadcasted_iota(jnp.int32, (HALF, HALF), 0)
    token = lax.broadcasted_iota(jnp.int32, (HALF, HALF), 1)
    return key <= token


def tiles_of(t, count):
    if t == 0:
        plain = 2 * count + HALF
        plain_bias = HALF
    else:
        plain = 0
        plain_bias = 0
    diagonal = t * HALF
    return plain, plain_bias, diagonal, 2 * count + diagonal


def scores_of(keys, query, t, count, near_ref, far_ref, tri):
    plain, plain_bias, own, old = tiles_of(t, count)
    columns = slice(t * HALF, (t + 1) * HALF)
    near = nt(keys(count, count), query) + near_ref[:, columns]
    far = nt(keys(plain, HALF), query) + far_ref[plain_bias : plain_bias + HALF, columns]
    edge = jnp.where(tri, nt(keys(own, HALF), query), nt(keys(old, HALF), query))
    edge = edge + far_ref[own : own + HALF, columns]
    return near, far, edge


def attend_kernel(
    place_ref, q_ref, kv0_ref, kv1_ref, kv2_ref, seg_ref, o_ref, lse_ref, k_s, vt_s, near_s, far_s
):
    count = q_ref.shape[0]
    pair = pl.program_id(0)

    @pl.when(pair == 0)
    def _():
        for i, ref in enumerate((kv0_ref, kv1_ref, kv2_ref)):
            spread_heads(ref[:, :LANES], k_s, i * count)
            turn_heads(ref[:, LANES:], vt_s, i * count)
        fill_bias(place_ref, seg_ref, near_s, far_s, count)

    tri = triangle()
    for t in range(count // HALF):
        plain, _, own, old = tiles_of(t, count)
        rows = slice(t * HALF, (t + 1) * HALF)
        query = q_ref[rows, :]
        turned = []
        for half in range(2):
            group = (2 * pair + half) // (HQ // KVH)
            near, far, edge = scores_of(
                lambda start, size: k_s[half, group, start : start + size, :],
                query,
                t,
                count,
                near_s,
                far_s,
                tri,
            )
            top = jnp.maximum(
                jnp.max(near, 0, keepdims=True),
                jnp.maximum(jnp.max(far, 0, keepdims=True), jnp.max(edge, 0, keepdims=True)),
            )
            near = jnp.exp(near - top)
            far = jnp.exp(far - top)
            edge = jnp.exp(edge - top)
            total = (
                jnp.sum(near, 0, keepdims=True)
                + jnp.sum(far, 0, keepdims=True)
                + jnp.sum(edge, 0, keepdims=True)
            )
            lse_ref[0, half : half + 1, rows] = top + jnp.log(total)
            mixed = nn(vt_s[group, :, count : 2 * count], near.astype(bf16))
            mixed += nn(vt_s[group, :, plain : plain + HALF], far.astype(bf16))
            mixed += nn(vt_s[group, :, own : own + HALF], jnp.where(tri, edge, 0.0).astype(bf16))
            mixed += nn(vt_s[group, :, old : old + HALF], jnp.where(tri, 0.0, edge).astype(bf16))
            turned.append(mixed * (1.0 / total))
        o_ref[rows, :] = jnp.concatenate(turned, 0).T.astype(bf16)


def attend(place, q, kv0, kv1, kv2, seg):
    count = q.shape[0]
    whole = lambda p: (0, 0)
    return call(
        attend_kernel,
        (
            jax.ShapeDtypeStruct((count, HQ * HD), bf16),
            jax.ShapeDtypeStruct((PAIRS, 8, count), f32),
        ),
        4 * HQ * count * 1280 * 256,
        4 * 1024 * 1024,
        grid=(PAIRS,),
        in_specs=[
            pl.BlockSpec(memory_space=pltpu.SMEM),
            pl.BlockSpec((count, LANES), lambda p: (0, p)),
            pl.BlockSpec(kv0.shape, whole),
            pl.BlockSpec(kv1.shape, whole),
            pl.BlockSpec(kv2.shape, whole),
            pl.BlockSpec(seg.shape, whole),
        ],
        out_specs=(
            pl.BlockSpec((count, LANES), lambda p: (0, p)),
            pl.BlockSpec((1, 8, count), lambda p: (p, 0, 0)),
        ),
        scratch_shapes=[
            pltpu.VMEM((2, KVH, 3 * count, LANES), bf16),
            pltpu.VMEM((KVH, HD, 3 * count), bf16),
            pltpu.VMEM((count, count), f32),
            pltpu.VMEM((count, count), f32),
        ],
    )(place, q, kv0, kv1, kv2, seg)


def attend_back_kernel(*refs, first_pair, first, final):
    (place_ref, q_ref, do_ref, kv0_ref, kv1_ref, kv2_ref, seg_ref, lse_ref, cos_ref, sin_ref) = refs[:10]
    refs = refs[10:]
    if not first:
        dk_in, dv_in = refs[:2]
        refs = refs[2:]
    dq_ref = refs[0]
    refs = refs[1:]
    if final:
        own_ref, one_ref, two_ref = refs[:3]
        refs = refs[3:]
        k_s, v_s, kt_s, near_s, far_s, dk_s, dv_s = refs
    else:
        dk_s, dv_s = refs[:2]
        k_s, v_s, kt_s, near_s, far_s = refs[2:]
    count = q_ref.shape[0]
    step = pl.program_id(0)
    pair = step + first_pair

    @pl.when(step == 0)
    def _():
        for i, ref in enumerate((kv0_ref, kv1_ref, kv2_ref)):
            spread_heads(ref[:, :LANES], k_s, i * count)
            spread_heads(ref[:, LANES:], v_s, i * count)
            turn_heads(ref[:, :LANES], kt_s, i * count)
        fill_bias(place_ref, seg_ref, near_s, far_s, count)
        if first:
            dk_s[...] = jnp.zeros_like(dk_s)
            dv_s[...] = jnp.zeros_like(dv_s)
        else:
            dk_s[...] = dk_in[...]
            dv_s[...] = dv_in[...]

    tri = triangle()
    for t in range(count // HALF):
        plain, _, own, old = tiles_of(t, count)
        rows = slice(t * HALF, (t + 1) * HALF)
        query = q_ref[rows, :]
        grad = do_ref[rows, :]
        low = lane_low(query.shape)
        turned = []
        for half in range(2):
            group = (2 * pair + half) // (HQ // KVH)
            mine = low if half == 0 else jnp.logical_not(low)
            query_half = jnp.where(mine, query.astype(f32), 0.0).astype(bf16)
            grad_half = jnp.where(mine, grad.astype(f32), 0.0).astype(bf16)
            log_total = lse_ref[0, half : half + 1, rows]
            scores = scores_of(
                lambda start, size: k_s[half, group, start : start + size, :],
                query,
                t,
                count,
                near_s,
                far_s,
                tri,
            )
            near, far, edge = (jnp.exp(part - log_total) for part in scores)
            values = lambda start, size: v_s[half, group, start : start + size, :]
            near_p = nt(values(count, count), grad)
            far_p = nt(values(plain, HALF), grad)
            edge_p = jnp.where(tri, nt(values(own, HALF), grad), nt(values(old, HALF), grad))
            inner = (
                jnp.sum(near * near_p, 0, keepdims=True)
                + jnp.sum(far * far_p, 0, keepdims=True)
                + jnp.sum(edge * edge_p, 0, keepdims=True)
            )
            near_g = near * (near_p - inner)
            far_g = far * (far_p - inner)
            edge_g = edge * (edge_p - inner)
            blocks = (
                (count, count, near, near_g),
                (plain, HALF, far, far_g),
                (own, HALF, jnp.where(tri, edge, 0.0), jnp.where(tri, edge_g, 0.0)),
                (old, HALF, jnp.where(tri, 0.0, edge), jnp.where(tri, 0.0, edge_g)),
            )
            total = None
            for start, size, weight, change in blocks:
                change = change.astype(bf16)
                keys = slice(start, start + size)
                dv_s[group, keys, :] += nn(weight.astype(bf16), grad_half)
                dk_s[group, keys, :] += nn(change, query_half)
                part = nn(kt_s[group, :, keys], change)
                total = part if total is None else total + part
            turned.append(total)
        turned = jnp.concatenate(turned, 0).T * HD**-0.5
        back = turned * cos_ref[rows, :] - flip_lanes_half(turned * sin_ref[rows, :])
        dq_ref[rows, :] = back.astype(bf16)

    if final:

        @pl.when(pair == PAIRS - 1)
        def _():
            for i, (ref, cast) in enumerate(((own_ref, f32), (one_ref, bf16), (two_ref, bf16))):
                keys = slice(i * count, (i + 1) * count)
                for j, source in enumerate((dk_s, dv_s)):
                    one = source[0, keys, :]
                    two = source[1, keys, :]
                    one = one + pltpu.roll(one, HD, 1)
                    two = two + pltpu.roll(two, HD, 1)
                    both = jnp.where(lane_low(one.shape), one, two)
                    ref[:, j * LANES : (j + 1) * LANES] = both.astype(cast)


def attend_back(place, q, do, kv0, kv1, kv2, seg, lse, cosine, sine, sums, *, first_pair, pairs):
    count = q.shape[0]
    first = sums is None
    final = first_pair + pairs == PAIRS
    sums = () if first else tuple(sums)
    whole = lambda p: (0, 0)
    stacked = pl.BlockSpec((KVH, 3 * count, LANES), lambda p: (0, 0, 0))
    lane_block = pl.BlockSpec((count, LANES), lambda p: (0, p + first_pair))
    row_block = pl.BlockSpec((1, 8, count), lambda p: (p + first_pair, 0, 0))
    token_block = pl.BlockSpec((count, 2 * LANES), whole)
    stack = jax.ShapeDtypeStruct((KVH, 3 * count, LANES), f32)
    if final:
        outs = [jax.ShapeDtypeStruct((count, 2 * LANES), t) for t in (f32, bf16, bf16)]
        out_specs = [token_block] * 3
        scratch = [pltpu.VMEM(stack.shape, f32)] * 2
    else:
        outs = [stack, stack]
        out_specs = [stacked] * 2
        scratch = []
    return call(
        functools.partial(attend_back_kernel, first_pair=first_pair, first=first, final=final),
        (jax.ShapeDtypeStruct((count, pairs * LANES), bf16), *outs),
        10 * 2 * pairs * count * 1280 * 256,
        6 * 1024 * 1024,
        grid=(pairs,),
        in_specs=[
            pl.BlockSpec(memory_space=pltpu.SMEM),
            lane_block,
            lane_block,
            pl.BlockSpec(kv0.shape, whole),
            pl.BlockSpec(kv1.shape, whole),
            pl.BlockSpec(kv2.shape, whole),
            pl.BlockSpec(seg.shape, whole),
            row_block,
            pl.BlockSpec(cosine.shape, whole),
            pl.BlockSpec(sine.shape, whole),
        ]
        + [stacked] * len(sums),
        out_specs=(pl.BlockSpec((count, LANES), lambda p: (0, p)), *out_specs),
        scratch_shapes=[
            pltpu.VMEM((2, KVH, 3 * count, LANES), bf16),
            pltpu.VMEM((2, KVH, 3 * count, LANES), bf16),
            pltpu.VMEM((KVH, HD, 3 * count), bf16),
            pltpu.VMEM((count, count), f32),
            pltpu.VMEM((count, count), f32),
        ]
        + scratch,
    )(place, q, do, kv0, kv1, kv2, seg, lse, cosine, sine, *sums)


def merge_kernel(place_ref, x_ref, o_ref, own_ref, other_ref, params_ref, h1_ref, n2_ref, w_ref):
    step = 256
    place_rows(w_ref, own_ref, other_ref, place_ref[0])

    def body(i, carry):
        rows = pl.ds(pl.multiple_of(i * step, step), step)
        hidden = x_ref[rows, :].astype(f32) + nn(o_ref[rows, :], w_ref[...])
        h1_ref[rows, :] = hidden
        scale = lax.rsqrt(jnp.mean(hidden * hidden, -1, keepdims=True) + eps_norm)
        n2_ref[rows, :] = (hidden * scale * params_ref[:, GAIN_TWO]).astype(bf16)
        return carry

    lax.fori_loop(0, x_ref.shape[0] // step, body, 0)


def merge(place, x, o, own, other, params):
    return call(
        merge_kernel,
        (
            jax.ShapeDtypeStruct(x.shape, f32),
            jax.ShapeDtypeStruct(x.shape, bf16),
            jax.ShapeDtypeStruct((2 * own.shape[0], own.shape[1]), bf16),
        ),
        4 * x.shape[0] * own.shape[0] * own.shape[1],
        6 * 1024 * 1024,
        in_specs=in_vmem(5),
    )(place, x, o, own, other, params)


def change_kernel(ca_ref, cb_ref, down_ref, out_ref):
    count = ca_ref.shape[0]
    out_ref[:count, :] = nt(ca_ref[...], down_ref[...]).astype(bf16)
    out_ref[count:, :] = nt(cb_ref[...], down_ref[...]).astype(bf16)


def change(ca, cb, down):
    count, features = ca.shape
    hidden = down.shape[0]
    block = 2 * LANES
    steps = pl.cdiv(hidden, block)
    whole = pl.BlockSpec((count, features), lambda i: (0, 0))
    return call(
        change_kernel,
        jax.ShapeDtypeStruct((2 * count, hidden), bf16),
        4 * count * features * hidden,
        12 * 1024 * 1024,
        grid=(steps,),
        in_specs=[whole, whole, pl.BlockSpec((block, features), lambda i: (i, 0))],
        out_specs=pl.BlockSpec((2 * count, block), lambda i: (0, i)),
    )(ca, cb, down)


def feed_kernel(*refs, start, first, sides):
    place_ref, na_ref, nb_ref, ca_ref, cb_ref, gate_ref, gate_o_ref, up_ref, up_o_ref, down_ref, change_ref = refs[:11]
    refs = refs[11:]
    if not first:
        sums = refs[:4]
        refs = refs[4:]
    grad_refs = refs[:6]
    outs = refs[6:10]
    refs = refs[10:]
    (n_s, c_s, wg, wu, wd, change_s, inner_s, gate_s, up_s, *part_s) = refs[:12]
    refs = refs[12:]
    if not first:
        held = refs[:2]
        refs = refs[2:]
    totals = refs[:2]
    in_sem, sum_sem, out_sem = refs[2:]
    tokens, features = n_s.shape
    count = tokens // 2
    width = wg.shape[1]
    rows_held = gate_ref.shape[0]
    hidden = down_ref.shape[0]
    me = place_ref[0]
    lanes = pl.ds(pl.multiple_of(me * hidden + start, LANES), width)
    own_rows = pl.ds(pl.multiple_of(me * rows_held, rows_held), rows_held)
    other_rows = pl.ds(pl.multiple_of((1 - me) * rows_held, rows_held), rows_held)
    low, high = pl.ds(0, count), pl.ds(count, count)

    moves = [
        (na_ref, n_s.at[low, :]),
        (nb_ref, n_s.at[high, :]),
        (gate_ref.at[:, lanes], wg.at[own_rows, :]),
        (gate_o_ref.at[:, lanes], wg.at[other_rows, :]),
        (up_ref.at[:, lanes], wu.at[own_rows, :]),
        (up_o_ref.at[:, lanes], wu.at[other_rows, :]),
        (change_ref.at[:, pl.ds(start, width)], change_s),
        (down_ref.at[pl.ds(start, width), :], wd),
        (ca_ref, c_s.at[low, :]),
        (cb_ref, c_s.at[high, :]),
    ]
    copies = [pltpu.make_async_copy(a, b, in_sem.at[i]) for i, (a, b) in enumerate(moves)]
    for copy in copies:
        copy.start()
    sum_copies = []
    if not first:
        places = ((held[0], low), (held[1], low), (held[0], high), (held[1], high))
        sum_copies = [
            pltpu.make_async_copy(sums[i], target.at[rows, :], sum_sem.at[i])
            for i, (target, rows) in enumerate(places)
        ]
        for copy in sum_copies:
            copy.start()
    for copy in copies[:8] + sum_copies:
        copy.wait()
    step = 256

    def body(i, carry):
        rows = pl.ds(pl.multiple_of(i * step, step), step)
        normed = n_s[rows, :]
        gate = nn(normed, wg[...])
        up = nn(normed, wu[...])
        change = change_s[rows, :].astype(f32)
        sigmoid = 1.0 / (1.0 + jnp.exp(-gate))
        activated = gate * sigmoid
        inner = (activated * up).astype(bf16)
        gate_g = (change * up * sigmoid * (1.0 + gate * (1.0 - sigmoid))).astype(bf16)
        up_g = (change * activated).astype(bf16)
        inner_s[rows, :] = inner
        gate_s[rows, :] = gate_g
        up_s[rows, :] = up_g
        result = nn(inner, wd[...])
        back = nt(gate_g, wg[...]) + nt(up_g, wu[...])
        if not first:
            result = result + held[0][rows, :].astype(f32)
            back = back + held[1][rows, :].astype(f32)
        totals[0][rows, :] = result.astype(bf16)
        totals[1][rows, :] = back.astype(bf16)
        return carry

    lax.fori_loop(0, tokens // step, body, 0)
    for copy in copies[8:]:
        copy.wait()
    leaving = []

    def leave(source, target):
        copy = pltpu.make_async_copy(source, target, out_sem.at[len(leaving)])
        copy.start()
        leaving.append(copy)

    for i, (total, rows) in enumerate(
        ((totals[0], low), (totals[1], low), (totals[0], high), (totals[1], high))
    ):
        leave(total.at[rows, :], outs[i])

    def part_leaves(i):
        keep, send = grad_refs[2 * i : 2 * i + 2]
        rows = part_s[i].shape[0] // 2
        side = place_ref[sides[i]]
        leave(part_s[i].at[pl.ds(pl.multiple_of((1 - side) * rows, 16), rows), :], send)
        leave(part_s[i].at[pl.ds(pl.multiple_of(side * rows, 16), rows), :], keep)

    mine_s, theirs_s, down_s = part_s

    def tiles_loop(body):
        def step(i, carry):
            body(i * HALF, HALF)
            return carry

        lax.fori_loop(0, width // HALF, step, 0)
        if width % HALF:
            body(width // HALF * HALF, width % HALF)

    def columns_of(at, size):
        return pl.ds(at if isinstance(at, int) else pl.multiple_of(at, HALF), size)

    def wide_grads(at, size):
        for kind, source in enumerate((gate_s, up_s)):
            grads = tn(n_s[...], source[:, columns_of(at, size)]).astype(bf16)
            for j in range(size // LANES):
                row = (kind * width // LANES + at // LANES + j) * rows_held
                rows = pl.ds(row if isinstance(row, int) else pl.multiple_of(row, 16), rows_held)
                tile = grads[:, j * LANES : (j + 1) * LANES]

                @pl.when(me == 0)
                def _():
                    mine_s[rows, :] = tile[:rows_held]
                    theirs_s[rows, :] = tile[rows_held:]

                @pl.when(me == 1)
                def _():
                    mine_s[rows, :] = tile[rows_held:]
                    theirs_s[rows, :] = tile[:rows_held]

    def down_grads(at, size):
        grads = tn(inner_s[:, columns_of(at, size)], c_s[...]).astype(bf16)
        for j in range(features // LANES):
            row = j * width + at
            rows = pl.ds(row if isinstance(row, int) else pl.multiple_of(row, 16), size)
            down_s[rows, :] = grads[:, j * LANES : (j + 1) * LANES]

    tiles_loop(wide_grads)
    part_leaves(0)
    part_leaves(1)
    tiles_loop(down_grads)
    part_leaves(2)
    for copy in leaving:
        copy.wait()


def feed(place, na, nb, ca, cb, gate, gate_o, up, up_o, down, change, sums, *, start, width, sides):
    count, features = na.shape
    first = sums is None
    sums = () if first else tuple(sums)
    anywhere = pl.BlockSpec(memory_space=pl.ANY)
    rows = features * width // LANES
    tokens = (2 * count, features)
    outs = [jax.ShapeDtypeStruct((rows // 2, LANES), bf16)] * 6
    outs += [jax.ShapeDtypeStruct((count, features), bf16)] * 4
    scratch = [pltpu.VMEM(tokens, bf16)] * 2
    scratch += [pltpu.VMEM((features, width), bf16)] * 2 + [pltpu.VMEM((width, features), bf16)]
    scratch += [pltpu.VMEM((2 * count, width), bf16)] * 4
    scratch += [pltpu.VMEM((rows, LANES), bf16)] * 3
    scratch += [pltpu.VMEM(tokens, bf16)] * (2 if first else 4)
    scratch += [pltpu.SemaphoreType.DMA((n,)) for n in (10, 4, 10)]
    return call(
        functools.partial(feed_kernel, start=start, first=first, sides=sides),
        tuple(outs),
        18 * 2 * count * features * width,
        30 * 1024 * 1024,
        in_specs=[pl.BlockSpec(memory_space=pltpu.SMEM)] + [anywhere] * (10 + len(sums)),
        out_specs=(anywhere,) * 10,
        scratch_shapes=scratch,
    )(place, na, nb, ca, cb, gate, gate_o, up, up_o, down, change, *sums)


def middle_kernel(
    place_ref, part_ref, got_ref, h1_ref, dy_ref, params_ref, w_ref, o_ref,
    dh1_ref, do_ref, gg_ref, mine_ref, theirs_ref, low_s,
):
    count, features = part_ref.shape
    step = 256
    gg_ref[...] = jnp.zeros_like(gg_ref)

    def body(i, carry):
        rows = pl.ds(pl.multiple_of(i * step, step), step)
        back = part_ref[rows, :].astype(f32) + got_ref[rows, :].astype(f32)
        hidden = h1_ref[rows, :]
        scale = lax.rsqrt(jnp.mean(hidden * hidden, -1, keepdims=True) + eps_norm)
        normal = hidden * scale
        gg_ref[...] += jnp.sum(back * normal, 0, keepdims=True)
        change = back * params_ref[:, GAIN_TWO]
        grad = dy_ref[rows, :].astype(f32) + scale * (
            change - normal * jnp.mean(change * normal, -1, keepdims=True)
        )
        dh1_ref[rows, :] = grad
        low = grad.astype(bf16)
        low_s[rows, :] = low
        do_ref[rows, :] = nt(low, w_ref[...]).astype(bf16)
        return carry

    lax.fori_loop(0, count // step, body, 0)
    store_split(place_ref, tn(o_ref[...], low_s[...]).astype(bf16), mine_ref, theirs_ref, 0)


def store_split(place_ref, grads, mine_ref, theirs_ref, first_tile):
    half_rows = grads.shape[0] // 2
    me = place_ref[0]
    for j in range(grads.shape[1] // LANES):
        row = (first_tile + j) * half_rows
        tile = grads[:, j * LANES : (j + 1) * LANES]

        @pl.when(me == 0)
        def _():
            mine_ref[row : row + half_rows, :] = tile[:half_rows]
            theirs_ref[row : row + half_rows, :] = tile[half_rows:]

        @pl.when(me == 1)
        def _():
            mine_ref[row : row + half_rows, :] = tile[half_rows:]
            theirs_ref[row : row + half_rows, :] = tile[:half_rows]


def middle(place, part, got, h1, dy, params, w, o):
    count, features = part.shape
    rows = (features // 2) * (features // LANES)
    return call(
        middle_kernel,
        (
            jax.ShapeDtypeStruct((count, features), f32),
            jax.ShapeDtypeStruct((count, HQ * HD), bf16),
            jax.ShapeDtypeStruct((1, features), f32),
            jax.ShapeDtypeStruct((rows, LANES), bf16),
            jax.ShapeDtypeStruct((rows, LANES), bf16),
        ),
        4 * count * features * features,
        12 * 1024 * 1024,
        in_specs=in_vmem(7),
        scratch_shapes=[pltpu.VMEM((count, features), bf16)],
    )(place, part, got, h1, dy, params, w, o)


def query_kernel(
    place_ref, dqa_ref, dqb_ref, n1_ref, w_ref, back_ref, gb_ref, mine_ref, theirs_ref, dp_s
):
    count = n1_ref.shape[0]
    width = HQ * HD
    split_at = dqa_ref.shape[1]
    step = 256
    gb_ref[...] = jnp.zeros_like(gb_ref)

    def body(i, carry):
        rows = pl.ds(pl.multiple_of(i * step, step), step)
        dp_s[rows, :split_at] = dqa_ref[rows, :]
        dp_s[rows, split_at:] = dqb_ref[rows, :]
        grads = dp_s[rows, :]
        gb_ref[...] += jnp.sum(grads.astype(f32), 0, keepdims=True)
        back_ref[rows, :] = nt(grads, w_ref[:, :width])
        return carry

    lax.fori_loop(0, count // step, body, 0)
    store_split(place_ref, tn(n1_ref[...], dp_s[...]).astype(bf16), mine_ref, theirs_ref, 0)


def query_back(place, dqa, dqb, n1, w):
    count, features = n1.shape
    width = HQ * HD
    rows = (features // 2) * (width // LANES)
    return call(
        query_kernel,
        (
            jax.ShapeDtypeStruct((count, features), f32),
            jax.ShapeDtypeStruct((1, width), f32),
            jax.ShapeDtypeStruct((rows, LANES), bf16),
            jax.ShapeDtypeStruct((rows, LANES), bf16),
        ),
        4 * count * features * width,
        10 * 1024 * 1024,
        in_specs=in_vmem(4),
        scratch_shapes=[pltpu.VMEM((count, width), bf16)],
    )(place, dqa, dqb, n1, w)


VECTOR_ROWS = 128


def last_kernel(
    place_ref, own_ref, one_ref, two_ref, n1_ref, x_ref, params_ref, w_ref, part_ref, dh1_ref, cos_ref, sin_ref,
    qm_ref, qt_ref, om_ref, ot_ref, gbq_ref, ggt_ref, dx_ref, mine_ref, theirs_ref, dp_s, gg_ref, gb_ref,
):
    count = n1_ref.shape[0]
    width = HQ * HD
    step = 256
    gg_ref[...] = jnp.zeros_like(gg_ref)
    gb_ref[...] = jnp.zeros_like(gb_ref)

    def body(i, carry):
        rows = pl.ds(pl.multiple_of(i * step, step), step)
        pairs = own_ref[rows, :] + one_ref[rows, :].astype(f32) + two_ref[rows, :].astype(f32)
        key = pairs[:, :LANES]
        key = key * cos_ref[rows, :] - flip_lanes_half(key * sin_ref[rows, :])
        dp_s[rows, :LANES] = key.astype(bf16)
        dp_s[rows, LANES:] = pairs[:, LANES:].astype(bf16)
        grads = dp_s[rows, :]
        gb_ref[...] += jnp.sum(grads.astype(f32), 0, keepdims=True)
        back = part_ref[rows, :] + nt(grads, w_ref[:, width:])
        x = x_ref[rows, :].astype(f32)
        scale = lax.rsqrt(jnp.mean(x * x, -1, keepdims=True) + eps_norm)
        normal = x * scale
        gg_ref[...] += jnp.sum(back * normal, 0, keepdims=True)
        change = back * params_ref[:, GAIN_ONE]
        grad = dh1_ref[rows, :] + scale * (
            change - normal * jnp.mean(change * normal, -1, keepdims=True)
        )
        dx_ref[rows, :] = grad.astype(bf16)
        return carry

    lax.fori_loop(0, count // step, body, 0)
    at = qm_ref.shape[0]
    tiles = (w_ref.shape[1] - width) // LANES
    rows_held = at * LANES // width
    store_split(
        place_ref, tn(n1_ref[...], dp_s[...]).astype(bf16), mine_ref, theirs_ref, at // rows_held
    )
    mine_ref[:at, :] = qm_ref[...]
    theirs_ref[:at, :] = qt_ref[...]
    at += tiles * rows_held
    after = at + om_ref.shape[0]
    mine_ref[at:after, :] = om_ref[...]
    theirs_ref[at:after, :] = ot_ref[...]
    vectors = []
    for ref in (gg_ref, gbq_ref, gb_ref, ggt_ref):
        vectors += [ref[:, j * LANES : (j + 1) * LANES] for j in range(ref.shape[1] // LANES)]
    vectors.append(jnp.zeros((VECTOR_ROWS - len(vectors), LANES), f32))
    vectors = jnp.concatenate(vectors, 0).astype(bf16)
    mine_ref[after:, :] = vectors
    theirs_ref[after:, :] = vectors


def last(place, own, one, two, n1, x, params, w, part, dh1, cosine, sine, qm, qt, om, ot, gbq, ggt):
    count, features = n1.shape
    columns = w.shape[1] - HQ * HD
    rows = (features // 2) * (columns // LANES) + qm.shape[0] + om.shape[0] + VECTOR_ROWS
    return call(
        last_kernel,
        (
            jax.ShapeDtypeStruct((count, features), bf16),
            jax.ShapeDtypeStruct((rows, LANES), bf16),
            jax.ShapeDtypeStruct((rows, LANES), bf16),
        ),
        4 * count * features * columns,
        14 * 1024 * 1024,
        in_specs=in_vmem(17),
        scratch_shapes=[
            pltpu.VMEM((count, columns), bf16),
            pltpu.VMEM((1, features), f32),
            pltpu.VMEM((1, columns), f32),
        ],
    )(place, own, one, two, n1, x, params, w, part, dh1, cosine, sine, qm, qt, om, ot, gbq, ggt)


def swap(values):
    return lax.ppermute(values, "fsdp", [(0, 1), (1, 0)])


def flip(values, dim):
    axis, bit = dim
    size = lax.axis_size(axis)
    return lax.ppermute(values, axis, [(i, i ^ (1 << bit)) for i in range(size)])


def side(dim):
    axis, bit = dim
    return (lax.axis_index(axis) >> bit) & 1


def add(*terms):
    total = terms[0].astype(f32)
    for term in terms[1:]:
        total = total + term.astype(f32)
    return total.astype(bf16)


def take(array, index):
    return lax.dynamic_index_in_dim(array, index, 0, False)


def join(low, other, index):
    out = jnp.zeros((2,) + low.shape, low.dtype)
    out = lax.dynamic_update_index_in_dim(out, low, index, 0)
    return lax.dynamic_update_index_in_dim(out, other, 1 - index, 0)


def rest_of_seq(values):
    for bit in range(2, lax.axis_size("seq").bit_length() - 1):
        values = add(values, flip(values, ("seq", bit)))
    return values


class Order:
    def __init__(self):
        self.token = None

    def __call__(self, step, *operands):
        if self.token is not None:
            operands, _ = lax.optimization_barrier((operands, self.token))
        out = step(*operands)
        self.token = jax.tree.leaves(out)[0]
        return out


def fold_kernel(place_ref, *refs, sides):
    n = 2 * len(sides)
    for i, number in enumerate(sides):
        kept, got = refs[2 * i : 2 * i + 2]
        keep, send = refs[n + 2 * i : n + 2 * i + 2]
        rows = keep.shape[0]
        side = place_ref[number]
        for target, at in ((keep, side), (send, 1 - side)):
            at = pl.ds(pl.multiple_of(at * rows, 16), rows)
            target[...] = (kept[at, :].astype(f32) + got[at, :].astype(f32)).astype(bf16)


def flatten(pairs):
    return [array for pair in pairs for array in pair]


def fold(place, pairs, sides):
    rows = [kept.shape[0] // 2 for kept, _ in pairs]
    outs = call(
        functools.partial(fold_kernel, sides=sides),
        tuple(jax.ShapeDtypeStruct((n, LANES), bf16) for n in rows for _ in range(2)),
        4 * sum(rows) * LANES,
        12 * sum(rows) * LANES,
        in_specs=in_vmem(2 * len(pairs)),
    )(place, *flatten(pairs))
    return list(zip(outs[::2], outs[1::2]))


def stack_kernel(*refs):
    total = refs[-1]
    at = 0
    for kept, got in zip(refs[:-1:2], refs[1:-1:2]):
        rows = kept.shape[0]
        total[at : at + rows, :] = (kept[...].astype(f32) + got[...].astype(f32)).astype(bf16)
        at += rows


def stack(pairs):
    rows = sum(kept.shape[0] for kept, _ in pairs)
    return call(
        stack_kernel, jax.ShapeDtypeStruct((rows, LANES), bf16), rows * LANES, 6 * rows * LANES
    )(*flatten(pairs))


def sum_kernel(*refs):
    n = 2 * len(refs) // 3
    for kept, got, total in zip(refs[:n:2], refs[1:n:2], refs[n:]):
        total[...] = (kept[...].astype(f32) + got[...].astype(f32)).astype(bf16)


def sum_parts(pairs):
    rows = [kept.shape[0] for kept, _ in pairs]
    return call(
        sum_kernel,
        tuple(jax.ShapeDtypeStruct((n, LANES), bf16) for n in rows),
        sum(rows) * LANES,
        6 * sum(rows) * LANES,
    )(*flatten(pairs))


def unstack_kernel(total, got, *parts):
    at = 0
    for part in parts:
        rows = part.shape[0]
        both = total[at : at + rows, :].astype(f32) + got[at : at + rows, :].astype(f32)
        part[...] = both.astype(bf16)
        at += rows


def unstack(total, got, sizes):
    return call(
        unstack_kernel,
        tuple(jax.ShapeDtypeStruct((n, LANES), bf16) for n in sizes),
        total.shape[0] * LANES,
        6 * total.shape[0] * LANES,
    )(total, got)


def join_kernel(place_ref, *refs, sides):
    for i, number in enumerate(sides):
        own, got = refs[2 * i : 2 * i + 2]
        both = refs[2 * len(sides) + i]
        rows = own.shape[0]
        side = place_ref[number]
        both[pl.ds(pl.multiple_of(side * rows, 16), rows), :] = own[...]
        both[pl.ds(pl.multiple_of((1 - side) * rows, 16), rows), :] = got[...]


def join_parts(place, pairs, sides):
    rows = [own.shape[0] for own, _ in pairs]
    return call(
        functools.partial(join_kernel, sides=sides),
        tuple(jax.ShapeDtypeStruct((2 * n, LANES), bf16) for n in rows),
        1,
        8 * sum(rows) * LANES,
        in_specs=in_vmem(2 * len(pairs)),
    )(place, *flatten(pairs))


def bring_halves(place_ref, refs, sides, targets, in_sem):
    copies = []
    for i, number in enumerate(sides):
        side = place_ref[number]
        rows = targets[i].shape[0] // 2
        for ref, at in ((refs[2 * i], side), (refs[2 * i + 1], 1 - side)):
            at = pl.ds(pl.multiple_of(at * rows, 16), rows)
            copy = pltpu.make_async_copy(ref, targets[i].at[at, :], in_sem.at[len(copies)])
            copy.start()
            copies.append(copy)
    for copy in copies:
        copy.wait()


def untile_kernel(*refs, start, width, first, sides, n_parts):
    place_ref = refs[0]
    parts = refs[1 : 1 + n_parts]
    refs = refs[1 + n_parts + (0 if first else 3) :]
    gate_ref, up_ref, down_ref, mine_s, theirs_s, downs_s, wide_s, down_s, in_sem, out_sem = refs
    me = place_ref[0]
    features = down_ref.shape[1]
    hidden = down_ref.shape[0]
    rows_held = gate_ref.shape[0]
    targets = (mine_s, theirs_s, downs_s)
    bring_halves(place_ref, parts, sides, targets, in_sem)
    leaving = []

    def leave(source, target):
        copy = pltpu.make_async_copy(source, target, out_sem.at[len(leaving)])
        copy.start()
        leaving.append(copy)

    tiles = width // LANES
    for i, (source, owner) in enumerate(((mine_s, me), (theirs_s, 1 - me))):
        lanes = pl.ds(pl.multiple_of(owner * hidden + start, LANES), width)
        for kind, target in enumerate((gate_ref, up_ref)):
            wide = wide_s.at[2 * i + kind]
            for j in range(tiles):
                row = (kind * tiles + j) * rows_held
                wide[:, j * LANES : (j + 1) * LANES] = source[row : row + rows_held, :].astype(f32)
            leave(wide, target.at[:, lanes])
    for j in range(features // LANES):
        row = j * width
        down_s[:, j * LANES : (j + 1) * LANES] = downs_s[row : row + width, :].astype(f32)
    leave(down_s, down_ref.at[pl.ds(start, width), :])
    for copy in leaving:
        copy.wait()


def untile(place, parts, outs, *, start, width, features, hidden, sides):
    first = outs is None
    rows_held = features // 2
    rows = features * width // LANES
    anywhere = pl.BlockSpec(memory_space=pl.ANY)
    outs = () if first else tuple(outs)
    n_parts = len(parts)
    return call(
        functools.partial(
            untile_kernel, start=start, width=width, first=first, sides=sides, n_parts=n_parts
        ),
        (
            jax.ShapeDtypeStruct((rows_held, 2 * hidden), f32),
            jax.ShapeDtypeStruct((rows_held, 2 * hidden), f32),
            jax.ShapeDtypeStruct((hidden, features), f32),
        ),
        3 * features * width,
        3 * features * width * 6,
        in_specs=[pl.BlockSpec(memory_space=pltpu.SMEM)] + [anywhere] * (n_parts + len(outs)),
        out_specs=(anywhere,) * 3,
        scratch_shapes=[pltpu.VMEM((rows, LANES), bf16)] * 3
        + [
            pltpu.VMEM((4, rows_held, width), f32),
            pltpu.VMEM((width, features), f32),
            pltpu.SemaphoreType.DMA((6,)),
            pltpu.SemaphoreType.DMA((5,)),
        ],
        input_output_aliases={} if first else {1 + n_parts + i: i for i in range(3)},
    )(place, *parts, *outs)


def split_kernel(place_ref, mine_ref, theirs_ref, *refs, sides):
    base = 0
    for i, number in enumerate(sides):
        side = place_ref[number]
        rows = refs[2 * i].shape[0]
        for target, at in zip(refs[2 * i : 2 * i + 2], (side, 1 - side)):
            at = pl.ds(pl.multiple_of(base + at * rows, 16), rows)
            target[...] = (mine_ref[at, :].astype(f32) + theirs_ref[at, :].astype(f32)).astype(bf16)
        base += 2 * rows


def split(place, mine, theirs, *, sides):
    rows = mine.shape[0] // (2 * len(sides))
    outs = call(
        functools.partial(split_kernel, sides=sides),
        (jax.ShapeDtypeStruct((rows, LANES), bf16),) * (2 * len(sides)),
        mine.shape[0] * LANES,
        6 * mine.shape[0] * LANES,
        in_specs=in_vmem(2),
    )(place, mine, theirs)
    return list(zip(outs[::2], outs[1::2]))


def untile_flat_kernel(*refs, sides):
    place_ref = refs[0]
    parts = refs[1 : 1 + 2 * len(sides)]
    *targets, vector_ref, flat_s, in_sem = refs[1 + 2 * len(sides) :]
    rows = flat_s.shape[0] // len(sides)
    halves = [flat_s.at[pl.ds(i * rows, rows), :] for i in range(len(sides))]
    bring_halves(place_ref, parts, sides, halves, in_sem)
    rows_held = targets[0].shape[0]
    row = 0
    for target in targets:
        for j in range(target.shape[1] // LANES):
            target[:, j * LANES : (j + 1) * LANES] = flat_s[row : row + rows_held, :].astype(f32)
            row += rows_held
    vector_ref[...] = flat_s[row:, :].astype(f32)


def untile_flat(place, parts, *, rows_held, widths, sides):
    rows = rows_held * sum(widths) // LANES + VECTOR_ROWS
    anywhere = pl.BlockSpec(memory_space=pl.ANY)
    return call(
        functools.partial(untile_flat_kernel, sides=sides),
        (
            *(jax.ShapeDtypeStruct((rows_held, width), f32) for width in widths),
            jax.ShapeDtypeStruct((VECTOR_ROWS, LANES), f32),
        ),
        rows * LANES,
        rows * LANES * 6,
        in_specs=[pl.BlockSpec(memory_space=pltpu.SMEM)] + [anywhere] * len(parts),
        out_specs=(pl.BlockSpec(memory_space=pltpu.VMEM),) * (len(widths) + 1),
        scratch_shapes=[
            pltpu.VMEM((rows, LANES), bf16), pltpu.SemaphoreType.DMA((2 * len(sides),))
        ],
    )(place, *parts)


class FlatSum:
    def __init__(self, place, order):
        self.place, self.order = place, order
        self.links, self.sides = ((X, Y), (Y, X)), ((1, 2), (2, 1))

    def over(self, arrays, level):
        return [flip(array, link) for array, link in zip(arrays, self.links[level])]

    def leave(self, mine, theirs):
        pairs = self.order(functools.partial(split, sides=self.sides[0]), self.place, mine, theirs)
        kept, sent = zip(*pairs)
        self.held = list(zip(kept, self.over(sent, 0)))

    def halve(self):
        pairs = self.order(lambda pairs: fold(self.place, pairs, self.sides[1]), self.held)
        kept, sent = zip(*pairs)
        self.held = list(zip(kept, self.over(sent, 1)))

    def sum(self):
        total = rest_of_seq(self.order(stack, self.held))
        self.total = total, flip(total, Z)

    def across(self):
        total = self.order(add, *self.total)
        for bit in range(2, lax.axis_size("ctx").bit_length() - 1):
            total = add(total, flip(total, ("ctx", bit)))
        self.total = total, flip(total, FAR)

    def turn(self):
        total, got = self.total
        sizes = (total.shape[0] // 2,) * 2
        own = self.order(lambda total, got: unstack(total, got, sizes), total, got)
        self.held = list(zip(own, self.over(own, 1)))

    def join(self):
        own = self.order(lambda pairs: join_parts(self.place, pairs, self.sides[1]), self.held)
        self.held = list(zip(own, self.over(own, 0)))


class LinkSum:
    def __init__(self, place, order):
        self.place, self.order = place, order
        links, numbers = (X, Y, Z), (1, 2, 4)
        self.links = [[links[(i + j) % 3] for i in range(3)] for j in range(3)]
        self.sides = [tuple(numbers[(i + j) % 3] for i in range(3)) for j in range(3)]

    def over(self, arrays, level):
        return [flip(array, link) for array, link in zip(arrays, self.links[level])]

    def leave(self, pairs):
        kept, sent = zip(*pairs)
        self.held = list(zip(kept, self.over(sent, 0)))

    def halve(self, level):
        pairs = self.order(lambda pairs: fold(self.place, pairs, self.sides[level]), self.held)
        kept, sent = zip(*pairs)
        self.held = list(zip(kept, self.over(sent, level)))

    def rest_of_axes(self, total):
        total = rest_of_seq(total)
        for bit in range(2, lax.axis_size("ctx").bit_length() - 1):
            total = add(total, flip(total, ("ctx", bit)))
        return total

    def across(self):
        self.sizes = [kept.shape[0] for kept, _ in self.held]
        total = self.rest_of_axes(self.order(stack, self.held))
        self.total = total, flip(total, FAR)

    def turn(self):
        own = list(self.order(lambda total, got: unstack(total, got, self.sizes), *self.total))
        own[1] = swap(own[1])
        self.held = list(zip(own, self.over(own, 2)))

    def across_each(self):
        totals = [self.rest_of_axes(total) for total in self.order(sum_parts, self.held)]
        self.held = [(total, flip(total, FAR)) for total in totals]

    def turn_each(self, i):
        own = self.order(add, *self.held[i])
        if i == 1:
            own = swap(own)
        self.held[i] = own, flip(own, self.links[2][i])

    def join(self, level):
        own = self.order(lambda pairs: join_parts(self.place, pairs, self.sides[level]), self.held)
        self.held = list(zip(own, self.over(own, level - 1)))

    @property
    def parts(self):
        return flatten(self.held)


X, Y, Z, FAR = ("seq", 0), ("seq", 1), ("ctx", 0), ("ctx", 1)


def on_device(
    block_input,
    segment_ids,
    out_cotangent,
    input_gain,
    query_weight,
    query_bias,
    key_weight,
    key_bias,
    value_weight,
    value_bias,
    output_weight,
    middle_gain,
    gate_weight,
    up_weight,
    down_weight,
):
    me = lax.axis_index("fsdp")
    ctx = lax.axis_index("ctx")
    chunks = lax.axis_size("ctx")
    place = jnp.stack([me, side(X), side(Y), ctx, side(Z)]).astype(jnp.int32)
    x = block_input[0]
    dy = out_cotangent[0]
    count, features = x.shape
    hidden = down_weight.shape[0]
    kv_width = KVH * HD

    own = (query_weight, key_weight, value_weight)
    other = tuple(swap(w) for w in own)
    vectors = (input_gain, query_bias, key_bias, value_bias, middle_gain)
    mine = jnp.concatenate(vectors)
    theirs = swap(mine)
    low = jnp.where(me == 0, mine, theirs).astype(f32)
    high = jnp.where(me == 0, theirs, mine).astype(f32)
    params = []
    at = 0
    for vector in vectors:
        size = vector.shape[0]
        params += [low[at : at + size], high[at : at + size]]
        at += size
    params = jnp.concatenate(params)[None]

    first = ctx * count
    positions = (first + jnp.arange(count, dtype=jnp.int32)).astype(f32)
    inverse = theta_base ** (-jnp.arange(0, HD, 2, dtype=f32) / HD)
    angle = positions[:, None] * jnp.tile(inverse, LANES // inverse.shape[0])[None, :]
    cosine, sine = jnp.cos(angle), jnp.sin(angle)

    n1, q, kv, w_in = project(place, x, params, own, other, cosine, sine)
    out_other = swap(output_weight)
    gate_other, up_other = swap(gate_weight), swap(up_weight)
    dy_other = swap(dy)

    reach = WINDOW // count
    before = [
        lax.ppermute(kv, "ctx", [(i, i + d) for i in range(chunks - d)])
        for d in range(1, reach + 1)
    ]
    order = Order()
    changes = order(change, dy, dy_other, down_weight)
    o, lse = order(attend, place, q, kv, *before, segment_ids)
    h1, n2, w_out = merge(place, x, o, output_weight, out_other, params)
    n2_other = swap(n2)

    widths = WIDTHS
    starts = tuple(sum(widths[:i]) for i in range(len(widths)))
    one, two = (LinkSum(place, order) for _ in range(2))
    first_sides = one.sides[0]

    def run_feed(i, token_sums):
        step = functools.partial(
            feed, start=starts[i], width=widths[i], sides=first_sides
        )
        *grads, own_result, own_back, other_result, other_back = order(
            step, place, n2, n2_other, dy, dy_other, gate_weight, gate_other, up_weight, up_other,
            down_weight, changes, token_sums,
        )
        pairs = [(grads[2 * i], grads[2 * i + 1]) for i in range(3)]
        return pairs, (own_result, own_back, other_result, other_back)

    def run_untile(i, parts, outs):
        step = functools.partial(
            untile, start=starts[i], width=widths[i], features=features, hidden=hidden,
            sides=first_sides,
        )
        return order(step, place, parts, outs)

    pairs, token_sums = run_feed(0, None)
    one.leave(pairs)
    pairs, token_sums = run_feed(1, token_sums)
    own_result, own_back, other_result, other_back = token_sums
    got_back = swap(other_back)
    one.halve(1)

    dh1, do, gg_two, out_mine, out_theirs = order(
        middle, place, own_back, got_back, h1, dy, params, w_out, o
    )
    one.halve(2)
    one.across()
    pairs = order(lambda pairs: pairs, pairs)
    two.leave(pairs)
    back_operands = (place, q, do, kv, *before, segment_ids, lse, cosine, sine)
    dq_low, *pair_sums = order(
        functools.partial(attend_back, first_pair=0, pairs=4), *back_operands, None
    )
    two.halve(1)
    dq_high, own_pairs, *sent_pairs = order(
        functools.partial(attend_back, first_pair=4, pairs=3), *back_operands, pair_sums
    )
    got_pairs = [
        lax.ppermute(pairs, "ctx", [(i + d, i) for i in range(chunks - d)])
        for d, pairs in enumerate(sent_pairs, 1)
    ]
    one.turn()
    two.halve(2)
    back_part, gb_query, query_mine, query_theirs = order(
        query_back, place, dq_low, dq_high, n1, w_in
    )
    two.across_each()
    dx, mine, theirs = order(
        last, place, own_pairs, *got_pairs, n1, x, params, w_in, back_part, dh1, cosine, sine,
        query_mine, query_theirs, out_mine, out_theirs, gb_query, gg_two,
    )
    input_grad = dx[None]
    width = HQ * HD
    rest = FlatSum(place, order)
    two.turn_each(0)
    rest.leave(mine, swap(theirs))
    two.turn_each(1)
    rest.halve()
    one.join(2)
    two.turn_each(2)
    rest.sum()
    one.join(1)
    two.join(2)
    rest.across()
    rest.turn()
    two.join(1)
    rest.join()
    outs = run_untile(0, one.parts, None)
    block_output = order(
        lambda a, b, c: (a + b.astype(f32) + c.astype(f32)).astype(bf16), h1, own_result, swap(other_result)
    )[None]
    gates, ups, gw_down = run_untile(1, two.parts, outs)
    gw_query, gw_key, gw_value, gw_out, vector = order(
        functools.partial(
            untile_flat, rows_held=features // 2, widths=(width, kv_width, kv_width, features),
            sides=rest.sides[0],
        ),
        place,
        flatten(rest.held),
    )
    vector = vector.reshape(-1)
    shares = []
    at = 0
    for size in (features, width, kv_width, kv_width, features):
        shares.append(lax.dynamic_slice_in_dim(vector, at + me * (size // 2), size // 2, 0))
        at += size
    gg_one, gb_query, gb_key, gb_value, gg_two = shares
    return (
        block_output,
        input_grad,
        gg_one,
        gw_query,
        gb_query,
        gw_key,
        gb_key,
        gw_value,
        gb_value,
        gw_out,
        gg_two,
        gates,
        ups,
        gw_down,
    )


def solution(mesh):
    return jax.shard_map(
        on_device,
        mesh=mesh,
        in_specs=(
            P(("seq", "fsdp"), "ctx", None),
            P(("seq", "fsdp"), None),
            P(("seq", "fsdp"), "ctx", None),
            P("fsdp"),
            P("fsdp", None),
            P("fsdp"),
            P("fsdp", None),
            P("fsdp"),
            P("fsdp", None),
            P("fsdp"),
            P("fsdp", None),
            P("fsdp"),
            P("fsdp", None),
            P("fsdp", None),
            P("fsdp", None),
        ),
        out_specs=(
            P(("seq", "fsdp"), "ctx", None),
            P(("seq", "fsdp"), "ctx", None),
            P("fsdp"),
            P("fsdp", None),
            P("fsdp"),
            P("fsdp", None),
            P("fsdp"),
            P("fsdp", None),
            P("fsdp"),
            P("fsdp", None),
            P("fsdp"),
            P("fsdp", None),
            P("fsdp", None),
            P("fsdp", None),
        ),
        check_vma=False,
    )
```

```python
import functools

import jax
import jax.numpy as jnp
from jax import lax
from jax.experimental import pallas as pl
from jax.experimental.pallas import tpu as pltpu
from jax.sharding import PartitionSpec as P

HQ = 14
KVH = 2
HD = 64
WINDOW = 1024
PAIRS = HQ // 2
LANES = 128
HALF = 256

theta_base = 1000000.0
eps_norm = 1e-06
masked_score = -1e30
f32 = jnp.float32
bf16 = jnp.bfloat16
VMEM_BYTES = 58 * 1024 * 1024
WIDTHS = (1408, 1024)


def nn(a, b):
    return lax.dot_general(a, b, (((1,), (0,)), ((), ())), preferred_element_type=f32)


def nt(a, b):
    return lax.dot_general(a, b, (((1,), (1,)), ((), ())), preferred_element_type=f32)


def tn(a, b):
    return lax.dot_general(a, b, (((0,), (0,)), ((), ())), preferred_element_type=f32)


def flip_lanes_half(values):
    width = values.shape[-1]
    lane = lax.broadcasted_iota(jnp.int32, values.shape, len(values.shape) - 1)
    up = pltpu.roll(values, width - 32, len(values.shape) - 1)
    down = pltpu.roll(values, 32, len(values.shape) - 1)
    return jnp.where((lane & 63) < 32, -up, down)


def call(kernel, out_shape, flops, moved, **kwargs):
    return pl.pallas_call(
        kernel,
        out_shape=out_shape,
        compiler_params=pltpu.CompilerParams(vmem_limit_bytes=VMEM_BYTES),
        cost_estimate=pl.CostEstimate(flops=flops, bytes_accessed=moved, transcendentals=0),
        **kwargs,
    )


GAIN_ONE = slice(0, 896)
BIAS = slice(896, 2048)
GAIN_TWO = slice(2048, 2944)


def place_rows(target, own_ref, other_ref, me, columns=slice(None)):
    rows = own_ref.shape[0]
    target[pl.ds(pl.multiple_of(me * rows, rows), rows), columns] = own_ref[...]
    target[pl.ds(pl.multiple_of((1 - me) * rows, rows), rows), columns] = other_ref[...]


def project_kernel(
    place_ref, x_ref, params_ref, wq_ref, wk_ref, wv_ref, oq_ref, ok_ref, ov_ref, cos_ref, sin_ref,
    n1_ref, q_ref, kv_ref, w_ref,
):
    count = x_ref.shape[0]
    step = 256
    me = place_ref[0]
    width = HQ * HD
    place_rows(w_ref, wq_ref, oq_ref, me, slice(0, width))
    place_rows(w_ref, wk_ref, ok_ref, me, slice(width, width + LANES))
    place_rows(w_ref, wv_ref, ov_ref, me, slice(width + LANES, width + 2 * LANES))

    def body(i, carry):
        rows = pl.ds(pl.multiple_of(i * step, step), step)
        x = x_ref[rows, :].astype(f32)
        scale = lax.rsqrt(jnp.mean(x * x, -1, keepdims=True) + eps_norm)
        normed = (x * scale * params_ref[:, GAIN_ONE]).astype(bf16)
        n1_ref[rows, :] = normed
        cosine = cos_ref[rows, :]
        sine = sin_ref[rows, :]
        out = nn(normed, w_ref[...]) + params_ref[:, BIAS]
        for j in range(PAIRS + 1):
            part = out[:, j * LANES : (j + 1) * LANES]
            part = part * cosine + flip_lanes_half(part) * sine
            if j < PAIRS:
                q_ref[rows, j * LANES : (j + 1) * LANES] = (part * HD**-0.5).astype(bf16)
            else:
                kv_ref[rows, :LANES] = part.astype(bf16)
        kv_ref[rows, LANES:] = out[:, (PAIRS + 1) * LANES :].astype(bf16)
        return carry

    lax.fori_loop(0, count // step, body, 0)


def in_vmem(n):
    return [pl.BlockSpec(memory_space=pltpu.SMEM)] + [pl.BlockSpec(memory_space=pltpu.VMEM)] * n


def project(place, x, params, own, other, cosine, sine):
    count, width = x.shape
    columns = sum(w.shape[1] for w in own)
    return call(
        project_kernel,
        (
            jax.ShapeDtypeStruct((count, width), bf16),
            jax.ShapeDtypeStruct((count, HQ * HD), bf16),
            jax.ShapeDtypeStruct((count, 2 * KVH * HD), bf16),
            jax.ShapeDtypeStruct((width, columns), bf16),
        ),
        2 * count * width * columns,
        6 * 1024 * 1024,
        in_specs=in_vmem(10),
    )(place, x, params, *own, *other, cosine, sine)


def lane_low(shape):
    return lax.broadcasted_iota(jnp.int32, shape, len(shape) - 1) < HD


def spread_heads(source, target, row):
    values = source.astype(f32)
    other = pltpu.roll(values, HD, 1)
    low = lane_low(values.shape)
    rows = pl.ds(row, values.shape[0])
    target[0, 0, rows, :] = jnp.where(low, values, 0.0).astype(bf16)
    target[1, 0, rows, :] = jnp.where(low, 0.0, other).astype(bf16)
    target[0, 1, rows, :] = jnp.where(low, other, 0.0).astype(bf16)
    target[1, 1, rows, :] = jnp.where(low, 0.0, values).astype(bf16)


def turn_heads(source, target, column):
    values = source.astype(f32).T.astype(bf16)
    columns = pl.ds(column, values.shape[1])
    target[0, :, columns] = values[:HD]
    target[1, :, columns] = values[HD:]


def fill_bias(place_ref, seg_ref, near_ref, far_ref, count):
    ctx = place_ref[3]

    def segments(back):
        start = pl.multiple_of(jnp.maximum(ctx - back, 0) * count, count)
        row = seg_ref[:, pl.ds(start, count)].astype(f32)
        row = jnp.where(ctx >= back, row, -1.0)
        return row, jnp.broadcast_to(row, (LANES, count)).T

    own_row, own = segments(0)
    _, one = segments(1)
    _, two = segments(2)
    for t in range(count // LANES):
        columns = slice(t * LANES, (t + 1) * LANES)
        query = own_row[:, columns]
        near_ref[:, columns] = jnp.where(one == query, 0.0, masked_score)
        key = lax.broadcasted_iota(jnp.int32, (count, LANES), 0)
        token = lax.broadcasted_iota(jnp.int32, (count, LANES), 1) + t * LANES
        far = jnp.where(key <= token, own, two)
        far_ref[:, columns] = jnp.where(far == query, 0.0, masked_score)


def triangle():
    key = lax.broadcasted_iota(jnp.int32, (HALF, HALF), 0)
    token = lax.broadcasted_iota(jnp.int32, (HALF, HALF), 1)
    return key <= token


def tiles_of(t, count):
    if t == 0:
        plain = 2 * count + HALF
        plain_bias = HALF
    else:
        plain = 0
        plain_bias = 0
    diagonal = t * HALF
    return plain, plain_bias, diagonal, 2 * count + diagonal


def scores_of(keys, query, t, count, near_ref, far_ref, tri):
    plain, plain_bias, own, old = tiles_of(t, count)
    columns = slice(t * HALF, (t + 1) * HALF)
    near = nt(keys(count, count), query) + near_ref[:, columns]
    far = nt(keys(plain, HALF), query) + far_ref[plain_bias : plain_bias + HALF, columns]
    edge = jnp.where(tri, nt(keys(own, HALF), query), nt(keys(old, HALF), query))
    edge = edge + far_ref[own : own + HALF, columns]
    return near, far, edge


def attend_kernel(
    place_ref, q_ref, kv0_ref, kv1_ref, kv2_ref, seg_ref, o_ref, lse_ref, k_s, vt_s, near_s, far_s
):
    count = q_ref.shape[0]
    pair = pl.program_id(0)

    @pl.when(pair == 0)
    def _():
        for i, ref in enumerate((kv0_ref, kv1_ref, kv2_ref)):
            spread_heads(ref[:, :LANES], k_s, i * count)
            turn_heads(ref[:, LANES:], vt_s, i * count)
        fill_bias(place_ref, seg_ref, near_s, far_s, count)

    tri = triangle()
    for t in range(count // HALF):
        plain, _, own, old = tiles_of(t, count)
        rows = slice(t * HALF, (t + 1) * HALF)
        query = q_ref[rows, :]
        turned = []
        for half in range(2):
            group = (2 * pair + half) // (HQ // KVH)
            near, far, edge = scores_of(
                lambda start, size: k_s[half, group, start : start + size, :],
                query,
                t,
                count,
                near_s,
                far_s,
                tri,
            )
            top = jnp.maximum(
                jnp.max(near, 0, keepdims=True),
                jnp.maximum(jnp.max(far, 0, keepdims=True), jnp.max(edge, 0, keepdims=True)),
            )
            near = jnp.exp(near - top)
            far = jnp.exp(far - top)
            edge = jnp.exp(edge - top)
            total = (
                jnp.sum(near, 0, keepdims=True)
                + jnp.sum(far, 0, keepdims=True)
                + jnp.sum(edge, 0, keepdims=True)
            )
            lse_ref[0, half : half + 1, rows] = top + jnp.log(total)
            mixed = nn(vt_s[group, :, count : 2 * count], near.astype(bf16))
            mixed += nn(vt_s[group, :, plain : plain + HALF], far.astype(bf16))
            mixed += nn(vt_s[group, :, own : own + HALF], jnp.where(tri, edge, 0.0).astype(bf16))
            mixed += nn(vt_s[group, :, old : old + HALF], jnp.where(tri, 0.0, edge).astype(bf16))
            turned.append(mixed * (1.0 / total))
        o_ref[rows, :] = jnp.concatenate(turned, 0).T.astype(bf16)


def attend(place, q, kv0, kv1, kv2, seg):
    count = q.shape[0]
    whole = lambda p: (0, 0)
    return call(
        attend_kernel,
        (
            jax.ShapeDtypeStruct((count, HQ * HD), bf16),
            jax.ShapeDtypeStruct((PAIRS, 8, count), f32),
        ),
        4 * HQ * count * 1280 * 256,
        4 * 1024 * 1024,
        grid=(PAIRS,),
        in_specs=[
            pl.BlockSpec(memory_space=pltpu.SMEM),
            pl.BlockSpec((count, LANES), lambda p: (0, p)),
            pl.BlockSpec(kv0.shape, whole),
            pl.BlockSpec(kv1.shape, whole),
            pl.BlockSpec(kv2.shape, whole),
            pl.BlockSpec(seg.shape, whole),
        ],
        out_specs=(
            pl.BlockSpec((count, LANES), lambda p: (0, p)),
            pl.BlockSpec((1, 8, count), lambda p: (p, 0, 0)),
        ),
        scratch_shapes=[
            pltpu.VMEM((2, KVH, 3 * count, LANES), bf16),
            pltpu.VMEM((KVH, HD, 3 * count), bf16),
            pltpu.VMEM((count, count), f32),
            pltpu.VMEM((count, count), f32),
        ],
    )(place, q, kv0, kv1, kv2, seg)


def attend_back_kernel(*refs, first_pair, first, final):
    (place_ref, q_ref, do_ref, kv0_ref, kv1_ref, kv2_ref, seg_ref, lse_ref, cos_ref, sin_ref) = refs[:10]
    refs = refs[10:]
    if not first:
        dk_in, dv_in = refs[:2]
        refs = refs[2:]
    dq_ref = refs[0]
    refs = refs[1:]
    if final:
        own_ref, one_ref, two_ref = refs[:3]
        refs = refs[3:]
        k_s, v_s, kt_s, near_s, far_s, dk_s, dv_s = refs
    else:
        dk_s, dv_s = refs[:2]
        k_s, v_s, kt_s, near_s, far_s = refs[2:]
    count = q_ref.shape[0]
    step = pl.program_id(0)
    pair = step + first_pair

    @pl.when(step == 0)
    def _():
        for i, ref in enumerate((kv0_ref, kv1_ref, kv2_ref)):
            spread_heads(ref[:, :LANES], k_s, i * count)
            spread_heads(ref[:, LANES:], v_s, i * count)
            turn_heads(ref[:, :LANES], kt_s, i * count)
        fill_bias(place_ref, seg_ref, near_s, far_s, count)
        if first:
            dk_s[...] = jnp.zeros_like(dk_s)
            dv_s[...] = jnp.zeros_like(dv_s)
        else:
            dk_s[...] = dk_in[...]
            dv_s[...] = dv_in[...]

    tri = triangle()
    for t in range(count // HALF):
        plain, _, own, old = tiles_of(t, count)
        rows = slice(t * HALF, (t + 1) * HALF)
        query = q_ref[rows, :]
        grad = do_ref[rows, :]
        low = lane_low(query.shape)
        turned = []
        for half in range(2):
            group = (2 * pair + half) // (HQ // KVH)
            mine = low if half == 0 else jnp.logical_not(low)
            query_half = jnp.where(mine, query.astype(f32), 0.0).astype(bf16)
            grad_half = jnp.where(mine, grad.astype(f32), 0.0).astype(bf16)
            log_total = lse_ref[0, half : half + 1, rows]
            scores = scores_of(
                lambda start, size: k_s[half, group, start : start + size, :],
                query,
                t,
                count,
                near_s,
                far_s,
                tri,
            )
            near, far, edge = (jnp.exp(part - log_total) for part in scores)
            values = lambda start, size: v_s[half, group, start : start + size, :]
            near_p = nt(values(count, count), grad)
            far_p = nt(values(plain, HALF), grad)
            edge_p = jnp.where(tri, nt(values(own, HALF), grad), nt(values(old, HALF), grad))
            inner = (
                jnp.sum(near * near_p, 0, keepdims=True)
                + jnp.sum(far * far_p, 0, keepdims=True)
                + jnp.sum(edge * edge_p, 0, keepdims=True)
            )
            near_g = near * (near_p - inner)
            far_g = far * (far_p - inner)
            edge_g = edge * (edge_p - inner)
            blocks = (
                (count, count, near, near_g),
                (plain, HALF, far, far_g),
                (own, HALF, jnp.where(tri, edge, 0.0), jnp.where(tri, edge_g, 0.0)),
                (old, HALF, jnp.where(tri, 0.0, edge), jnp.where(tri, 0.0, edge_g)),
            )
            total = None
            for start, size, weight, change in blocks:
                change = change.astype(bf16)
                keys = slice(start, start + size)
                dv_s[group, keys, :] += nn(weight.astype(bf16), grad_half)
                dk_s[group, keys, :] += nn(change, query_half)
                part = nn(kt_s[group, :, keys], change)
                total = part if total is None else total + part
            turned.append(total)
        turned = jnp.concatenate(turned, 0).T * HD**-0.5
        back = turned * cos_ref[rows, :] - flip_lanes_half(turned * sin_ref[rows, :])
        dq_ref[rows, :] = back.astype(bf16)

    if final:

        @pl.when(pair == PAIRS - 1)
        def _():
            for i, (ref, cast) in enumerate(((own_ref, f32), (one_ref, bf16), (two_ref, bf16))):
                keys = slice(i * count, (i + 1) * count)
                for j, source in enumerate((dk_s, dv_s)):
                    one = source[0, keys, :]
                    two = source[1, keys, :]
                    one = one + pltpu.roll(one, HD, 1)
                    two = two + pltpu.roll(two, HD, 1)
                    both = jnp.where(lane_low(one.shape), one, two)
                    ref[:, j * LANES : (j + 1) * LANES] = both.astype(cast)


def attend_back(place, q, do, kv0, kv1, kv2, seg, lse, cosine, sine, sums, *, first_pair, pairs):
    count = q.shape[0]
    first = sums is None
    final = first_pair + pairs == PAIRS
    sums = () if first else tuple(sums)
    whole = lambda p: (0, 0)
    stacked = pl.BlockSpec((KVH, 3 * count, LANES), lambda p: (0, 0, 0))
    lane_block = pl.BlockSpec((count, LANES), lambda p: (0, p + first_pair))
    row_block = pl.BlockSpec((1, 8, count), lambda p: (p + first_pair, 0, 0))
    token_block = pl.BlockSpec((count, 2 * LANES), whole)
    stack = jax.ShapeDtypeStruct((KVH, 3 * count, LANES), f32)
    if final:
        outs = [jax.ShapeDtypeStruct((count, 2 * LANES), t) for t in (f32, bf16, bf16)]
        out_specs = [token_block] * 3
        scratch = [pltpu.VMEM(stack.shape, f32)] * 2
    else:
        outs = [stack, stack]
        out_specs = [stacked] * 2
        scratch = []
    return call(
        functools.partial(attend_back_kernel, first_pair=first_pair, first=first, final=final),
        (jax.ShapeDtypeStruct((count, pairs * LANES), bf16), *outs),
        10 * 2 * pairs * count * 1280 * 256,
        6 * 1024 * 1024,
        grid=(pairs,),
        in_specs=[
            pl.BlockSpec(memory_space=pltpu.SMEM),
            lane_block,
            lane_block,
            pl.BlockSpec(kv0.shape, whole),
            pl.BlockSpec(kv1.shape, whole),
            pl.BlockSpec(kv2.shape, whole),
            pl.BlockSpec(seg.shape, whole),
            row_block,
            pl.BlockSpec(cosine.shape, whole),
            pl.BlockSpec(sine.shape, whole),
        ]
        + [stacked] * len(sums),
        out_specs=(pl.BlockSpec((count, LANES), lambda p: (0, p)), *out_specs),
        scratch_shapes=[
            pltpu.VMEM((2, KVH, 3 * count, LANES), bf16),
            pltpu.VMEM((2, KVH, 3 * count, LANES), bf16),
            pltpu.VMEM((KVH, HD, 3 * count), bf16),
            pltpu.VMEM((count, count), f32),
            pltpu.VMEM((count, count), f32),
        ]
        + scratch,
    )(place, q, do, kv0, kv1, kv2, seg, lse, cosine, sine, *sums)


def merge_kernel(place_ref, x_ref, o_ref, own_ref, other_ref, params_ref, h1_ref, n2_ref, w_ref):
    step = 256
    place_rows(w_ref, own_ref, other_ref, place_ref[0])

    def body(i, carry):
        rows = pl.ds(pl.multiple_of(i * step, step), step)
        hidden = x_ref[rows, :].astype(f32) + nn(o_ref[rows, :], w_ref[...])
        h1_ref[rows, :] = hidden
        scale = lax.rsqrt(jnp.mean(hidden * hidden, -1, keepdims=True) + eps_norm)
        n2_ref[rows, :] = (hidden * scale * params_ref[:, GAIN_TWO]).astype(bf16)
        return carry

    lax.fori_loop(0, x_ref.shape[0] // step, body, 0)


def merge(place, x, o, own, other, params):
    return call(
        merge_kernel,
        (
            jax.ShapeDtypeStruct(x.shape, f32),
            jax.ShapeDtypeStruct(x.shape, bf16),
            jax.ShapeDtypeStruct((2 * own.shape[0], own.shape[1]), bf16),
        ),
        4 * x.shape[0] * own.shape[0] * own.shape[1],
        6 * 1024 * 1024,
        in_specs=in_vmem(5),
    )(place, x, o, own, other, params)


def change_kernel(ca_ref, cb_ref, down_ref, out_ref):
    count = ca_ref.shape[0]
    out_ref[:count, :] = nt(ca_ref[...], down_ref[...]).astype(bf16)
    out_ref[count:, :] = nt(cb_ref[...], down_ref[...]).astype(bf16)


def change(ca, cb, down):
    count, features = ca.shape
    hidden = down.shape[0]
    block = 2 * LANES
    steps = pl.cdiv(hidden, block)
    whole = pl.BlockSpec((count, features), lambda i: (0, 0))
    return call(
        change_kernel,
        jax.ShapeDtypeStruct((2 * count, hidden), bf16),
        4 * count * features * hidden,
        12 * 1024 * 1024,
        grid=(steps,),
        in_specs=[whole, whole, pl.BlockSpec((block, features), lambda i: (i, 0))],
        out_specs=pl.BlockSpec((2 * count, block), lambda i: (0, i)),
    )(ca, cb, down)


def feed_kernel(*refs, start, first, sides):
    place_ref, na_ref, nb_ref, ca_ref, cb_ref, gate_ref, gate_o_ref, up_ref, up_o_ref, down_ref, change_ref = refs[:11]
    refs = refs[11:]
    if not first:
        sums = refs[:4]
        refs = refs[4:]
    grad_refs = refs[:6]
    outs = refs[6:10]
    refs = refs[10:]
    (n_s, c_s, wg, wu, wd, change_s, inner_s, gate_s, up_s, *part_s) = refs[:12]
    refs = refs[12:]
    if not first:
        held = refs[:2]
        refs = refs[2:]
    totals = refs[:2]
    in_sem, sum_sem, out_sem = refs[2:]
    tokens, features = n_s.shape
    count = tokens // 2
    width = wg.shape[1]
    rows_held = gate_ref.shape[0]
    hidden = down_ref.shape[0]
    me = place_ref[0]
    lanes = pl.ds(pl.multiple_of(me * hidden + start, LANES), width)
    own_rows = pl.ds(pl.multiple_of(me * rows_held, rows_held), rows_held)
    other_rows = pl.ds(pl.multiple_of((1 - me) * rows_held, rows_held), rows_held)
    low, high = pl.ds(0, count), pl.ds(count, count)

    moves = [
        (na_ref, n_s.at[low, :]),
        (nb_ref, n_s.at[high, :]),
        (gate_ref.at[:, lanes], wg.at[own_rows, :]),
        (gate_o_ref.at[:, lanes], wg.at[other_rows, :]),
        (up_ref.at[:, lanes], wu.at[own_rows, :]),
        (up_o_ref.at[:, lanes], wu.at[other_rows, :]),
        (change_ref.at[:, pl.ds(start, width)], change_s),
        (down_ref.at[pl.ds(start, width), :], wd),
        (ca_ref, c_s.at[low, :]),
        (cb_ref, c_s.at[high, :]),
    ]
    copies = [pltpu.make_async_copy(a, b, in_sem.at[i]) for i, (a, b) in enumerate(moves)]
    for copy in copies:
        copy.start()
    sum_copies = []
    if not first:
        places = ((held[0], low), (held[1], low), (held[0], high), (held[1], high))
        sum_copies = [
            pltpu.make_async_copy(sums[i], target.at[rows, :], sum_sem.at[i])
            for i, (target, rows) in enumerate(places)
        ]
        for copy in sum_copies:
            copy.start()
    for copy in copies[:8] + sum_copies:
        copy.wait()
    step = 256

    def body(i, carry):
        rows = pl.ds(pl.multiple_of(i * step, step), step)
        normed = n_s[rows, :]
        gate = nn(normed, wg[...])
        up = nn(normed, wu[...])
        change = change_s[rows, :].astype(f32)
        sigmoid = 1.0 / (1.0 + jnp.exp(-gate))
        activated = gate * sigmoid
        inner = (activated * up).astype(bf16)
        gate_g = (change * up * sigmoid * (1.0 + gate * (1.0 - sigmoid))).astype(bf16)
        up_g = (change * activated).astype(bf16)
        inner_s[rows, :] = inner
        gate_s[rows, :] = gate_g
        up_s[rows, :] = up_g
        result = nn(inner, wd[...])
        back = nt(gate_g, wg[...]) + nt(up_g, wu[...])
        if not first:
            result = result + held[0][rows, :].astype(f32)
            back = back + held[1][rows, :].astype(f32)
        totals[0][rows, :] = result.astype(bf16)
        totals[1][rows, :] = back.astype(bf16)
        return carry

    lax.fori_loop(0, tokens // step, body, 0)
    for copy in copies[8:]:
        copy.wait()
    leaving = []

    def leave(source, target):
        copy = pltpu.make_async_copy(source, target, out_sem.at[len(leaving)])
        copy.start()
        leaving.append(copy)

    for i, (total, rows) in enumerate(
        ((totals[0], low), (totals[1], low), (totals[0], high), (totals[1], high))
    ):
        leave(total.at[rows, :], outs[i])

    def part_leaves(i):
        keep, send = grad_refs[2 * i : 2 * i + 2]
        rows = part_s[i].shape[0] // 2
        side = place_ref[sides[i]]
        leave(part_s[i].at[pl.ds(pl.multiple_of((1 - side) * rows, 16), rows), :], send)
        leave(part_s[i].at[pl.ds(pl.multiple_of(side * rows, 16), rows), :], keep)

    mine_s, theirs_s, down_s = part_s

    def tiles_loop(body):
        def step(i, carry):
            body(i * HALF, HALF)
            return carry

        lax.fori_loop(0, width // HALF, step, 0)
        if width % HALF:
            body(width // HALF * HALF, width % HALF)

    def columns_of(at, size):
        return pl.ds(at if isinstance(at, int) else pl.multiple_of(at, HALF), size)

    def wide_grads(at, size):
        for kind, source in enumerate((gate_s, up_s)):
            grads = tn(n_s[...], source[:, columns_of(at, size)]).astype(bf16)
            for j in range(size // LANES):
                row = (kind * width // LANES + at // LANES + j) * rows_held
                rows = pl.ds(row if isinstance(row, int) else pl.multiple_of(row, 16), rows_held)
                tile = grads[:, j * LANES : (j + 1) * LANES]

                @pl.when(me == 0)
                def _():
                    mine_s[rows, :] = tile[:rows_held]
                    theirs_s[rows, :] = tile[rows_held:]

                @pl.when(me == 1)
                def _():
                    mine_s[rows, :] = tile[rows_held:]
                    theirs_s[rows, :] = tile[:rows_held]

    def down_grads(at, size):
        grads = tn(inner_s[:, columns_of(at, size)], c_s[...]).astype(bf16)
        for j in range(features // LANES):
            row = j * width + at
            rows = pl.ds(row if isinstance(row, int) else pl.multiple_of(row, 16), size)
            down_s[rows, :] = grads[:, j * LANES : (j + 1) * LANES]

    tiles_loop(wide_grads)
    part_leaves(0)
    part_leaves(1)
    tiles_loop(down_grads)
    part_leaves(2)
    for copy in leaving:
        copy.wait()


def feed(place, na, nb, ca, cb, gate, gate_o, up, up_o, down, change, sums, *, start, width, sides):
    count, features = na.shape
    first = sums is None
    sums = () if first else tuple(sums)
    anywhere = pl.BlockSpec(memory_space=pl.ANY)
    rows = features * width // LANES
    tokens = (2 * count, features)
    outs = [jax.ShapeDtypeStruct((rows // 2, LANES), bf16)] * 6
    outs += [jax.ShapeDtypeStruct((count, features), bf16)] * 4
    scratch = [pltpu.VMEM(tokens, bf16)] * 2
    scratch += [pltpu.VMEM((features, width), bf16)] * 2 + [pltpu.VMEM((width, features), bf16)]
    scratch += [pltpu.VMEM((2 * count, width), bf16)] * 4
    scratch += [pltpu.VMEM((rows, LANES), bf16)] * 3
    scratch += [pltpu.VMEM(tokens, bf16)] * (2 if first else 4)
    scratch += [pltpu.SemaphoreType.DMA((n,)) for n in (10, 4, 10)]
    return call(
        functools.partial(feed_kernel, start=start, first=first, sides=sides),
        tuple(outs),
        18 * 2 * count * features * width,
        30 * 1024 * 1024,
        in_specs=[pl.BlockSpec(memory_space=pltpu.SMEM)] + [anywhere] * (10 + len(sums)),
        out_specs=(anywhere,) * 10,
        scratch_shapes=scratch,
    )(place, na, nb, ca, cb, gate, gate_o, up, up_o, down, change, *sums)


def middle_kernel(
    place_ref, part_ref, got_ref, h1_ref, dy_ref, params_ref, w_ref, o_ref,
    dh1_ref, do_ref, gg_ref, mine_ref, theirs_ref, low_s,
):
    count, features = part_ref.shape
    step = 256
    gg_ref[...] = jnp.zeros_like(gg_ref)

    def body(i, carry):
        rows = pl.ds(pl.multiple_of(i * step, step), step)
        back = part_ref[rows, :].astype(f32) + got_ref[rows, :].astype(f32)
        hidden = h1_ref[rows, :]
        scale = lax.rsqrt(jnp.mean(hidden * hidden, -1, keepdims=True) + eps_norm)
        normal = hidden * scale
        gg_ref[...] += jnp.sum(back * normal, 0, keepdims=True)
        change = back * params_ref[:, GAIN_TWO]
        grad = dy_ref[rows, :].astype(f32) + scale * (
            change - normal * jnp.mean(change * normal, -1, keepdims=True)
        )
        dh1_ref[rows, :] = grad
        low = grad.astype(bf16)
        low_s[rows, :] = low
        do_ref[rows, :] = nt(low, w_ref[...]).astype(bf16)
        return carry

    lax.fori_loop(0, count // step, body, 0)
    store_split(place_ref, tn(o_ref[...], low_s[...]).astype(bf16), mine_ref, theirs_ref, 0)


def store_split(place_ref, grads, mine_ref, theirs_ref, first_tile):
    half_rows = grads.shape[0] // 2
    me = place_ref[0]
    for j in range(grads.shape[1] // LANES):
        row = (first_tile + j) * half_rows
        tile = grads[:, j * LANES : (j + 1) * LANES]

        @pl.when(me == 0)
        def _():
            mine_ref[row : row + half_rows, :] = tile[:half_rows]
            theirs_ref[row : row + half_rows, :] = tile[half_rows:]

        @pl.when(me == 1)
        def _():
            mine_ref[row : row + half_rows, :] = tile[half_rows:]
            theirs_ref[row : row + half_rows, :] = tile[:half_rows]


def middle(place, part, got, h1, dy, params, w, o):
    count, features = part.shape
    rows = (features // 2) * (features // LANES)
    return call(
        middle_kernel,
        (
            jax.ShapeDtypeStruct((count, features), f32),
            jax.ShapeDtypeStruct((count, HQ * HD), bf16),
            jax.ShapeDtypeStruct((1, features), f32),
            jax.ShapeDtypeStruct((rows, LANES), bf16),
            jax.ShapeDtypeStruct((rows, LANES), bf16),
        ),
        4 * count * features * features,
        12 * 1024 * 1024,
        in_specs=in_vmem(7),
        scratch_shapes=[pltpu.VMEM((count, features), bf16)],
    )(place, part, got, h1, dy, params, w, o)


def query_kernel(
    place_ref, dqa_ref, dqb_ref, n1_ref, w_ref, back_ref, gb_ref, mine_ref, theirs_ref, dp_s
):
    count = n1_ref.shape[0]
    width = HQ * HD
    split_at = dqa_ref.shape[1]
    step = 256
    gb_ref[...] = jnp.zeros_like(gb_ref)

    def body(i, carry):
        rows = pl.ds(pl.multiple_of(i * step, step), step)
        dp_s[rows, :split_at] = dqa_ref[rows, :]
        dp_s[rows, split_at:] = dqb_ref[rows, :]
        grads = dp_s[rows, :]
        gb_ref[...] += jnp.sum(grads.astype(f32), 0, keepdims=True)
        back_ref[rows, :] = nt(grads, w_ref[:, :width])
        return carry

    lax.fori_loop(0, count // step, body, 0)
    store_split(place_ref, tn(n1_ref[...], dp_s[...]).astype(bf16), mine_ref, theirs_ref, 0)


def query_back(place, dqa, dqb, n1, w):
    count, features = n1.shape
    width = HQ * HD
    rows = (features // 2) * (width // LANES)
    return call(
        query_kernel,
        (
            jax.ShapeDtypeStruct((count, features), f32),
            jax.ShapeDtypeStruct((1, width), f32),
            jax.ShapeDtypeStruct((rows, LANES), bf16),
            jax.ShapeDtypeStruct((rows, LANES), bf16),
        ),
        4 * count * features * width,
        10 * 1024 * 1024,
        in_specs=in_vmem(4),
        scratch_shapes=[pltpu.VMEM((count, width), bf16)],
    )(place, dqa, dqb, n1, w)


VECTOR_ROWS = 128


def last_kernel(
    place_ref, own_ref, one_ref, two_ref, n1_ref, x_ref, params_ref, w_ref, part_ref, dh1_ref, cos_ref, sin_ref,
    qm_ref, qt_ref, om_ref, ot_ref, gbq_ref, ggt_ref, dx_ref, mine_ref, theirs_ref, dp_s, gg_ref, gb_ref,
):
    count = n1_ref.shape[0]
    width = HQ * HD
    step = 256
    gg_ref[...] = jnp.zeros_like(gg_ref)
    gb_ref[...] = jnp.zeros_like(gb_ref)

    def body(i, carry):
        rows = pl.ds(pl.multiple_of(i * step, step), step)
        pairs = own_ref[rows, :] + one_ref[rows, :].astype(f32) + two_ref[rows, :].astype(f32)
        key = pairs[:, :LANES]
        key = key * cos_ref[rows, :] - flip_lanes_half(key * sin_ref[rows, :])
        dp_s[rows, :LANES] = key.astype(bf16)
        dp_s[rows, LANES:] = pairs[:, LANES:].astype(bf16)
        grads = dp_s[rows, :]
        gb_ref[...] += jnp.sum(grads.astype(f32), 0, keepdims=True)
        back = part_ref[rows, :] + nt(grads, w_ref[:, width:])
        x = x_ref[rows, :].astype(f32)
        scale = lax.rsqrt(jnp.mean(x * x, -1, keepdims=True) + eps_norm)
        normal = x * scale
        gg_ref[...] += jnp.sum(back * normal, 0, keepdims=True)
        change = back * params_ref[:, GAIN_ONE]
        grad = dh1_ref[rows, :] + scale * (
            change - normal * jnp.mean(change * normal, -1, keepdims=True)
        )
        dx_ref[rows, :] = grad.astype(bf16)
        return carry

    lax.fori_loop(0, count // step, body, 0)
    at = qm_ref.shape[0]
    tiles = (w_ref.shape[1] - width) // LANES
    rows_held = at * LANES // width
    store_split(
        place_ref, tn(n1_ref[...], dp_s[...]).astype(bf16), mine_ref, theirs_ref, at // rows_held
    )
    mine_ref[:at, :] = qm_ref[...]
    theirs_ref[:at, :] = qt_ref[...]
    at += tiles * rows_held
    after = at + om_ref.shape[0]
    mine_ref[at:after, :] = om_ref[...]
    theirs_ref[at:after, :] = ot_ref[...]
    vectors = []
    for ref in (gg_ref, gbq_ref, gb_ref, ggt_ref):
        vectors += [ref[:, j * LANES : (j + 1) * LANES] for j in range(ref.shape[1] // LANES)]
    vectors.append(jnp.zeros((VECTOR_ROWS - len(vectors), LANES), f32))
    vectors = jnp.concatenate(vectors, 0).astype(bf16)
    mine_ref[after:, :] = vectors
    theirs_ref[after:, :] = vectors


def last(place, own, one, two, n1, x, params, w, part, dh1, cosine, sine, qm, qt, om, ot, gbq, ggt):
    count, features = n1.shape
    columns = w.shape[1] - HQ * HD
    rows = (features // 2) * (columns // LANES) + qm.shape[0] + om.shape[0] + VECTOR_ROWS
    return call(
        last_kernel,
        (
            jax.ShapeDtypeStruct((count, features), bf16),
            jax.ShapeDtypeStruct((rows, LANES), bf16),
            jax.ShapeDtypeStruct((rows, LANES), bf16),
        ),
        4 * count * features * columns,
        14 * 1024 * 1024,
        in_specs=in_vmem(17),
        scratch_shapes=[
            pltpu.VMEM((count, columns), bf16),
            pltpu.VMEM((1, features), f32),
            pltpu.VMEM((1, columns), f32),
        ],
    )(place, own, one, two, n1, x, params, w, part, dh1, cosine, sine, qm, qt, om, ot, gbq, ggt)


def swap(values):
    return lax.ppermute(values, "fsdp", [(0, 1), (1, 0)])


def flip(values, dim):
    axis, bit = dim
    size = lax.axis_size(axis)
    return lax.ppermute(values, axis, [(i, i ^ (1 << bit)) for i in range(size)])


def side(dim):
    axis, bit = dim
    return (lax.axis_index(axis) >> bit) & 1


def add(*terms):
    total = terms[0].astype(f32)
    for term in terms[1:]:
        total = total + term.astype(f32)
    return total.astype(bf16)


def take(array, index):
    return lax.dynamic_index_in_dim(array, index, 0, False)


def join(low, other, index):
    out = jnp.zeros((2,) + low.shape, low.dtype)
    out = lax.dynamic_update_index_in_dim(out, low, index, 0)
    return lax.dynamic_update_index_in_dim(out, other, 1 - index, 0)


def rest_of_seq(values):
    for bit in range(2, lax.axis_size("seq").bit_length() - 1):
        values = add(values, flip(values, ("seq", bit)))
    return values


class Order:
    def __init__(self):
        self.token = None

    def __call__(self, step, *operands):
        if self.token is not None:
            operands, _ = lax.optimization_barrier((operands, self.token))
        out = step(*operands)
        self.token = jax.tree.leaves(out)[0]
        return out


def fold_kernel(place_ref, *refs, sides):
    n = 2 * len(sides)
    for i, number in enumerate(sides):
        kept, got = refs[2 * i : 2 * i + 2]
        keep, send = refs[n + 2 * i : n + 2 * i + 2]
        rows = keep.shape[0]
        side = place_ref[number]
        for target, at in ((keep, side), (send, 1 - side)):
            at = pl.ds(pl.multiple_of(at * rows, 16), rows)
            target[...] = (kept[at, :].astype(f32) + got[at, :].astype(f32)).astype(bf16)


def flatten(pairs):
    return [array for pair in pairs for array in pair]


def fold(place, pairs, sides):
    rows = [kept.shape[0] // 2 for kept, _ in pairs]
    outs = call(
        functools.partial(fold_kernel, sides=sides),
        tuple(jax.ShapeDtypeStruct((n, LANES), bf16) for n in rows for _ in range(2)),
        4 * sum(rows) * LANES,
        12 * sum(rows) * LANES,
        in_specs=in_vmem(2 * len(pairs)),
    )(place, *flatten(pairs))
    return list(zip(outs[::2], outs[1::2]))


def stack_kernel(*refs):
    total = refs[-1]
    at = 0
    for kept, got in zip(refs[:-1:2], refs[1:-1:2]):
        rows = kept.shape[0]
        total[at : at + rows, :] = (kept[...].astype(f32) + got[...].astype(f32)).astype(bf16)
        at += rows


def stack(pairs):
    rows = sum(kept.shape[0] for kept, _ in pairs)
    return call(
        stack_kernel, jax.ShapeDtypeStruct((rows, LANES), bf16), rows * LANES, 6 * rows * LANES
    )(*flatten(pairs))


def sum_kernel(*refs):
    n = 2 * len(refs) // 3
    for kept, got, total in zip(refs[:n:2], refs[1:n:2], refs[n:]):
        total[...] = (kept[...].astype(f32) + got[...].astype(f32)).astype(bf16)


def sum_parts(pairs):
    rows = [kept.shape[0] for kept, _ in pairs]
    return call(
        sum_kernel,
        tuple(jax.ShapeDtypeStruct((n, LANES), bf16) for n in rows),
        sum(rows) * LANES,
        6 * sum(rows) * LANES,
    )(*flatten(pairs))


def unstack_kernel(total, got, *parts):
    at = 0
    for part in parts:
        rows = part.shape[0]
        both = total[at : at + rows, :].astype(f32) + got[at : at + rows, :].astype(f32)
        part[...] = both.astype(bf16)
        at += rows


def unstack(total, got, sizes):
    return call(
        unstack_kernel,
        tuple(jax.ShapeDtypeStruct((n, LANES), bf16) for n in sizes),
        total.shape[0] * LANES,
        6 * total.shape[0] * LANES,
    )(total, got)


def join_kernel(place_ref, *refs, sides):
    for i, number in enumerate(sides):
        own, got = refs[2 * i : 2 * i + 2]
        both = refs[2 * len(sides) + i]
        rows = own.shape[0]
        side = place_ref[number]
        both[pl.ds(pl.multiple_of(side * rows, 16), rows), :] = own[...]
        both[pl.ds(pl.multiple_of((1 - side) * rows, 16), rows), :] = got[...]


def join_parts(place, pairs, sides):
    rows = [own.shape[0] for own, _ in pairs]
    return call(
        functools.partial(join_kernel, sides=sides),
        tuple(jax.ShapeDtypeStruct((2 * n, LANES), bf16) for n in rows),
        1,
        8 * sum(rows) * LANES,
        in_specs=in_vmem(2 * len(pairs)),
    )(place, *flatten(pairs))


def bring_halves(place_ref, refs, sides, targets, in_sem):
    copies = []
    for i, number in enumerate(sides):
        side = place_ref[number]
        rows = targets[i].shape[0] // 2
        for ref, at in ((refs[2 * i], side), (refs[2 * i + 1], 1 - side)):
            at = pl.ds(pl.multiple_of(at * rows, 16), rows)
            copy = pltpu.make_async_copy(ref, targets[i].at[at, :], in_sem.at[len(copies)])
            copy.start()
            copies.append(copy)
    for copy in copies:
        copy.wait()


def untile_kernel(*refs, start, width, first, sides, n_parts):
    place_ref = refs[0]
    parts = refs[1 : 1 + n_parts]
    refs = refs[1 + n_parts + (0 if first else 3) :]
    gate_ref, up_ref, down_ref, mine_s, theirs_s, downs_s, wide_s, down_s, in_sem, out_sem = refs
    me = place_ref[0]
    features = down_ref.shape[1]
    hidden = down_ref.shape[0]
    rows_held = gate_ref.shape[0]
    targets = (mine_s, theirs_s, downs_s)
    bring_halves(place_ref, parts, sides, targets, in_sem)
    leaving = []

    def leave(source, target):
        copy = pltpu.make_async_copy(source, target, out_sem.at[len(leaving)])
        copy.start()
        leaving.append(copy)

    tiles = width // LANES
    for i, (source, owner) in enumerate(((mine_s, me), (theirs_s, 1 - me))):
        lanes = pl.ds(pl.multiple_of(owner * hidden + start, LANES), width)
        for kind, target in enumerate((gate_ref, up_ref)):
            wide = wide_s.at[2 * i + kind]
            for j in range(tiles):
                row = (kind * tiles + j) * rows_held
                wide[:, j * LANES : (j + 1) * LANES] = source[row : row + rows_held, :].astype(f32)
            leave(wide, target.at[:, lanes])
    for j in range(features // LANES):
        row = j * width
        down_s[:, j * LANES : (j + 1) * LANES] = downs_s[row : row + width, :].astype(f32)
    leave(down_s, down_ref.at[pl.ds(start, width), :])
    for copy in leaving:
        copy.wait()


def untile(place, parts, outs, *, start, width, features, hidden, sides):
    first = outs is None
    rows_held = features // 2
    rows = features * width // LANES
    anywhere = pl.BlockSpec(memory_space=pl.ANY)
    outs = () if first else tuple(outs)
    n_parts = len(parts)
    return call(
        functools.partial(
            untile_kernel, start=start, width=width, first=first, sides=sides, n_parts=n_parts
        ),
        (
            jax.ShapeDtypeStruct((rows_held, 2 * hidden), f32),
            jax.ShapeDtypeStruct((rows_held, 2 * hidden), f32),
            jax.ShapeDtypeStruct((hidden, features), f32),
        ),
        3 * features * width,
        3 * features * width * 6,
        in_specs=[pl.BlockSpec(memory_space=pltpu.SMEM)] + [anywhere] * (n_parts + len(outs)),
        out_specs=(anywhere,) * 3,
        scratch_shapes=[pltpu.VMEM((rows, LANES), bf16)] * 3
        + [
            pltpu.VMEM((4, rows_held, width), f32),
            pltpu.VMEM((width, features), f32),
            pltpu.SemaphoreType.DMA((6,)),
            pltpu.SemaphoreType.DMA((5,)),
        ],
        input_output_aliases={} if first else {1 + n_parts + i: i for i in range(3)},
    )(place, *parts, *outs)


def split_kernel(place_ref, mine_ref, theirs_ref, *refs, sides):
    base = 0
    for i, number in enumerate(sides):
        side = place_ref[number]
        rows = refs[2 * i].shape[0]
        for target, at in zip(refs[2 * i : 2 * i + 2], (side, 1 - side)):
            at = pl.ds(pl.multiple_of(base + at * rows, 16), rows)
            target[...] = (mine_ref[at, :].astype(f32) + theirs_ref[at, :].astype(f32)).astype(bf16)
        base += 2 * rows


def split(place, mine, theirs, *, sides):
    rows = mine.shape[0] // (2 * len(sides))
    outs = call(
        functools.partial(split_kernel, sides=sides),
        (jax.ShapeDtypeStruct((rows, LANES), bf16),) * (2 * len(sides)),
        mine.shape[0] * LANES,
        6 * mine.shape[0] * LANES,
        in_specs=in_vmem(2),
    )(place, mine, theirs)
    return list(zip(outs[::2], outs[1::2]))


def untile_flat_kernel(*refs, sides):
    place_ref = refs[0]
    parts = refs[1 : 1 + 2 * len(sides)]
    *targets, vector_ref, flat_s, in_sem = refs[1 + 2 * len(sides) :]
    rows = flat_s.shape[0] // len(sides)
    halves = [flat_s.at[pl.ds(i * rows, rows), :] for i in range(len(sides))]
    bring_halves(place_ref, parts, sides, halves, in_sem)
    rows_held = targets[0].shape[0]
    row = 0
    for target in targets:
        for j in range(target.shape[1] // LANES):
            target[:, j * LANES : (j + 1) * LANES] = flat_s[row : row + rows_held, :].astype(f32)
            row += rows_held
    vector_ref[...] = flat_s[row:, :].astype(f32)


def untile_flat(place, parts, *, rows_held, widths, sides):
    rows = rows_held * sum(widths) // LANES + VECTOR_ROWS
    anywhere = pl.BlockSpec(memory_space=pl.ANY)
    return call(
        functools.partial(untile_flat_kernel, sides=sides),
        (
            *(jax.ShapeDtypeStruct((rows_held, width), f32) for width in widths),
            jax.ShapeDtypeStruct((VECTOR_ROWS, LANES), f32),
        ),
        rows * LANES,
        rows * LANES * 6,
        in_specs=[pl.BlockSpec(memory_space=pltpu.SMEM)] + [anywhere] * len(parts),
        out_specs=(pl.BlockSpec(memory_space=pltpu.VMEM),) * (len(widths) + 1),
        scratch_shapes=[
            pltpu.VMEM((rows, LANES), bf16), pltpu.SemaphoreType.DMA((2 * len(sides),))
        ],
    )(place, *parts)


class FlatSum:
    def __init__(self, place, order):
        self.place, self.order = place, order
        self.links, self.sides = ((X, Y), (Y, X)), ((1, 2), (2, 1))

    def over(self, arrays, level):
        return [flip(array, link) for array, link in zip(arrays, self.links[level])]

    def leave(self, mine, theirs):
        pairs = self.order(functools.partial(split, sides=self.sides[0]), self.place, mine, theirs)
        kept, sent = zip(*pairs)
        self.held = list(zip(kept, self.over(sent, 0)))

    def halve(self):
        pairs = self.order(lambda pairs: fold(self.place, pairs, self.sides[1]), self.held)
        kept, sent = zip(*pairs)
        self.held = list(zip(kept, self.over(sent, 1)))

    def sum(self):
        total = rest_of_seq(self.order(stack, self.held))
        self.total = total, flip(total, Z)

    def across(self):
        total = self.order(add, *self.total)
        for bit in range(2, lax.axis_size("ctx").bit_length() - 1):
            total = add(total, flip(total, ("ctx", bit)))
        self.total = total, flip(total, FAR)

    def turn(self):
        total, got = self.total
        sizes = (total.shape[0] // 2,) * 2
        own = self.order(lambda total, got: unstack(total, got, sizes), total, got)
        self.held = list(zip(own, self.over(own, 1)))

    def join(self):
        own = self.order(lambda pairs: join_parts(self.place, pairs, self.sides[1]), self.held)
        self.held = list(zip(own, self.over(own, 0)))


class LinkSum:
    def __init__(self, place, order):
        self.place, self.order = place, order
        links, numbers = (X, Y, Z), (1, 2, 4)
        self.links = [[links[(i + j) % 3] for i in range(3)] for j in range(3)]
        self.sides = [tuple(numbers[(i + j) % 3] for i in range(3)) for j in range(3)]

    def over(self, arrays, level):
        return [flip(array, link) for array, link in zip(arrays, self.links[level])]

    def leave(self, pairs):
        kept, sent = zip(*pairs)
        self.held = list(zip(kept, self.over(sent, 0)))

    def halve(self, level):
        pairs = self.order(lambda pairs: fold(self.place, pairs, self.sides[level]), self.held)
        kept, sent = zip(*pairs)
        self.held = list(zip(kept, self.over(sent, level)))

    def rest_of_axes(self, total):
        total = rest_of_seq(total)
        for bit in range(2, lax.axis_size("ctx").bit_length() - 1):
            total = add(total, flip(total, ("ctx", bit)))
        return total

    def across(self):
        self.sizes = [kept.shape[0] for kept, _ in self.held]
        total = self.rest_of_axes(self.order(stack, self.held))
        self.total = total, flip(total, FAR)

    def turn(self):
        own = list(self.order(lambda total, got: unstack(total, got, self.sizes), *self.total))
        own[1] = swap(own[1])
        self.held = list(zip(own, self.over(own, 2)))

    def across_each(self):
        totals = [self.rest_of_axes(total) for total in self.order(sum_parts, self.held)]
        self.held = [(total, flip(total, FAR)) for total in totals]

    def turn_each(self, i):
        own = self.order(add, *self.held[i])
        if i == 1:
            own = swap(own)
        self.held[i] = own, flip(own, self.links[2][i])

    def join(self, level):
        own = self.order(lambda pairs: join_parts(self.place, pairs, self.sides[level]), self.held)
        self.held = list(zip(own, self.over(own, level - 1)))

    @property
    def parts(self):
        return flatten(self.held)


X, Y, Z, FAR = ("seq", 0), ("seq", 1), ("ctx", 0), ("ctx", 1)


def on_device(
    block_input,
    segment_ids,
    out_cotangent,
    input_gain,
    query_weight,
    query_bias,
    key_weight,
    key_bias,
    value_weight,
    value_bias,
    output_weight,
    middle_gain,
    gate_weight,
    up_weight,
    down_weight,
):
    me = lax.axis_index("fsdp")
    ctx = lax.axis_index("ctx")
    chunks = lax.axis_size("ctx")
    place = jnp.stack([me, side(X), side(Y), ctx, side(Z)]).astype(jnp.int32)
    x = block_input[0]
    dy = out_cotangent[0]
    count, features = x.shape
    hidden = down_weight.shape[0]
    kv_width = KVH * HD

    own = (query_weight, key_weight, value_weight)
    other = tuple(swap(w) for w in own)
    vectors = (input_gain, query_bias, key_bias, value_bias, middle_gain)
    mine = jnp.concatenate(vectors)
    theirs = swap(mine)
    low = jnp.where(me == 0, mine, theirs).astype(f32)
    high = jnp.where(me == 0, theirs, mine).astype(f32)
    params = []
    at = 0
    for vector in vectors:
        size = vector.shape[0]
        params += [low[at : at + size], high[at : at + size]]
        at += size
    params = jnp.concatenate(params)[None]

    first = ctx * count
    positions = (first + jnp.arange(count, dtype=jnp.int32)).astype(f32)
    inverse = theta_base ** (-jnp.arange(0, HD, 2, dtype=f32) / HD)
    angle = positions[:, None] * jnp.tile(inverse, LANES // inverse.shape[0])[None, :]
    cosine, sine = jnp.cos(angle), jnp.sin(angle)

    n1, q, kv, w_in = project(place, x, params, own, other, cosine, sine)
    out_other = swap(output_weight)
    gate_other, up_other = swap(gate_weight), swap(up_weight)
    dy_other = swap(dy)

    reach = WINDOW // count
    before = [
        lax.ppermute(kv, "ctx", [(i, i + d) for i in range(chunks - d)])
        for d in range(1, reach + 1)
    ]
    order = Order()
    changes = order(change, dy, dy_other, down_weight)
    o, lse = order(attend, place, q, kv, *before, segment_ids)
    h1, n2, w_out = merge(place, x, o, output_weight, out_other, params)
    n2_other = swap(n2)

    widths = WIDTHS
    starts = tuple(sum(widths[:i]) for i in range(len(widths)))
    one, two = (LinkSum(place, order) for _ in range(2))
    first_sides = one.sides[0]

    def run_feed(i, token_sums):
        step = functools.partial(
            feed, start=starts[i], width=widths[i], sides=first_sides
        )
        *grads, own_result, own_back, other_result, other_back = order(
            step, place, n2, n2_other, dy, dy_other, gate_weight, gate_other, up_weight, up_other,
            down_weight, changes, token_sums,
        )
        pairs = [(grads[2 * i], grads[2 * i + 1]) for i in range(3)]
        return pairs, (own_result, own_back, other_result, other_back)

    def run_untile(i, parts, outs):
        step = functools.partial(
            untile, start=starts[i], width=widths[i], features=features, hidden=hidden,
            sides=first_sides,
        )
        return order(step, place, parts, outs)

    pairs, token_sums = run_feed(0, None)
    one.leave(pairs)
    pairs, token_sums = run_feed(1, token_sums)
    own_result, own_back, other_result, other_back = token_sums
    got_back = swap(other_back)
    one.halve(1)

    dh1, do, gg_two, out_mine, out_theirs = order(
        middle, place, own_back, got_back, h1, dy, params, w_out, o
    )
    one.halve(2)
    one.across()
    pairs = order(lambda pairs: pairs, pairs)
    two.leave(pairs)
    back_operands = (place, q, do, kv, *before, segment_ids, lse, cosine, sine)
    dq_low, *pair_sums = order(
        functools.partial(attend_back, first_pair=0, pairs=4), *back_operands, None
    )
    two.halve(1)
    dq_high, own_pairs, *sent_pairs = order(
        functools.partial(attend_back, first_pair=4, pairs=3), *back_operands, pair_sums
    )
    got_pairs = [
        lax.ppermute(pairs, "ctx", [(i + d, i) for i in range(chunks - d)])
        for d, pairs in enumerate(sent_pairs, 1)
    ]
    one.turn()
    two.halve(2)
    back_part, gb_query, query_mine, query_theirs = order(
        query_back, place, dq_low, dq_high, n1, w_in
    )
    two.across_each()
    dx, mine, theirs = order(
        last, place, own_pairs, *got_pairs, n1, x, params, w_in, back_part, dh1, cosine, sine,
        query_mine, query_theirs, out_mine, out_theirs, gb_query, gg_two,
    )
    input_grad = dx[None]
    width = HQ * HD
    rest = FlatSum(place, order)
    two.turn_each(0)
    rest.leave(mine, swap(theirs))
    two.turn_each(1)
    rest.halve()
    one.join(2)
    two.turn_each(2)
    rest.sum()
    one.join(1)
    two.join(2)
    rest.across()
    rest.turn()
    two.join(1)
    rest.join()
    outs = run_untile(0, one.parts, None)
    block_output = order(
        lambda a, b, c: (a + b.astype(f32) + c.astype(f32)).astype(bf16), h1, own_result, swap(other_result)
    )[None]
    gates, ups, gw_down = run_untile(1, two.parts, outs)
    gw_query, gw_key, gw_value, gw_out, vector = order(
        functools.partial(
            untile_flat, rows_held=features // 2, widths=(width, kv_width, kv_width, features),
            sides=rest.sides[0],
        ),
        place,
        flatten(rest.held),
    )
    vector = vector.reshape(-1)
    shares = []
    at = 0
    for size in (features, width, kv_width, kv_width, features):
        shares.append(lax.dynamic_slice_in_dim(vector, at + me * (size // 2), size // 2, 0))
        at += size
    gg_one, gb_query, gb_key, gb_value, gg_two = shares
    return (
        block_output,
        input_grad,
        gg_one,
        gw_query,
        gb_query,
        gw_key,
        gb_key,
        gw_value,
        gb_value,
        gw_out,
        gg_two,
        gates,
        ups,
        gw_down,
    )


def solution(mesh):
    return jax.shard_map(
        on_device,
        mesh=mesh,
        in_specs=(
            P(("seq", "fsdp"), "ctx", None),
            P(("seq", "fsdp"), None),
            P(("seq", "fsdp"), "ctx", None),
            P("fsdp"),
            P("fsdp", None),
            P("fsdp"),
            P("fsdp", None),
            P("fsdp"),
            P("fsdp", None),
            P("fsdp"),
            P("fsdp", None),
            P("fsdp"),
            P("fsdp", None),
            P("fsdp", None),
            P("fsdp", None),
        ),
        out_specs=(
            P(("seq", "fsdp"), "ctx", None),
            P(("seq", "fsdp"), "ctx", None),
            P("fsdp"),
            P("fsdp", None),
            P("fsdp"),
            P("fsdp", None),
            P("fsdp"),
            P("fsdp", None),
            P("fsdp"),
            P("fsdp", None),
            P("fsdp"),
            P("fsdp", None),
            P("fsdp", None),
            P("fsdp", None),
        ),
        check_vma=False,
    )
```
